256 devices in a mesh: ta: 16 (over x_hi, y, core), gz: 16 (over z, x_lo).
Axes of the slice: x: 4 (x_hi: 2, x_lo: 2; x = x_hi * 2 + x_lo), y: 4, z: 8, core: 2. Of those that a mesh axis runs over, the one named last changes fastest.
Arguments:
- link_phases: float32 [3, 2, 48, 64, 128], P(None, None, 'ta', 'gz'), may hold values from -4 to 4
- active: int32 [48, 64, 128], P('ta', 'gz'), may hold values 0 or 1
- bin_index: int32 [2, 48, 64, 128], P(None, 'ta', 'gz'), may hold values from 0 to 7
- first_weight: bfloat16 [9, 32, 54], replicated, may hold values from -0.25 to 0.25
- first_bias: float32 [32], replicated, may hold values from -3 to 3
- second_weight: bfloat16 [9, 48, 288], replicated, may hold values from -0.125 to 0.125
- second_bias: float32 [48], replicated, may hold values from -3 to 3
- cotangent: float32 [2, 48, 64, 128], P(None, 'ta', 'gz'), may hold values from -6 to 6
- logdet_cotangent: float32 [48, 64, 128], P('ta', 'gz'), may hold values from -6 to 6
Outputs:
- link_grad: float32 [3, 2, 48, 64, 128], P(None, None, 'ta', 'gz')
- first_weight_grad: float32 [9, 32, 54], replicated
- first_bias_grad: float32 [32], replicated
- second_weight_grad: float32 [9, 48, 288], replicated
- second_bias_grad: float32 [48], replicated
The draws below stay inside these ranges and needn't reach their ends.
All inputs are finite; a program needn't handle non-finite values. No bound on the sum of `active` on one device may be relied on, other than what follows from the above.
Results may differ from the reference program's by a relative error of at most 0.0064.
Values may be sent and summed in bfloat16 or wider, within the bound.
A program may use at most 128 MiB of HBM per device.

```python
import math
import jax
import jax.numpy as jnp
from jax import lax

SX = 8
SY = 16
HID = 32
CIN = 6
K = 8
NT = 48
NZ = 64
OUTC = 48


def place_ends(drawn, own_key, least, top_value):
    longest = drawn.shape.index(max(drawn.shape))
    spots = []
    for shift in (0, 1):
        where = [jax.random.randint(jax.random.fold_in(own_key, axis), (), 0, length) for axis, length in enumerate(drawn.shape)]
        where[longest] = (where[longest] + shift) % drawn.shape[longest]
        spots.append(tuple(where))
    return drawn.at[spots[0]].set(least).at[spots[1]].set(top_value)


def block_scale(key, dims, shards, least, top_value):
    gain, own = 1.0, jax.random.fold_in(key, 6)
    for dim, shards_of in shards:
        steps = jnp.exp(jax.random.uniform(jax.random.fold_in(own, dim), (shards_of,), jnp.float32, least / len(shards), top_value / len(shards)))
        gain = gain * jnp.repeat(steps, dims[dim] // shards_of).reshape([-1 if axis == dim else 1 for axis in range(len(dims))])
    return gain


def scatter_about(key, extent, scale, limit, shards=(), held_as=jnp.bfloat16):
    values = jax.random.normal(key, extent, jnp.float32) * scale
    if len(shards) > 0:
        values = block_scale(key, extent, shards, -0.22, 0.18) * values
    return jnp.clip(values, min=-limit, max=limit).astype(held_as)


def setup_inputs(seed: int = 0) -> dict:
    key_of = jax.random.split(jax.random.key(seed), 10)
    link_phases = scatter_about(key_of[0], (3, 2, NT, NZ, SX * SY), 0.6, 4.0, ((2, 16), (3, 16)), jnp.float32)
    active = place_ends((jax.random.randint(key_of[1], (NT, NZ, SX * SY), 0, 2) < 1).astype(jnp.int32), jax.random.fold_in(key_of[1], 1), 0, 1)
    bin_index = place_ends(jax.random.randint(key_of[2], (2, NT, NZ, SX * SY), 0, K), jax.random.fold_in(key_of[2], 1), 0, K - 1).astype(jnp.int32)
    first_weight = scatter_about(key_of[3], (9, HID, 9 * CIN), (81 * CIN) ** -0.5, 0.25)
    first_bias = scatter_about(key_of[4], (HID,), 0.5, 3.0, (), jnp.float32)
    second_weight = scatter_about(key_of[5], (9, OUTC, 9 * HID), (81 * HID) ** -0.5, 0.125)
    second_bias = scatter_about(key_of[6], (OUTC,), 0.5, 3.0, (), jnp.float32)
    cotangent = scatter_about(key_of[7], (2, NT, NZ, SX * SY), 1.0, 6.0, ((1, 16), (2, 16)), jnp.float32)
    logdet_cotangent = scatter_about(key_of[8], (NT, NZ, SX * SY), 1.0, 6.0, ((0, 16), (1, 16)), jnp.float32)
    return dict(link_phases=link_phases, active=active, bin_index=bin_index, first_weight=first_weight, first_bias=first_bias, second_weight=second_weight, second_bias=second_bias, cotangent=cotangent, logdet_cotangent=logdet_cotangent)


min_share = 0.001
min_deriv = 0.001

def shifted(field, step_y, step_x):
    leading = field.shape[:-1]
    planar = field.reshape(leading + (SY, SX))
    planar = jnp.roll(planar, (-step_y, -step_x), axis=(-2, -1))
    return planar.reshape(leading + (SY * SX,))

def plane_columns(field, orient):
    blocks = []
    for step_y in (-1, 0, 1):
        for step_x in (-1, 0, 1):
            blocks.append(shifted(field, orient * step_y, orient * step_x))
    return jnp.concatenate(blocks, axis=0)

def flip_weight(weight):
    outs_n = weight.shape[1]
    chans = weight.shape[2] // 9
    return weight.reshape(9, outs_n, 9, chans).transpose(0, 3, 2, 1).reshape(9, chans, 9 * outs_n)

def lattice_stencil(field, weight, orient):
    channels = field.shape[0]

    def one_slice(t_index):
        total = jnp.zeros((weight.shape[1], NZ * SX * SY), jnp.float32)
        for step_t in (-1, 0, 1):
            layer = lax.dynamic_index_in_dim(field, (t_index + orient * step_t) % NT, 1, keepdims=False)
            columns = plane_columns(layer, orient)
            for step_z in (-1, 0, 1):
                rolled = jnp.roll(columns, -orient * step_z, axis=1).reshape(9 * channels, NZ * SX * SY)
                total = total + jnp.dot(weight[3 * (step_t + 1) + step_z + 1], rolled, preferred_element_type=jnp.float32)
        return total.reshape(weight.shape[1], NZ, SX * SY)
    result = lax.map(one_slice, jnp.arange(NT, dtype=jnp.int32))
    return jnp.transpose(result, (1, 0, 2, 3))

def weight_terms(grad, field):
    channels = field.shape[0]
    outs_n = grad.shape[0]

    def one_slice(total, t_index):
        grad_slice = lax.dynamic_index_in_dim(grad, t_index, 1, keepdims=False).reshape(outs_n, NZ * SX * SY)
        pieces = []
        for step_t in (-1, 0, 1):
            layer = lax.dynamic_index_in_dim(field, (t_index + step_t) % NT, 1, keepdims=False)
            columns = plane_columns(layer, 1)
            for step_z in (-1, 0, 1):
                rolled = jnp.roll(columns, -step_z, axis=1).reshape(9 * channels, NZ * SX * SY)
                pieces.append(lax.dot_general(grad_slice, rolled, (((1,), (1,)), ((), ())), preferred_element_type=jnp.float32))
        return (total + jnp.stack(pieces), None)
    start = jnp.zeros((9, outs_n, 9 * channels), jnp.float32)
    total, _ = lax.scan(one_slice, start, jnp.arange(NT, dtype=jnp.int32))
    return total

def full_phases(given):
    return jnp.concatenate([given, -(given[0:1] + given[1:2])], axis=0)

def loop_features(x_link, y_link):
    x_full = full_phases(x_link)
    y_full = full_phases(y_link)
    plaquette = x_full + shifted(y_full, 0, 1) - shifted(x_full, 1, 0) - y_full
    rect_wide = x_full + shifted(x_full, 0, 1) + shifted(y_full, 0, 2) - shifted(x_full, 1, 1) - shifted(x_full, 1, 0) - y_full
    rect_tall = x_full + shifted(y_full, 0, 1) + shifted(y_full, 1, 1) - shifted(x_full, 2, 0) - shifted(y_full, 1, 0) - y_full
    blocks = []
    for loop in (plaquette, rect_wide, rect_tall):
        blocks.append(lax.optimization_barrier(jnp.mean(jnp.cos(loop), axis=0, keepdims=True)))
        blocks.append(lax.optimization_barrier(jnp.mean(jnp.sin(loop), axis=0, keepdims=True)))
    return jnp.concatenate(blocks, axis=0)

def spline(phases, params, bin_index):
    rest = phases.shape[1:]
    raw = params.reshape((2, 3, K) + rest)
    widths = jax.nn.softplus(raw[:, 0])
    widths = min_share + (1.0 - K * min_share) * widths / lax.optimization_barrier(jnp.sum(widths, axis=1, keepdims=True))
    heights = jax.nn.softplus(raw[:, 1])
    heights = min_share + (1.0 - K * min_share) * heights / lax.optimization_barrier(jnp.sum(heights, axis=1, keepdims=True))
    derivs = min_deriv + jax.nn.softplus(raw[:, 2])
    levels = jnp.arange(K, dtype=jnp.int32).reshape((1, K) + (1,) * len(rest))
    chosen = bin_index[:, None].astype(jnp.int32)
    pick = (levels == chosen).astype(jnp.float32)
    below = (levels < chosen).astype(jnp.float32)
    after = (levels == (chosen + 1) % K).astype(jnp.float32)
    width = lax.optimization_barrier(jnp.sum(pick * widths, axis=1))
    height = lax.optimization_barrier(jnp.sum(pick * heights, axis=1))
    base = -math.pi + 2.0 * math.pi * lax.optimization_barrier(jnp.sum(below * heights, axis=1))
    left_der = lax.optimization_barrier(jnp.sum(pick * derivs, axis=1))
    right_der = lax.optimization_barrier(jnp.sum(after * derivs, axis=1))
    bin_slope = height / width
    inside = jax.nn.sigmoid(phases)
    spread = inside * (1.0 - inside)
    denom = bin_slope + (left_der + right_der - 2.0 * bin_slope) * spread
    new_phase = base + 2.0 * math.pi * height * (bin_slope * inside * inside + left_der * spread) / denom
    numer = right_der * inside * inside + 2.0 * bin_slope * spread + left_der * (1.0 - inside) ** 2
    logdet = jnp.log(2.0 * math.pi * height) + jnp.log(bin_slope) + jnp.log(numer) - 2.0 * jnp.log(denom) - jax.nn.softplus(phases) - jax.nn.softplus(-phases)
    return (new_phase, lax.optimization_barrier(jnp.sum(logdet, axis=0)))

def silu_slope(value):
    sigma_v = jax.nn.sigmoid(value)
    return sigma_v * (1.0 + value * (1.0 - sigma_v))

def reference(link_phases, active, bin_index, first_weight, first_bias, second_weight, second_bias, cotangent, logdet_cotangent):
    x_link, y_link, t_link = (link_phases[0], link_phases[1], link_phases[2])
    feats, feat_pull = jax.vjp(loop_features, x_link, y_link)
    feats_half = feats.astype(jnp.bfloat16)
    preact = lattice_stencil(feats_half, first_weight, 1) + first_bias[:, None, None, None]
    hidden = jax.nn.silu(preact).astype(jnp.bfloat16)
    params = lattice_stencil(hidden, second_weight, 1) + second_bias[:, None, None, None]
    loop_phase = x_link + shifted(t_link, 0, 1) - jnp.roll(x_link, -1, axis=1) - t_link
    live_mask = active.astype(jnp.float32)

    def local_spline(phases, values):
        return spline(phases, values, bin_index)
    _, spline_pull = jax.vjp(local_spline, loop_phase, params)
    phase_part, param_grad = spline_pull((-live_mask * cotangent, live_mask * logdet_cotangent))
    phase_grad = phase_part + live_mask * cotangent
    x_grad = phase_grad - jnp.roll(phase_grad, 1, axis=1)
    t_grad = cotangent - phase_grad + shifted(phase_grad, 0, -1)
    param_half = param_grad.astype(jnp.bfloat16)
    hidden_grad = lattice_stencil(param_half, flip_weight(second_weight), -1)
    preact_grad = hidden_grad * silu_slope(preact)
    preact_half = preact_grad.astype(jnp.bfloat16)
    feature_grad = lattice_stencil(preact_half, flip_weight(first_weight), -1)
    x_ctx, y_ctx = feat_pull(feature_grad)
    link_grad = jnp.stack([x_grad + x_ctx, y_ctx, t_grad])
    norm_root = math.sqrt(NT * NZ * SX * SY)
    second_weight_grad = weight_terms(param_half, hidden) / norm_root
    second_bias_grad = lax.optimization_barrier(jnp.sum(param_grad, axis=(1, 2, 3))) / norm_root
    first_weight_grad = weight_terms(preact_half, feats_half) / norm_root
    first_bias_grad = lax.optimization_barrier(jnp.sum(preact_grad, axis=(1, 2, 3))) / norm_root
    return (link_grad, first_weight_grad, first_bias_grad, second_weight_grad, second_bias_grad)
```

```python
import functools
import math

import jax
import jax.numpy as jnp
from jax import lax
from jax.experimental import pallas as pl
from jax.experimental.pallas import tpu as pltpu
from jax.sharding import PartitionSpec as P

K = 8
LT = 3
LZ = 4
LANES = 128
HID = 32
OUTC = 48
PLANES = LT * LZ
MESH_ID = pl.DeviceIdType.MESH

min_share = 0.001
min_deriv = 0.001
keep_share = 1.0 - K * min_share
two_pi = 2.0 * math.pi

f32 = jnp.float32
bf16 = jnp.bfloat16


def lane_x(rows):
    return lax.broadcasted_iota(jnp.int32, (rows, LANES), 1) % 8


def rolled(value, amount):
    amount = amount % LANES
    if amount == 0:
        return value
    return pltpu.roll(value, amount, 1)


def shifted(value, step_y, step_x):
    near = rolled(value, -(8 * step_y + step_x))
    if step_x == 0:
        return near
    xs = lane_x(value.shape[0])
    if step_x > 0:
        wrap = rolled(value, -(8 * step_y + step_x - 8))
        return jnp.where(xs < 8 - step_x, near, wrap)
    wrap = rolled(value, -(8 * step_y + step_x + 8))
    return jnp.where(xs >= -step_x, near, wrap)


def nine_shifts(value):
    return [shifted(value, sy, sx) for sy in (-1, 0, 1) for sx in (-1, 0, 1)]


def shift_sum(blocks):
    total = None
    for ix, dx in enumerate((-1, 0, 1)):
        part = None
        for iy, dy in enumerate((-1, 0, 1)):
            piece = rolled(blocks[3 * iy + ix], 8 * dy)
            part = piece if part is None else part + piece
        part = shifted(part, 0, -dx)
        total = part if total is None else total + part
    return total


def sin_cos(angle):
    turns = jnp.floor(angle * (2.0 / math.pi) + 0.5)
    rest = angle - turns * 1.5703125
    rest = rest - turns * 4.837512969970703125e-4
    rest = rest - turns * 7.54978995489188e-8
    sq = rest * rest
    s = rest + rest * sq * (-1.6666654611e-1 + sq * (8.3321608736e-3 - sq * 1.9515295891e-4))
    c = 1.0 - 0.5 * sq + sq * sq * (
        4.166664568298827e-2 + sq * (-1.388731625493765e-3 + sq * 2.443315711809948e-5)
    )
    quad = turns.astype(jnp.int32)
    swap = (quad & 1) == 1
    sin_v = jnp.where(swap, c, s)
    cos_v = jnp.where(swap, s, c)
    sin_v = jnp.where((quad & 2) == 2, -sin_v, sin_v)
    cos_v = jnp.where(((quad + 1) & 2) == 2, -cos_v, cos_v)
    return sin_v, cos_v


def loop_phases(x_two, y_two):
    plaq, wide, tall = [], [], []
    for x, y in zip(x_two, y_two):
        y_x = shifted(y, 0, 1)
        x_y = shifted(x, 1, 0)
        plaq.append(x + y_x - x_y - y)
        wide.append(x + shifted(x, 0, 1) + shifted(y, 0, 2) - shifted(x, 1, 1) - x_y - y)
        tall.append(x + y_x + shifted(y, 1, 1) - shifted(x, 2, 0) - shifted(y, 1, 0) - y)
    out = []
    for two in (plaq, wide, tall):
        out.append((two[0], two[1], -(two[0] + two[1])))
    return out


DIRS = [(dt, dz) for dt in (-1, 0, 1) for dz in (-1, 0, 1) if (dt, dz) != (0, 0)]


def neighbour(dt, dz):
    nt, nz = lax.axis_size("ta"), lax.axis_size("gz")
    mt, mz = lax.axis_index("ta"), lax.axis_index("gz")
    return (lax.rem(mt + dt + nt, nt), lax.rem(mz + dz + nz, nz))


def main_kernel(
    links, act, bins, w1p, b1, w2k, b2, wt2, wt1, cot, ldc,
    out_link, out_grad,
    lbuf, fs, fcols, pres, cols, sigs, red, coef, xab, pgs, pgr, pgv,
    pbuf, qbuf, fgs, g1s,
    send_l, recv_l, send_p, recv_p, send_q, recv_q, send_g, recv_g,
):
    barrier = pltpu.get_barrier_semaphore()
    for dt, dz in DIRS:
        pl.semaphore_signal(barrier, inc=1, device_id=neighbour(dt, dz), device_id_type=MESH_ID)

    for comp in range(4):
        for t in range(LT):
            lbuf[2 + t, pl.ds(8 + comp, LZ, stride=4), :] = links[pl.ds(comp * PLANES + t * LZ, LZ), :]
    pl.semaphore_wait(barrier, len(DIRS))

    t_from = {-1: slice(2, 4), 0: slice(2, 5), 1: slice(3, 5)}
    t_into = {-1: slice(5, 7), 0: slice(2, 5), 1: slice(0, 2)}
    z_from = {-1: slice(8, 16), 0: slice(8, 24), 1: slice(16, 24)}
    z_into = {-1: slice(24, 32), 0: slice(8, 24), 1: slice(0, 8)}
    link_copies = []
    for i, (dt, dz) in enumerate(DIRS):
        copy = pltpu.make_async_remote_copy(
            src_ref=lbuf.at[t_from[dt], z_from[dz]],
            dst_ref=lbuf.at[t_into[dt], z_into[dz]],
            send_sem=send_l.at[i], recv_sem=recv_l.at[i],
            device_id=neighbour(dt, dz), device_id_type=MESH_ID,
        )
        copy.start()
        link_copies.append(copy)
    fs[...] = jnp.zeros_like(fs)
    for copy in link_copies:
        copy.wait()

    def feature_slice(t, carry):
        x_two = [lbuf[t, pl.ds(comp, 8, stride=4), :] for comp in (0, 1)]
        y_two = [lbuf[t, pl.ds(comp, 8, stride=4), :] for comp in (2, 3)]
        for which, three in enumerate(loop_phases(x_two, y_two)):
            pairs = [sin_cos(psi) for psi in three]
            fs[pl.ds(2 * which, 8, stride=8), :] = (pairs[0][1] + pairs[1][1] + pairs[2][1]) * (1.0 / 3.0)
            fs[pl.ds(2 * which + 1, 8, stride=8), :] = (pairs[0][0] + pairs[1][0] + pairs[2][0]) * (1.0 / 3.0)
        row = pl.multiple_of(t * 80, 16)
        for z in range(8):
            blocks = nine_shifts(fs[z * 8 : z * 8 + 8, :])
            blocks.append(jnp.zeros((8, LANES), f32))
            fcols[pl.ds(row, 80), z * LANES : (z + 1) * LANES] = jnp.concatenate(blocks, axis=0).astype(bf16)
        return carry

    lax.fori_loop(0, 7, feature_slice, 0)

    def hidden_slice(t, carry):
        got = jnp.dot(
            w1p[...], fcols[pl.ds(pl.multiple_of(t * 80, 16), 240), :], preferred_element_type=f32
        )
        pre = got[0:32, 0:768] + got[32:64, 128:896] + got[64:96, 256:1024] + b1[...]
        pres[t] = pre[:, 128:640]
        hid = pre / (1.0 + jnp.exp(-pre))
        row = pl.multiple_of(t * 288, 16)
        for z in range(6):
            blocks = nine_shifts(hid[:, z * LANES : (z + 1) * LANES])
            cols[pl.ds(row, 288), z * LANES : (z + 1) * LANES] = jnp.concatenate(blocks, axis=0).astype(bf16)
        return carry

    lax.fori_loop(0, 5, hidden_slice, 0)

    level = lax.broadcasted_iota(jnp.int32, (K, LANES), 0)

    def param_slice(t, carry):
        got = jnp.dot(
            w2k[...], cols[pl.ds(pl.multiple_of(t * 288, 16), 864), :], preferred_element_type=f32
        )
        par = got[0:48, 0:512] + got[48:96, 128:640] + got[96:144, 256:768] + b2[...]
        grow = jnp.exp(-jnp.abs(par))
        soft = jnp.maximum(par, 0.0) + jnp.log1p(grow)
        sigs[t] = jnp.where(par >= 0.0, 1.0, grow) / (1.0 + grow)
        for z in range(LZ):
            for c in range(2):
                plane = t * LZ + z
                chosen = bins[pl.ds(c * PLANES + plane, 1), :]
                pick = level == chosen
                below = level < chosen
                after = level == ((chosen + 1) & 7)
                cut = soft[c * 24 : c * 24 + 24, z * LANES : (z + 1) * LANES]
                sw, sh, sd = cut[0:8], cut[8:16], cut[16:24]
                sums = (
                    sw, jnp.where(pick, sw, 0.0),
                    sh, jnp.where(pick, sh, 0.0), jnp.where(below, sh, 0.0),
                    jnp.where(pick, sd, 0.0), jnp.where(after, sd, 0.0),
                )
                for q, value in enumerate(sums):
                    red[q, pl.ds(c * 16 + plane, 1), :] = jnp.sum(value, axis=0, keepdims=True)
        return carry

    lax.fori_loop(0, LT, param_slice, 0)

    live = act[...].astype(f32)
    g_log = live * ldc[...]
    for c in range(2):
        x = links[c * 12 : c * 12 + 12, :]
        tl = links[48 + c * 12 : 60 + c * 12, :]
        xab[0:8, :] = links[c * 12 + 4 : c * 12 + 12, :]
        xab[8:12, :] = lbuf[5, pl.ds(8 + c, LZ, stride=4), :]
        theta = x + shifted(tl, 0, 1) - xab[0:12, :] - tl
        my_cot = cot[c * 12 : c * 12 + 12, :]
        g_new = -live * my_cot
        rows = slice(c * 16, c * 16 + 12)
        sum_w, pick_w = red[0, rows, :], red[1, rows, :]
        sum_h, pick_h, low_h = red[2, rows, :], red[3, rows, :], red[4, rows, :]
        d0 = min_deriv + red[5, rows, :]
        d1 = min_deriv + red[6, rows, :]
        inv_w, inv_h = 1.0 / sum_w, 1.0 / sum_h
        frac_w, frac_h, frac_low = pick_w * inv_w, pick_h * inv_h, low_h * inv_h
        width = min_share + keep_share * frac_w
        height = min_share + keep_share * frac_h
        r = height / width
        u = 1.0 / (1.0 + jnp.exp(-theta))
        v = 1.0 - u
        q = u * v
        den = r + (d0 + d1 - 2.0 * r) * q
        top = r * u * u + d0 * q
        numer = d1 * u * u + 2.0 * r * q + d0 * v * v
        inv_den = 1.0 / den
        g_top = g_new * two_pi * height * inv_den
        g_den = -(g_top * top + 2.0 * g_log) * inv_den
        g_num = g_log / numer
        g_h = g_new * two_pi * top * inv_den + g_log / height
        g_r = g_top * u * u + g_den * (1.0 - 2.0 * q) + 2.0 * g_num * q + g_log / r
        g_d0 = (g_top + g_den) * q + g_num * v * v
        g_d1 = g_den * q + g_num * u * u
        g_q = g_top * d0 + g_den * (d0 + d1 - 2.0 * r) + 2.0 * g_num * r
        g_u = 2.0 * g_top * r * u + 2.0 * g_num * (d1 * u - d0 * v) + g_q * (1.0 - 2.0 * u)
        g_theta = g_u * q + g_log * (1.0 - 2.0 * u)
        all_h = g_h + g_r / width
        all_w = -g_r * r / width
        base = two_pi * g_new
        a_w = keep_share * all_w * inv_w
        coef[0, rows, :] = a_w
        coef[1, rows, :] = a_w * frac_w
        coef[2, rows, :] = keep_share * all_h * inv_h
        coef[3, rows, :] = keep_share * base * inv_h
        coef[4, rows, :] = keep_share * (all_h * frac_h + base * frac_low) * inv_h
        coef[5, rows, :] = g_d0
        coef[6, rows, :] = g_d1
        grad = g_theta + live * my_cot
        pgv[c, 4:16, :] = grad
        pgs[c * 4 : c * 4 + 4, :] = grad[8:12, :]

    phase_copy = pltpu.make_async_remote_copy(
        src_ref=pgs, dst_ref=pgr, send_sem=send_g, recv_sem=recv_g,
        device_id=neighbour(1, 0), device_id_type=MESH_ID,
    )
    phase_copy.start()

    def param_grad_slice(t, total):
        for z in range(LZ):
            plane = t * LZ + z
            parts = []
            for c in range(2):
                chosen = bins[pl.ds(c * PLANES + plane, 1), :]
                pick = level == chosen
                below = level < chosen
                after = level == ((chosen + 1) & 7)
                a = [coef[k, pl.ds(c * 16 + plane, 1), :] for k in range(7)]
                sig = sigs[t, c * 24 : c * 24 + 24, z * LANES : (z + 1) * LANES]
                parts.append((jnp.where(pick, a[0], 0.0) - a[1]) * sig[0:8])
                parts.append((jnp.where(pick, a[2], jnp.where(below, a[3], 0.0)) - a[4]) * sig[8:16])
                parts.append((jnp.where(pick, a[5], jnp.where(after, a[6], 0.0))) * sig[16:24])
            grad = jnp.concatenate(parts, axis=0)
            pbuf[t + 1, z + 1] = grad.astype(bf16)
            total = total + grad
        return total

    bias2 = jnp.sum(
        lax.fori_loop(0, LT, param_grad_slice, jnp.zeros((OUTC, LANES), f32)), axis=1, keepdims=True
    )

    h_from = {-1: slice(1, 2), 0: slice(1, 4), 1: slice(3, 4)}
    h_into = {-1: slice(4, 5), 0: slice(1, 4), 1: slice(0, 1)}
    v_from = {-1: slice(1, 2), 0: slice(1, 5), 1: slice(4, 5)}
    v_into = {-1: slice(5, 6), 0: slice(1, 5), 1: slice(0, 1)}

    def send_halo(buf, send, recv):
        copies = []
        for i, (dt, dz) in enumerate(DIRS):
            copy = pltpu.make_async_remote_copy(
                src_ref=buf.at[h_from[dt], v_from[dz]],
                dst_ref=buf.at[h_into[dt], v_into[dz]],
                send_sem=send.at[i], recv_sem=recv.at[i],
                device_id=neighbour(dt, dz), device_id_type=MESH_ID,
            )
            copy.start()
            copies.append(copy)
        return copies

    param_copies = send_halo(pbuf, send_p, recv_p)

    def spread(buf, t, rows):
        own = jnp.concatenate([buf[t + 1, z + 1] for z in range(LZ)], axis=1)
        one = jnp.zeros((rows, LANES), bf16)
        two = jnp.zeros((rows, 2 * LANES), bf16)
        return jnp.concatenate(
            [
                jnp.concatenate([own, two], axis=1),
                jnp.concatenate([one, own, one], axis=1),
                jnp.concatenate([two, own], axis=1),
            ],
            axis=0,
        )

    nt_dims = (((1,), (1,)), ((), ()))
    spread_p = [spread(pbuf, t, OUTC) for t in range(LT)]
    g2 = []
    for i in range(3):
        total = None
        for t in range(LT):
            part = lax.dot_general(
                spread_p[t], cols[(t + i) * 288 : (t + i + 1) * 288, :], nt_dims, preferred_element_type=f32
            )
            total = part if total is None else total + part
        g2.append(total)
        out_grad[i * 144 : (i + 1) * 144, 0:256] = total[:, 0:256].astype(bf16)
        g1s[i * 144 : (i + 1) * 144, 0:32] = total[:, 256:288]

    for copy in param_copies:
        copy.wait()

    def stacked(buf, t):
        rows = []
        for i in range(3):
            for j in range(3):
                rows.append(jnp.concatenate([buf[t + 2 - i, z + 2 - j] for z in range(LZ)], axis=1))
        return jnp.concatenate(rows, axis=0)

    def hidden_grad_slice(t, total):
        got = jnp.dot(wt2[...], stacked(pbuf, t), preferred_element_type=f32)
        for z in range(LZ):
            lanes = slice(z * LANES, (z + 1) * LANES)
            grad = shift_sum([got[b * HID : (b + 1) * HID, lanes] for b in range(9)])
            pre = pres[t + 1, :, lanes]
            sig = 1.0 / (1.0 + jnp.exp(-pre))
            grad = grad * (sig * (1.0 + pre * (1.0 - sig)))
            qbuf[t + 1, z + 1] = grad.astype(bf16)
            total = total + grad
        return total

    bias1 = jnp.sum(
        lax.fori_loop(0, LT, hidden_grad_slice, jnp.zeros((HID, LANES), f32)), axis=1, keepdims=True
    )

    preact_copies = send_halo(qbuf, send_q, recv_q)

    spread_q = [spread(qbuf, t, HID) for t in range(LT)]
    g1 = []
    for i in range(3):
        total = None
        for t in range(LT):
            row = (t + 1 + i) * 80
            part = lax.dot_general(
                spread_q[t], fcols[row : row + 80, 128:896], nt_dims, preferred_element_type=f32
            )
            total = part if total is None else total + part
        g1.append(jnp.concatenate([total, jnp.zeros((96, 48), f32)], axis=1))
    first = jnp.concatenate(
        [pltpu.roll(g, 48, 1) for g in g1] + [jnp.zeros((144, LANES), f32)], axis=0
    )
    bias = jnp.concatenate([bias2, bias1, jnp.zeros((432 - 80, 1), f32)], axis=0)
    lane = lax.broadcasted_iota(jnp.int32, (432, LANES), 1)
    tail = jnp.where(lane < 32, g1s[...], jnp.where(lane == 32, bias, first))
    out_grad[0:432, 256:384] = tail.astype(bf16)
    out_grad[432:512, :] = jnp.zeros((80, 384), bf16)

    x_two = [links[0:12, :], links[12:24, :]]
    y_two = [links[24:36, :], links[36:48, :]]
    pairs = [[sin_cos(psi) for psi in three] for three in loop_phases(x_two, y_two)]

    phase_copy.wait()
    for copy in preact_copies:
        copy.wait()

    def feature_grad_slice(t, carry):
        got = jnp.dot(wt1[...], stacked(qbuf, t), preferred_element_type=f32)
        for z in range(LZ):
            lanes = slice(z * LANES, (z + 1) * LANES)
            grad = shift_sum([got[b * 8 : (b + 1) * 8, lanes] for b in range(9)])
            fgs[pl.ds(pl.multiple_of((t * LZ + z) * 8, 8), 8), :] = grad
        return carry

    lax.fori_loop(0, LT, feature_grad_slice, 0)

    third = 1.0 / 3.0
    loop_grads = []
    for which in range(3):
        g_cos = fgs[pl.ds(2 * which, PLANES, stride=8), :] * third
        g_sin = fgs[pl.ds(2 * which + 1, PLANES, stride=8), :] * third
        three = [g_sin * cos_v - g_cos * sin_v for sin_v, cos_v in pairs[which]]
        loop_grads.append((three[0] - three[2], three[1] - three[2]))
    for c in range(2):
        dp, dw, dr = loop_grads[0][c], loop_grads[1][c], loop_grads[2][c]
        side = dp + dr
        x_ctx = (
            dp + dw + dr
            - shifted(dp + dw, -1, 0)
            + shifted(dw, 0, -1)
            - shifted(dw, -1, -1)
            - shifted(dr, -2, 0)
        )
        y_ctx = (
            shifted(side, 0, -1)
            - side
            - dw
            + shifted(dw, 0, -2)
            + shifted(dr, -1, -1)
            - shifted(dr, -1, 0)
        )
        pgv[c, 0:4, :] = pgr[c * 4 : c * 4 + 4, :]
        grad = pgv[c, 4:16, :]
        prev = pgv[c, 0:12, :]
        out_link[c * 12 : c * 12 + 12, :] = grad - prev + x_ctx
        out_link[24 + c * 12 : 36 + c * 12, :] = y_ctx
        out_link[48 + c * 12 : 60 + c * 12, :] = cot[c * 12 : c * 12 + 12, :] - grad + shifted(grad, 0, -1)


def sum_kernel(scale, grad, out, got1, mid, got2, fin, send1, recv1, send2, recv2, send3, recv3):
    nt, nz = lax.axis_size("ta"), lax.axis_size("gz")
    mt, mz = lax.axis_index("ta"), lax.axis_index("gz")
    rows = grad.shape[0] // nt
    barrier = pltpu.get_barrier_semaphore()
    for k in range(1, nt):
        pl.semaphore_signal(barrier, inc=1, device_id=(lax.rem(mt + k, nt), mz), device_id_type=MESH_ID)
    for k in range(1, nz):
        pl.semaphore_signal(barrier, inc=1, device_id=(mt, lax.rem(mz + k, nz)), device_id_type=MESH_ID)
    pl.semaphore_wait(barrier, nt + nz - 2)

    copies = []
    for k in range(1, nt):
        peer = lax.rem(mt + k, nt)
        copy = pltpu.make_async_remote_copy(
            src_ref=grad.at[pl.ds(pl.multiple_of(peer * rows, 16), rows)],
            dst_ref=got1.at[k],
            send_sem=send1.at[k], recv_sem=recv1.at[k],
            device_id=(peer, mz), device_id_type=MESH_ID,
        )
        copy.start()
        copies.append(copy)
    total = grad[pl.ds(pl.multiple_of(mt * rows, 16), rows), :].astype(f32)
    for k, copy in enumerate(copies):
        copy.wait()
        total = total + got1[k + 1].astype(f32)
    mid[...] = (total * scale).astype(bf16)

    copies = []
    for k in range(1, nz):
        peer = lax.rem(mz + k, nz)
        copy = pltpu.make_async_remote_copy(
            src_ref=mid, dst_ref=got2.at[mz],
            send_sem=send2.at[k], recv_sem=recv2.at[k],
            device_id=(mt, peer), device_id_type=MESH_ID,
        )
        copy.start()
        copies.append(copy)
    got2[mz] = mid[...]
    for copy in copies:
        copy.wait()
    total = got2[0].astype(f32)
    for k in range(1, nz):
        total = total + got2[k].astype(f32)
    fin[...] = total.astype(bf16)

    copies = []
    mine = pl.ds(pl.multiple_of(mt * rows, 16), rows)
    for k in range(1, nt):
        peer = lax.rem(mt + k, nt)
        copy = pltpu.make_async_remote_copy(
            src_ref=fin, dst_ref=out.at[mine],
            send_sem=send3.at[k], recv_sem=recv3.at[k],
            device_id=(peer, mz), device_id_type=MESH_ID,
        )
        copy.start()
        copies.append(copy)
    out[mine, :] = fin[...]
    for copy in copies:
        copy.wait()


def vmem():
    return pl.BlockSpec(memory_space=pltpu.VMEM)


def local(
    link_phases, active, bin_index, first_weight, first_bias,
    second_weight, second_bias, cotangent, logdet_cotangent,
):
    nt, nz = lax.axis_size("ta"), lax.axis_size("gz")
    fw = first_weight.reshape(3, 3, HID, 9, 6)
    fw = jnp.pad(fw, ((0, 0), (0, 0), (0, 0), (0, 0), (0, 2))).reshape(3, 96, 72)
    wt1 = fw.reshape(288, 72).T
    w1p = jnp.pad(fw, ((0, 0), (0, 0), (0, 8))).transpose(1, 0, 2).reshape(96, 240)
    w2k = second_weight.reshape(3, 144, 288).transpose(1, 0, 2).reshape(144, 864)
    wt2 = second_weight.reshape(432, 288).T

    dma = pltpu.SemaphoreType.DMA
    out_link, out_grad = pl.pallas_call(
        main_kernel,
        out_shape=(
            jax.ShapeDtypeStruct((72, LANES), f32),
            jax.ShapeDtypeStruct((512, 384), bf16),
        ),
        in_specs=[vmem()] * 11,
        out_specs=(vmem(), vmem()),
        scratch_shapes=[
            pltpu.VMEM((7, 32, LANES), f32),
            pltpu.VMEM((64, LANES), f32),
            pltpu.VMEM((560, 1024), bf16),
            pltpu.VMEM((5, HID, 512), f32),
            pltpu.VMEM((1440, 768), bf16),
            pltpu.VMEM((LT, OUTC, 512), f32),
            pltpu.VMEM((7, 32, LANES), f32),
            pltpu.VMEM((7, 32, LANES), f32),
            pltpu.VMEM((16, LANES), f32),
            pltpu.VMEM((8, LANES), f32),
            pltpu.VMEM((8, LANES), f32),
            pltpu.VMEM((2, 16, LANES), f32),
            pltpu.VMEM((5, 6, OUTC, LANES), bf16),
            pltpu.VMEM((5, 6, HID, LANES), bf16),
            pltpu.VMEM((96, LANES), f32),
            pltpu.VMEM((432, LANES), f32),
            dma((8,)), dma((8,)), dma((8,)), dma((8,)), dma((8,)), dma((8,)), dma, dma,
        ],
        compiler_params=pltpu.CompilerParams(
            collective_id=0, has_side_effects=True, vmem_limit_bytes=40 * 1024 * 1024
        ),
        name="main_kernel",
    )(
        link_phases.reshape(72, LANES),
        active.reshape(PLANES, LANES),
        bin_index.reshape(2 * PLANES, LANES),
        w1p, first_bias.reshape(HID, 1), w2k, second_bias.reshape(OUTC, 1), wt2, wt1,
        cotangent.reshape(2 * PLANES, LANES),
        logdet_cotangent.reshape(PLANES, LANES),
    )

    rows = 512 // nt
    scale = 1.0 / math.sqrt(nt * nz * PLANES * LANES)
    summed = pl.pallas_call(
        functools.partial(sum_kernel, scale),
        out_shape=jax.ShapeDtypeStruct((512, 384), bf16),
        in_specs=[vmem()],
        out_specs=vmem(),
        scratch_shapes=[
            pltpu.VMEM((nt, rows, 384), bf16),
            pltpu.VMEM((rows, 384), bf16),
            pltpu.VMEM((nz, rows, 384), bf16),
            pltpu.VMEM((rows, 384), bf16),
            dma((nt,)), dma((nt,)), dma((nz,)), dma((nz,)), dma((nt,)), dma((nt,)),
        ],
        compiler_params=pltpu.CompilerParams(
            collective_id=1, has_side_effects=True, vmem_limit_bytes=40 * 1024 * 1024
        ),
        name="sum_kernel",
    )(out_grad)
    second = summed[0:432, 0:288].astype(f32).reshape(9, OUTC, 288)
    first = summed[0:288, 304:376].astype(f32).reshape(9, HID, 9, 8)[..., 0:6].reshape(9, HID, 54)
    bias = summed[0:80, 288].astype(f32)
    return (out_link.reshape(3, 2, LT, LZ, LANES), first, bias[48:80], second, bias[0:48])


def solution(mesh):
    return jax.shard_map(
        local,
        mesh=mesh,
        in_specs=(
            P(None, None, "ta", "gz", None),
            P("ta", "gz", None),
            P(None, "ta", "gz", None),
            P(), P(), P(), P(),
            P(None, "ta", "gz", None),
            P("ta", "gz", None),
        ),
        out_specs=(P(None, None, "ta", "gz", None), P(), P(), P(), P()),
        check_vma=False,
    )
```

```python
import functools
import math

import jax
import jax.numpy as jnp
from jax import lax
from jax.experimental import pallas as pl
from jax.experimental.pallas import tpu as pltpu
from jax.sharding import PartitionSpec as P

K = 8
LT = 3
LZ = 4
LANES = 128
HID = 32
OUTC = 48
PLANES = LT * LZ
MESH_ID = pl.DeviceIdType.MESH

min_share = 0.001
min_deriv = 0.001
keep_share = 1.0 - K * min_share
two_pi = 2.0 * math.pi

f32 = jnp.float32
bf16 = jnp.bfloat16


def lane_x(rows):
    return lax.broadcasted_iota(jnp.int32, (rows, LANES), 1) % 8


def rolled(value, amount):
    amount = amount % LANES
    if amount == 0:
        return value
    return pltpu.roll(value, amount, 1)


def shifted(value, step_y, step_x):
    near = rolled(value, -(8 * step_y + step_x))
    if step_x == 0:
        return near
    xs = lane_x(value.shape[0])
    if step_x > 0:
        wrap = rolled(value, -(8 * step_y + step_x - 8))
        return jnp.where(xs < 8 - step_x, near, wrap)
    wrap = rolled(value, -(8 * step_y + step_x + 8))
    return jnp.where(xs >= -step_x, near, wrap)


def nine_shifts(value):
    return [shifted(value, sy, sx) for sy in (-1, 0, 1) for sx in (-1, 0, 1)]


def shift_sum(blocks):
    total = None
    for ix, dx in enumerate((-1, 0, 1)):
        part = None
        for iy, dy in enumerate((-1, 0, 1)):
            piece = rolled(blocks[3 * iy + ix], 8 * dy)
            part = piece if part is None else part + piece
        part = shifted(part, 0, -dx)
        total = part if total is None else total + part
    return total


def sin_cos(angle):
    turns = jnp.floor(angle * (2.0 / math.pi) + 0.5)
    rest = angle - turns * 1.5703125
    rest = rest - turns * 4.837512969970703125e-4
    rest = rest - turns * 7.54978995489188e-8
    sq = rest * rest
    s = rest + rest * sq * (-1.6666654611e-1 + sq * (8.3321608736e-3 - sq * 1.9515295891e-4))
    c = 1.0 - 0.5 * sq + sq * sq * (
        4.166664568298827e-2 + sq * (-1.388731625493765e-3 + sq * 2.443315711809948e-5)
    )
    quad = turns.astype(jnp.int32)
    swap = (quad & 1) == 1
    sin_v = jnp.where(swap, c, s)
    cos_v = jnp.where(swap, s, c)
    sin_v = jnp.where((quad & 2) == 2, -sin_v, sin_v)
    cos_v = jnp.where(((quad + 1) & 2) == 2, -cos_v, cos_v)
    return sin_v, cos_v


def loop_phases(x_two, y_two):
    plaq, wide, tall = [], [], []
    for x, y in zip(x_two, y_two):
        y_x = shifted(y, 0, 1)
        x_y = shifted(x, 1, 0)
        plaq.append(x + y_x - x_y - y)
        wide.append(x + shifted(x, 0, 1) + shifted(y, 0, 2) - shifted(x, 1, 1) - x_y - y)
        tall.append(x + y_x + shifted(y, 1, 1) - shifted(x, 2, 0) - shifted(y, 1, 0) - y)
    out = []
    for two in (plaq, wide, tall):
        out.append((two[0], two[1], -(two[0] + two[1])))
    return out


DIRS = [(dt, dz) for dt in (-1, 0, 1) for dz in (-1, 0, 1) if (dt, dz) != (0, 0)]


def neighbour(dt, dz):
    nt, nz = lax.axis_size("ta"), lax.axis_size("gz")
    mt, mz = lax.axis_index("ta"), lax.axis_index("gz")
    return (lax.rem(mt + dt + nt, nt), lax.rem(mz + dz + nz, nz))


def main_kernel(
    scale, links, act, bins_in, first_w, b1, second_w, b2, cot_in, ldc_in,
    out_link, out2, out1,
    lk, bins, cot, site, w1p, w2k, wt2, wt1,
    lbuf, fs, fcols, pres, cols, sigs, red, coef, xab, pgs, pgr, pgv,
    pbuf, qbuf, fgs, tails, gm2, got_a, mid_b, got_b, part_c, all_c, fin_d,
    gm1, got_e, mid_f, got_f, fin_g,
    send_l, recv_l, send_p, recv_p, send_q, recv_q, send_g, recv_g,
    send_a, recv_a, send_b, recv_b, send_c, recv_c, send_d, recv_d,
    send_e, recv_e, send_f, recv_f, send_h, recv_h,
):
    nt, nz = lax.axis_size("ta"), lax.axis_size("gz")
    mt, mz = lax.axis_index("ta"), lax.axis_index("gz")
    barrier = pltpu.get_barrier_semaphore()
    corners = [(dt, dz) for dt, dz in DIRS if dt != 0 and dz != 0]
    for dt, dz in corners:
        pl.semaphore_signal(barrier, inc=1, device_id=neighbour(dt, dz), device_id_type=MESH_ID)
    for k in range(1, nt):
        pl.semaphore_signal(barrier, inc=1, device_id=(lax.rem(mt + k, nt), mz), device_id_type=MESH_ID)
    for k in range(1, nz):
        pl.semaphore_signal(barrier, inc=1, device_id=(mt, lax.rem(mz + k, nz)), device_id_type=MESH_ID)

    def to_others(axis, src, dst, send, recv):
        count, me = (nt, mt) if axis == "ta" else (nz, mz)
        copies = []
        for k in range(1, count):
            peer = lax.rem(me + k, count)
            copy = pltpu.make_async_remote_copy(
                src_ref=src(peer), dst_ref=dst(k),
                send_sem=send.at[k], recv_sem=recv.at[k],
                device_id=(peer, mz) if axis == "ta" else (mt, peer), device_id_type=MESH_ID,
            )
            copy.start()
            copies.append(copy)
        return copies

    for d in range(3):
        for c in range(2):
            for t in range(LT):
                lk[pl.ds(d * 24 + c * 12 + t * 4, LZ), :] = links[d, c, t]
    for comp in range(4):
        for t in range(LT):
            lbuf[2 + t, pl.ds(8 + comp, LZ, stride=4), :] = lk[pl.ds(comp * PLANES + t * LZ, LZ), :]
    pl.semaphore_wait(barrier, nt + nz - 2 + len(corners))

    t_from = {-1: slice(2, 4), 0: slice(2, 5), 1: slice(3, 5)}
    t_into = {-1: slice(5, 7), 0: slice(2, 5), 1: slice(0, 2)}
    z_from = {-1: slice(8, 16), 0: slice(8, 24), 1: slice(16, 24)}
    z_into = {-1: slice(24, 32), 0: slice(8, 24), 1: slice(0, 8)}
    link_copies = []
    for i, (dt, dz) in enumerate(DIRS):
        copy = pltpu.make_async_remote_copy(
            src_ref=lbuf.at[t_from[dt], z_from[dz]],
            dst_ref=lbuf.at[t_into[dt], z_into[dz]],
            send_sem=send_l.at[i], recv_sem=recv_l.at[i],
            device_id=neighbour(dt, dz), device_id_type=MESH_ID,
        )
        copy.start()
        link_copies.append(copy)
    fs[...] = jnp.zeros_like(fs)

    for t in range(LT):
        site[0, pl.ds(t * LZ, LZ), :] = act[t].astype(f32)
        site[1, pl.ds(t * LZ, LZ), :] = ldc_in[t]
        for c in range(2):
            bins[pl.ds(c * 12 + t * LZ, LZ), :] = bins_in[c, t]
            cot[pl.ds(c * 12 + t * LZ, LZ), :] = cot_in[c, t]
    nt_dims = (((1,), (1,)), ((), ()))

    def one_hot(rows, padded_dim):
        shape = (rows, 54) if padded_dim == 0 else (54, rows)
        wide = lax.broadcasted_iota(jnp.int32, shape, padded_dim)
        tight = lax.broadcasted_iota(jnp.int32, shape, 1 - padded_dim)
        hit = (wide < 72) & (wide % 8 < 6) & (tight == (wide // 8) * 6 + wide % 8)
        return jnp.where(hit, 1.0, 0.0).astype(bf16)

    spread80 = one_hot(80, 1)
    w1p[...] = jnp.concatenate(
        [
            jnp.dot(first_w[i * 96 : (i + 1) * 96, :], spread80, preferred_element_type=f32)
            for i in range(3)
        ],
        axis=1,
    ).astype(bf16)
    wt1[...] = lax.dot_general(
        one_hot(72, 0), first_w[...], nt_dims, preferred_element_type=f32
    ).astype(bf16)
    w2k[...] = jnp.concatenate(
        [second_w[i * 144 : (i + 1) * 144, :].astype(f32) for i in range(3)], axis=1
    ).astype(bf16)
    diag = lax.broadcasted_iota(jnp.int32, (288, 288), 0) == lax.broadcasted_iota(jnp.int32, (288, 288), 1)
    wt2[...] = lax.dot_general(
        jnp.where(diag, 1.0, 0.0).astype(bf16), second_w[...], nt_dims, preferred_element_type=f32
    ).astype(bf16)

    def as_column(row_ref, count):
        eye = lax.broadcasted_iota(jnp.int32, (count, count), 0) == lax.broadcasted_iota(
            jnp.int32, (count, count), 1
        )
        return jnp.sum(jnp.where(eye, row_ref[...], 0.0), axis=1, keepdims=True)

    b1_col, b2_col = as_column(b1, HID), as_column(b2, OUTC)
    for copy in link_copies:
        copy.wait()

    def feature_slice(t, carry):
        x_two = [lbuf[t, pl.ds(comp, 8, stride=4), :] for comp in (0, 1)]
        y_two = [lbuf[t, pl.ds(comp, 8, stride=4), :] for comp in (2, 3)]
        for which, three in enumerate(loop_phases(x_two, y_two)):
            pairs = [sin_cos(psi) for psi in three]
            fs[pl.ds(2 * which, 8, stride=8), :] = (pairs[0][1] + pairs[1][1] + pairs[2][1]) * (1.0 / 3.0)
            fs[pl.ds(2 * which + 1, 8, stride=8), :] = (pairs[0][0] + pairs[1][0] + pairs[2][0]) * (1.0 / 3.0)
        row = pl.multiple_of(t * 80, 16)
        for z in range(8):
            blocks = nine_shifts(fs[z * 8 : z * 8 + 8, :])
            blocks.append(jnp.zeros((8, LANES), f32))
            fcols[pl.ds(row, 80), z * LANES : (z + 1) * LANES] = jnp.concatenate(blocks, axis=0).astype(bf16)
        return carry

    lax.fori_loop(0, 7, feature_slice, 0)

    def hidden_slice(t, carry):
        got = jnp.dot(
            w1p[...], fcols[pl.ds(pl.multiple_of(t * 80, 16), 240), :], preferred_element_type=f32
        )
        pre = got[0:32, 0:768] + got[32:64, 128:896] + got[64:96, 256:1024] + b1_col
        pres[t] = pre[:, 128:640]
        hid = pre / (1.0 + jnp.exp(-pre))
        row = pl.multiple_of(t * 288, 16)
        for z in range(6):
            blocks = nine_shifts(hid[:, z * LANES : (z + 1) * LANES])
            cols[pl.ds(row, 288), z * LANES : (z + 1) * LANES] = jnp.concatenate(blocks, axis=0).astype(bf16)
        return carry

    lax.fori_loop(0, 5, hidden_slice, 0)

    level = lax.broadcasted_iota(jnp.int32, (K, LANES), 0)

    def param_slice(t, carry):
        got = jnp.dot(
            w2k[...], cols[pl.ds(pl.multiple_of(t * 288, 16), 864), :], preferred_element_type=f32
        )
        par = got[0:48, 0:512] + got[48:96, 128:640] + got[96:144, 256:768] + b2_col
        grow = jnp.exp(-jnp.abs(par))
        soft = jnp.maximum(par, 0.0) + jnp.log1p(grow)
        sigs[t] = jnp.where(par >= 0.0, 1.0, grow) / (1.0 + grow)
        for z in range(LZ):
            for c in range(2):
                plane = t * LZ + z
                chosen = bins[pl.ds(c * PLANES + plane, 1), :]
                pick = level == chosen
                below = level < chosen
                after = level == ((chosen + 1) & 7)
                cut = soft[c * 24 : c * 24 + 24, z * LANES : (z + 1) * LANES]
                sw, sh, sd = cut[0:8], cut[8:16], cut[16:24]
                sums = (
                    sw, jnp.where(pick, sw, 0.0),
                    sh, jnp.where(pick, sh, 0.0), jnp.where(below, sh, 0.0),
                    jnp.where(pick, sd, 0.0), jnp.where(after, sd, 0.0),
                )
                for q, value in enumerate(sums):
                    red[q, pl.ds(c * 16 + plane, 1), :] = jnp.sum(value, axis=0, keepdims=True)
        return carry

    lax.fori_loop(0, LT, param_slice, 0)

    live = site[0, 0:12, :]
    g_log = live * site[1, 0:12, :]
    for c in range(2):
        x = lk[c * 12 : c * 12 + 12, :]
        tl = lk[48 + c * 12 : 60 + c * 12, :]
        xab[0:8, :] = lk[c * 12 + 4 : c * 12 + 12, :]
        xab[8:12, :] = lbuf[5, pl.ds(8 + c, LZ, stride=4), :]
        theta = x + shifted(tl, 0, 1) - xab[0:12, :] - tl
        my_cot = cot[c * 12 : c * 12 + 12, :]
        g_new = -live * my_cot
        rows = slice(c * 16, c * 16 + 12)
        sum_w, pick_w = red[0, rows, :], red[1, rows, :]
        sum_h, pick_h, low_h = red[2, rows, :], red[3, rows, :], red[4, rows, :]
        d0 = min_deriv + red[5, rows, :]
        d1 = min_deriv + red[6, rows, :]
        inv_w, inv_h = 1.0 / sum_w, 1.0 / sum_h
        frac_w, frac_h, frac_low = pick_w * inv_w, pick_h * inv_h, low_h * inv_h
        width = min_share + keep_share * frac_w
        height = min_share + keep_share * frac_h
        r = height / width
        u = 1.0 / (1.0 + jnp.exp(-theta))
        v = 1.0 - u
        q = u * v
        den = r + (d0 + d1 - 2.0 * r) * q
        top = r * u * u + d0 * q
        numer = d1 * u * u + 2.0 * r * q + d0 * v * v
        inv_den = 1.0 / den
        g_top = g_new * two_pi * height * inv_den
        g_den = -(g_top * top + 2.0 * g_log) * inv_den
        g_num = g_log / numer
        g_h = g_new * two_pi * top * inv_den + g_log / height
        g_r = g_top * u * u + g_den * (1.0 - 2.0 * q) + 2.0 * g_num * q + g_log / r
        g_d0 = (g_top + g_den) * q + g_num * v * v
        g_d1 = g_den * q + g_num * u * u
        g_q = g_top * d0 + g_den * (d0 + d1 - 2.0 * r) + 2.0 * g_num * r
        g_u = 2.0 * g_top * r * u + 2.0 * g_num * (d1 * u - d0 * v) + g_q * (1.0 - 2.0 * u)
        g_theta = g_u * q + g_log * (1.0 - 2.0 * u)
        all_h = g_h + g_r / width
        all_w = -g_r * r / width
        base = two_pi * g_new
        a_w = keep_share * all_w * inv_w
        coef[0, rows, :] = a_w
        coef[1, rows, :] = a_w * frac_w
        coef[2, rows, :] = keep_share * all_h * inv_h
        coef[3, rows, :] = keep_share * base * inv_h
        coef[4, rows, :] = keep_share * (all_h * frac_h + base * frac_low) * inv_h
        coef[5, rows, :] = g_d0
        coef[6, rows, :] = g_d1
        grad = g_theta + live * my_cot
        pgv[c, 4:16, :] = grad
        pgs[c * 4 : c * 4 + 4, :] = grad[8:12, :]

    phase_copy = pltpu.make_async_remote_copy(
        src_ref=pgs, dst_ref=pgr, send_sem=send_g, recv_sem=recv_g,
        device_id=neighbour(1, 0), device_id_type=MESH_ID,
    )
    phase_copy.start()

    def param_grad_slice(t, total):
        for z in range(LZ):
            plane = t * LZ + z
            parts = []
            for c in range(2):
                chosen = bins[pl.ds(c * PLANES + plane, 1), :]
                pick = level == chosen
                below = level < chosen
                after = level == ((chosen + 1) & 7)
                a = [coef[k, pl.ds(c * 16 + plane, 1), :] for k in range(7)]
                sig = sigs[t, c * 24 : c * 24 + 24, z * LANES : (z + 1) * LANES]
                parts.append((jnp.where(pick, a[0], 0.0) - a[1]) * sig[0:8])
                parts.append((jnp.where(pick, a[2], jnp.where(below, a[3], 0.0)) - a[4]) * sig[8:16])
                parts.append((jnp.where(pick, a[5], jnp.where(after, a[6], 0.0))) * sig[16:24])
            grad = jnp.concatenate(parts, axis=0)
            pbuf[t + 1, z + 1] = grad.astype(bf16)
            total = total + grad
        return total

    bias2 = jnp.sum(
        lax.fori_loop(0, LT, param_grad_slice, jnp.zeros((OUTC, LANES), f32)), axis=1, keepdims=True
    )

    h_from = {-1: slice(1, 2), 0: slice(1, 4), 1: slice(3, 4)}
    h_into = {-1: slice(4, 5), 0: slice(1, 4), 1: slice(0, 1)}
    v_from = {-1: slice(1, 2), 0: slice(1, 5), 1: slice(4, 5)}
    v_into = {-1: slice(5, 6), 0: slice(1, 5), 1: slice(0, 1)}

    def send_halo(buf, send, recv):
        copies = []
        for i, (dt, dz) in enumerate(DIRS):
            copy = pltpu.make_async_remote_copy(
                src_ref=buf.at[h_from[dt], v_from[dz]],
                dst_ref=buf.at[h_into[dt], v_into[dz]],
                send_sem=send.at[i], recv_sem=recv.at[i],
                device_id=neighbour(dt, dz), device_id_type=MESH_ID,
            )
            copy.start()
            copies.append(copy)
        return copies

    param_copies = send_halo(pbuf, send_p, recv_p)

    def spread(buf, t, rows):
        own = jnp.concatenate([buf[t + 1, z + 1] for z in range(LZ)], axis=1)
        one = jnp.zeros((rows, LANES), bf16)
        two = jnp.zeros((rows, 2 * LANES), bf16)
        return jnp.concatenate(
            [
                jnp.concatenate([own, two], axis=1),
                jnp.concatenate([one, own, one], axis=1),
                jnp.concatenate([two, own], axis=1),
            ],
            axis=0,
        )

    spread_p = [spread(pbuf, t, OUTC) for t in range(LT)]
    for i in range(3):
        total = None
        for t in range(LT):
            part = lax.dot_general(
                spread_p[t], cols[(t + i) * 288 : (t + i + 1) * 288, :], nt_dims, preferred_element_type=f32
            )
            total = part if total is None else total + part
        gm2[i * 144 : (i + 1) * 144, :] = total[:, 0:128].astype(bf16)
        gm2[432 + i * 144 : 576 + i * 144, :] = total[:, 128:256].astype(bf16)
        tails[i * 144 : (i + 1) * 144, :] = jnp.concatenate(
            [total[:, 256:288], jnp.zeros((144, 96), f32)], axis=1
        )
    tails[432:448, :] = jnp.zeros((16, LANES), f32)
    tail = tails[0:112, :]
    for g in range(1, 4):
        tail = tail + pltpu.roll(tails[g * 112 : (g + 1) * 112, :], 32 * g, 1)
    gm2[864:976, :] = tail.astype(bf16)
    gm2[976:1024, :] = jnp.zeros((48, LANES), bf16)

    rows2 = 1024 // nt
    rows_part = rows2 // nz
    copies_a = to_others(
        "ta", lambda peer: gm2.at[pl.ds(pl.multiple_of(peer * rows2, 16), rows2)],
        lambda k: got_a.at[k], send_a, recv_a,
    )

    for copy in param_copies:
        copy.wait()

    def stacked(buf, t):
        rows = []
        for i in range(3):
            for j in range(3):
                rows.append(jnp.concatenate([buf[t + 2 - i, z + 2 - j] for z in range(LZ)], axis=1))
        return jnp.concatenate(rows, axis=0)

    def hidden_grad_slice(t, total):
        got = jnp.dot(wt2[...], stacked(pbuf, t), preferred_element_type=f32)
        for z in range(LZ):
            lanes = slice(z * LANES, (z + 1) * LANES)
            grad = shift_sum([got[b * HID : (b + 1) * HID, lanes] for b in range(9)])
            pre = pres[t + 1, :, lanes]
            sig = 1.0 / (1.0 + jnp.exp(-pre))
            grad = grad * (sig * (1.0 + pre * (1.0 - sig)))
            qbuf[t + 1, z + 1] = grad.astype(bf16)
            total = total + grad
        return total

    bias1 = jnp.sum(
        lax.fori_loop(0, LT, hidden_grad_slice, jnp.zeros((HID, LANES), f32)), axis=1, keepdims=True
    )

    preact_copies = send_halo(qbuf, send_q, recv_q)

    total = gm2[pl.ds(pl.multiple_of(mt * rows2, 16), rows2), :].astype(f32)
    for k, copy in enumerate(copies_a):
        copy.wait()
        total = total + got_a[k + 1].astype(f32)
    total = total * scale
    for p in range(nz):
        mid_b[p] = total[p * rows_part : (p + 1) * rows_part, :]
    copies_b = to_others("gz", lambda peer: mid_b.at[peer], lambda k: got_b.at[k], send_b, recv_b)

    tight80 = one_hot(80, 0)
    spread_q = [spread(qbuf, t, HID) for t in range(LT)]
    g1 = []
    for i in range(3):
        total = None
        for t in range(LT):
            row = (t + 1 + i) * 80
            part = lax.dot_general(
                spread_q[t], fcols[row : row + 80, 128:896], nt_dims, preferred_element_type=f32
            )
            total = part if total is None else total + part
        g1.append(jnp.dot(total.astype(bf16), tight80, preferred_element_type=f32))
    g1 = jnp.concatenate(g1, axis=0)
    g1 = jnp.concatenate([g1, jnp.zeros((288, 74), f32)], axis=1)
    gm1[0:144, :] = (g1[0:144] + pltpu.roll(g1[144:288], 64, 1)).astype(bf16)
    bias = jnp.concatenate([bias2, bias1, jnp.zeros((32, 1), f32)], axis=0)
    lane = lax.broadcasted_iota(jnp.int32, (112, LANES), 1)
    gm1[144:256, :] = jnp.where(lane == 0, bias, 0.0).astype(bf16)
    rows1 = 256 // nt
    copies_e = to_others(
        "ta", lambda peer: gm1.at[pl.ds(pl.multiple_of(peer * rows1, 16), rows1)],
        lambda k: got_e.at[k], send_e, recv_e,
    )

    x_two = [lk[0:12, :], lk[12:24, :]]
    y_two = [lk[24:36, :], lk[36:48, :]]
    pairs = [[sin_cos(psi) for psi in three] for three in loop_phases(x_two, y_two)]

    total = mid_b[mz]
    for k, copy in enumerate(copies_b):
        copy.wait()
        total = total + got_b[k + 1]
    part_c[...] = total
    copies_c = to_others("gz", lambda peer: part_c, lambda k: all_c.at[mz], send_c, recv_c)
    all_c[mz] = total

    phase_copy.wait()
    for copy in preact_copies:
        copy.wait()

    def feature_grad_slice(t, carry):
        got = jnp.dot(wt1[...], stacked(qbuf, t), preferred_element_type=f32)
        for z in range(LZ):
            lanes = slice(z * LANES, (z + 1) * LANES)
            grad = shift_sum([got[b * 8 : (b + 1) * 8, lanes] for b in range(9)])
            fgs[pl.ds(pl.multiple_of((t * LZ + z) * 8, 8), 8), :] = grad
        return carry

    lax.fori_loop(0, LT, feature_grad_slice, 0)

    third = 1.0 / 3.0
    loop_grads = []
    for which in range(3):
        g_cos = fgs[pl.ds(2 * which, PLANES, stride=8), :] * third
        g_sin = fgs[pl.ds(2 * which + 1, PLANES, stride=8), :] * third
        three = [g_sin * cos_v - g_cos * sin_v for sin_v, cos_v in pairs[which]]
        loop_grads.append((three[0] - three[2], three[1] - three[2]))
    for c in range(2):
        dp, dw, dr = loop_grads[0][c], loop_grads[1][c], loop_grads[2][c]
        side = dp + dr
        x_ctx = (
            dp + dw + dr
            - shifted(dp + dw, -1, 0)
            + shifted(dw, 0, -1)
            - shifted(dw, -1, -1)
            - shifted(dr, -2, 0)
        )
        y_ctx = (
            shifted(side, 0, -1)
            - side
            - dw
            + shifted(dw, 0, -2)
            + shifted(dr, -1, -1)
            - shifted(dr, -1, 0)
        )
        pgv[c, 0:4, :] = pgr[c * 4 : c * 4 + 4, :]
        grad = pgv[c, 4:16, :]
        prev = pgv[c, 0:12, :]
        out_link[c * 12 : c * 12 + 12, :] = grad - prev + x_ctx
        out_link[24 + c * 12 : 36 + c * 12, :] = y_ctx
        out_link[48 + c * 12 : 60 + c * 12, :] = cot[c * 12 : c * 12 + 12, :] - grad + shifted(grad, 0, -1)

    total = gm1[pl.ds(pl.multiple_of(mt * rows1, 16), rows1), :].astype(f32)
    for k, copy in enumerate(copies_e):
        copy.wait()
        total = total + got_e[k + 1].astype(f32)
    mid_f[...] = (total * scale).astype(bf16)
    copies_f = to_others("gz", lambda peer: mid_f, lambda k: got_f.at[mz], send_f, recv_f)
    got_f[mz] = mid_f[...]

    for copy in copies_c:
        copy.wait()
    fin_d[...] = jnp.concatenate([all_c[p] for p in range(nz)], axis=0).astype(bf16)
    mine2 = pl.ds(pl.multiple_of(mt * rows2, 16), rows2)
    copies_d = to_others("ta", lambda peer: fin_d, lambda k: out2.at[mine2], send_d, recv_d)
    out2[mine2, :] = fin_d[...]

    for copy in copies_f:
        copy.wait()
    total = got_f[0].astype(f32)
    for k in range(1, nz):
        total = total + got_f[k].astype(f32)
    fin_g[...] = total.astype(bf16)
    mine1 = pl.ds(pl.multiple_of(mt * rows1, 16), rows1)
    copies_h = to_others("ta", lambda peer: fin_g, lambda k: out1.at[mine1], send_h, recv_h)
    out1[mine1, :] = fin_g[...]
    for copy in copies_d:
        copy.wait()
    for copy in copies_h:
        copy.wait()


def write_kernel(link, sum2, sum1, out_link, out_first, out_bias1, out_second, out_bias2):
    for d in range(3):
        for c in range(2):
            for t in range(LT):
                out_link[d, c, t] = link[pl.ds(d * 24 + c * 12 + t * 4, LZ), :]
    out_second[:, 0:128] = sum2[0:432, :].astype(f32)
    out_second[:, 128:256] = sum2[432:864, :].astype(f32)
    tail = sum2[864:976, :].astype(f32)
    for g in range(4):
        count = min(112, 432 - g * 112)
        out_second[g * 112 : g * 112 + count, 256:288] = rolled(tail, -32 * g)[0:count, 0:32]
    half = sum1[0:144, :].astype(f32)
    out_first[0:144, :] = half[:, 0:54]
    out_first[144:288, :] = pltpu.roll(half, 64, 1)[:, 0:54]
    for out, begin, count in ((out_bias2, 144, OUTC), (out_bias1, 192, HID)):
        col = sum1[begin : begin + count, :].astype(f32)[:, 0:1]
        eye = lax.broadcasted_iota(jnp.int32, (count, count), 0) == lax.broadcasted_iota(
            jnp.int32, (count, count), 1
        )
        out[...] = jnp.sum(jnp.where(eye, col, 0.0), axis=0, keepdims=True)


def vmem():
    return pl.BlockSpec(memory_space=pltpu.VMEM)


def local(
    link_phases, active, bin_index, first_weight, first_bias,
    second_weight, second_bias, cotangent, logdet_cotangent,
):
    nt, nz = lax.axis_size("ta"), lax.axis_size("gz")
    dma = pltpu.SemaphoreType.DMA
    mem = pltpu.VMEM
    rows2, rows1 = 1024 // nt, 256 // nt
    part = rows2 // nz
    scale = 1.0 / math.sqrt(nt * nz * PLANES * LANES)
    link, sum2, sum1 = pl.pallas_call(
        functools.partial(main_kernel, scale),
        out_shape=(
            jax.ShapeDtypeStruct((72, LANES), f32),
            jax.ShapeDtypeStruct((1024, LANES), bf16),
            jax.ShapeDtypeStruct((256, LANES), bf16),
        ),
        in_specs=[vmem()] * 9,
        out_specs=(vmem(), vmem(), vmem()),
        scratch_shapes=[
            mem((72, LANES), f32),
            mem((24, LANES), jnp.int32),
            mem((24, LANES), f32),
            mem((2, 16, LANES), f32),
            mem((96, 240), bf16),
            mem((144, 864), bf16),
            mem((288, 432), bf16),
            mem((72, 288), bf16),
            mem((7, 32, LANES), f32),
            mem((64, LANES), f32),
            mem((560, 1024), bf16),
            mem((5, HID, 512), f32),
            mem((1440, 768), bf16),
            mem((LT, OUTC, 512), f32),
            mem((7, 32, LANES), f32),
            mem((7, 32, LANES), f32),
            mem((16, LANES), f32),
            mem((8, LANES), f32),
            mem((8, LANES), f32),
            mem((2, 16, LANES), f32),
            mem((5, 6, OUTC, LANES), bf16),
            mem((5, 6, HID, LANES), bf16),
            mem((96, LANES), f32),
            mem((448, LANES), f32),
            mem((1024, LANES), bf16),
            mem((nt, rows2, LANES), bf16),
            mem((nz, part, LANES), f32),
            mem((nz, part, LANES), f32),
            mem((part, LANES), f32),
            mem((nz, part, LANES), f32),
            mem((rows2, LANES), bf16),
            mem((256, LANES), bf16),
            mem((nt, rows1, LANES), bf16),
            mem((rows1, LANES), bf16),
            mem((nz, rows1, LANES), bf16),
            mem((rows1, LANES), bf16),
            dma((8,)), dma((8,)), dma((8,)), dma((8,)), dma((8,)), dma((8,)), dma, dma,
            dma((nt,)), dma((nt,)), dma((nz,)), dma((nz,)), dma((nz,)), dma((nz,)), dma((nt,)), dma((nt,)),
            dma((nt,)), dma((nt,)), dma((nz,)), dma((nz,)), dma((nt,)), dma((nt,)),
        ],
        compiler_params=pltpu.CompilerParams(
            collective_id=0, has_side_effects=True, vmem_limit_bytes=40 * 1024 * 1024
        ),
        name="main_kernel",
    )(
        link_phases, active, bin_index,
        first_weight.reshape(288, 54), first_bias.reshape(1, HID),
        second_weight.reshape(432, 288), second_bias.reshape(1, OUTC),
        cotangent, logdet_cotangent,
    )
    link_grad, first, bias1, second, bias2 = pl.pallas_call(
        write_kernel,
        out_shape=(
            jax.ShapeDtypeStruct((3, 2, LT, LZ, LANES), f32),
            jax.ShapeDtypeStruct((288, 54), f32),
            jax.ShapeDtypeStruct((1, HID), f32),
            jax.ShapeDtypeStruct((432, 288), f32),
            jax.ShapeDtypeStruct((1, OUTC), f32),
        ),
        in_specs=[vmem()] * 3,
        out_specs=(vmem(),) * 5,
        name="write_kernel",
    )(link, sum2, sum1)
    return (
        link_grad,
        first.reshape(9, HID, 54),
        bias1.reshape(HID),
        second.reshape(9, OUTC, 288),
        bias2.reshape(OUTC),
    )


def solution(mesh):
    return jax.shard_map(
        local,
        mesh=mesh,
        in_specs=(
            P(None, None, "ta", "gz", None),
            P("ta", "gz", None),
            P(None, "ta", "gz", None),
            P(), P(), P(), P(),
            P(None, "ta", "gz", None),
            P("ta", "gz", None),
        ),
        out_specs=(P(None, None, "ta", "gz", None), P(), P(), P(), P()),
        check_vma=False,
    )
```

```python
import functools
import math

import jax
import jax.numpy as jnp
from jax import lax
from jax.experimental import pallas as pl
from jax.experimental.pallas import tpu as pltpu
from jax.sharding import PartitionSpec as P

K = 8
LT = 3
LZ = 4
LANES = 128
HID = 32
OUTC = 48
PLANES = LT * LZ
MESH_ID = pl.DeviceIdType.MESH

min_share = 0.001
min_deriv = 0.001
keep_share = 1.0 - K * min_share
two_pi = 2.0 * math.pi

f32 = jnp.float32
bf16 = jnp.bfloat16


def lane_x(rows):
    return lax.broadcasted_iota(jnp.int32, (rows, LANES), 1) % 8


def rolled(value, amount):
    amount = amount % LANES
    if amount == 0:
        return value
    return pltpu.roll(value, amount, 1)


def shifted(value, step_y, step_x):
    near = rolled(value, -(8 * step_y + step_x))
    if step_x == 0:
        return near
    xs = lane_x(value.shape[0])
    if step_x > 0:
        wrap = rolled(value, -(8 * step_y + step_x - 8))
        return jnp.where(xs < 8 - step_x, near, wrap)
    wrap = rolled(value, -(8 * step_y + step_x + 8))
    return jnp.where(xs >= -step_x, near, wrap)


def nine_shifts(value):
    return [shifted(value, sy, sx) for sy in (-1, 0, 1) for sx in (-1, 0, 1)]


def shift_sum(blocks):
    total = None
    for ix, dx in enumerate((-1, 0, 1)):
        part = None
        for iy, dy in enumerate((-1, 0, 1)):
            piece = rolled(blocks[3 * iy + ix], 8 * dy)
            part = piece if part is None else part + piece
        part = shifted(part, 0, -dx)
        total = part if total is None else total + part
    return total


def sin_cos(angle):
    turns = jnp.floor(angle * (2.0 / math.pi) + 0.5)
    rest = angle - turns * 1.5703125
    rest = rest - turns * 4.837512969970703125e-4
    rest = rest - turns * 7.54978995489188e-8
    sq = rest * rest
    s = rest + rest * sq * (-1.6666654611e-1 + sq * (8.3321608736e-3 - sq * 1.9515295891e-4))
    c = 1.0 - 0.5 * sq + sq * sq * (
        4.166664568298827e-2 + sq * (-1.388731625493765e-3 + sq * 2.443315711809948e-5)
    )
    quad = turns.astype(jnp.int32)
    swap = (quad & 1) == 1
    sin_v = jnp.where(swap, c, s)
    cos_v = jnp.where(swap, s, c)
    sin_v = jnp.where((quad & 2) == 2, -sin_v, sin_v)
    cos_v = jnp.where(((quad + 1) & 2) == 2, -cos_v, cos_v)
    return sin_v, cos_v


def loop_phases(x_two, y_two):
    plaq, wide, tall = [], [], []
    for x, y in zip(x_two, y_two):
        y_x = shifted(y, 0, 1)
        x_y = shifted(x, 1, 0)
        plaq.append(x + y_x - x_y - y)
        wide.append(x + shifted(x, 0, 1) + shifted(y, 0, 2) - shifted(x, 1, 1) - x_y - y)
        tall.append(x + y_x + shifted(y, 1, 1) - shifted(x, 2, 0) - shifted(y, 1, 0) - y)
    out = []
    for two in (plaq, wide, tall):
        out.append((two[0], two[1], -(two[0] + two[1])))
    return out


DIRS = [(dt, dz) for dt in (-1, 0, 1) for dz in (-1, 0, 1) if (dt, dz) != (0, 0)]


def neighbour(dt, dz):
    nt, nz = lax.axis_size("ta"), lax.axis_size("gz")
    mt, mz = lax.axis_index("ta"), lax.axis_index("gz")
    return (lax.rem(mt + dt + nt, nt), lax.rem(mz + dz + nz, nz))


def main_kernel(
    scale, *refs
):
    given, refs = refs[:9], refs[9:]
    (out_link, out2, out1), refs = refs[:3], refs[3:]
    held, refs = refs[:9], refs[9:]
    links, act, bins_in, first_w, b1, second_w, b2, cot_in, ldc_in = held
    (
        lk, bins, cot, site, w1p, w2k, wt2, wt1,
        lbuf, fs, fcols, pres, cols, sigs, red, coef, xab, pgs, pgr, pgv,
        pbuf, qbuf, fgs, tails, gm2, got_a, mid_b, got_b, fin_d,
        gm1, got_e, mid_f, got_f, fin_g, link_out,
        in_sem, out_sem, send_l, recv_l, send_p, recv_p, send_q, recv_q, send_g, recv_g,
        send_a, recv_a, send_b, recv_b, send_d, recv_d,
        send_e, recv_e, send_f, recv_f, send_h, recv_h,
    ) = refs
    loads = [pltpu.make_async_copy(src, dst, in_sem.at[i]) for i, (src, dst) in enumerate(zip(given, held))]
    for load in loads:
        load.start()

    nt, nz = lax.axis_size("ta"), lax.axis_size("gz")
    mt, mz = lax.axis_index("ta"), lax.axis_index("gz")
    nx, nd = 2 * nt, nz // 2
    side, deep = lax.rem(mz, 2), mz // 2
    mx = 2 * mt + side

    def wide_peer(k):
        return (lax.rem(mt + k // 2, nt), mz + (k % 2) * (1 - 2 * side))

    def deep_peer(k):
        return (mt, lax.rem(mz + 2 * k, nz))

    wide_order = list(range(1, nx))
    deep_order = sorted(range(1, nd), key=lambda k: -min(k, nd - k))
    barrier = pltpu.get_barrier_semaphore()
    cross = lax.rem(mz - 1 + 2 * side + nz, nz)
    greeted = [(lax.rem(mt + dt + nt, nt), cross) for dt in (-1, 0, 1)]
    greeted += [wide_peer(k) for k in wide_order] + [deep_peer(k) for k in deep_order]
    for peer in greeted:
        pl.semaphore_signal(barrier, inc=1, device_id=peer, device_id_type=MESH_ID)

    def to_wide(src, dst, send, recv):
        copies = []
        for k in wide_order:
            peer = wide_peer(k)
            copy = pltpu.make_async_remote_copy(
                src_ref=src(2 * peer[0] + lax.rem(peer[1], 2)), dst_ref=dst(k),
                send_sem=send.at[k], recv_sem=recv.at[k], device_id=peer, device_id_type=MESH_ID,
            )
            copy.start()
            copies.append(copy)
        return copies

    def to_deep(src, dst, send, recv):
        copies = []
        for k in deep_order:
            copy = pltpu.make_async_remote_copy(
                src_ref=src, dst_ref=dst,
                send_sem=send.at[k], recv_sem=recv.at[k], device_id=deep_peer(k), device_id_type=MESH_ID,
            )
            copy.start()
            copies.append(copy)
        return copies

    loads[0].wait()
    for d in range(3):
        for c in range(2):
            for t in range(LT):
                lk[pl.ds(d * 24 + c * 12 + t * 4, LZ), :] = links[d, c, t]
    for comp in range(4):
        for t in range(LT):
            lbuf[2 + t, pl.ds(8 + comp, LZ, stride=4), :] = lk[pl.ds(comp * PLANES + t * LZ, LZ), :]
    pl.semaphore_wait(barrier, len(greeted))

    t_from = {-1: slice(2, 4), 0: slice(2, 5), 1: slice(3, 5)}
    t_into = {-1: slice(5, 7), 0: slice(2, 5), 1: slice(0, 2)}
    z_from = {-1: slice(8, 16), 0: slice(8, 24), 1: slice(16, 24)}
    z_into = {-1: slice(24, 32), 0: slice(8, 24), 1: slice(0, 8)}
    link_copies = []
    for i, (dt, dz) in enumerate(DIRS):
        copy = pltpu.make_async_remote_copy(
            src_ref=lbuf.at[t_from[dt], z_from[dz]],
            dst_ref=lbuf.at[t_into[dt], z_into[dz]],
            send_sem=send_l.at[i], recv_sem=recv_l.at[i],
            device_id=neighbour(dt, dz), device_id_type=MESH_ID,
        )
        copy.start()
        link_copies.append(copy)
    fs[...] = jnp.zeros_like(fs)

    for load in loads[1:]:
        load.wait()
    for t in range(LT):
        site[0, pl.ds(t * LZ, LZ), :] = act[t].astype(f32)
        site[1, pl.ds(t * LZ, LZ), :] = ldc_in[t]
        for c in range(2):
            bins[pl.ds(c * 12 + t * LZ, LZ), :] = bins_in[c, t]
            cot[pl.ds(c * 12 + t * LZ, LZ), :] = cot_in[c, t]
    nt_dims = (((1,), (1,)), ((), ()))

    def one_hot(rows, padded_dim):
        shape = (rows, 54) if padded_dim == 0 else (54, rows)
        wide = lax.broadcasted_iota(jnp.int32, shape, padded_dim)
        tight = lax.broadcasted_iota(jnp.int32, shape, 1 - padded_dim)
        hit = (wide < 72) & (wide % 8 < 6) & (tight == (wide // 8) * 6 + wide % 8)
        return jnp.where(hit, 1.0, 0.0).astype(bf16)

    spread80 = one_hot(80, 1)
    w1p[...] = jnp.concatenate(
        [
            jnp.dot(first_w[i * 96 : (i + 1) * 96, :], spread80, preferred_element_type=f32)
            for i in range(3)
        ],
        axis=1,
    ).astype(bf16)
    w2k[...] = jnp.concatenate(
        [second_w[i * 144 : (i + 1) * 144, :].astype(f32) for i in range(3)], axis=1
    ).astype(bf16)
    diag = lax.broadcasted_iota(jnp.int32, (288, 288), 0) == lax.broadcasted_iota(jnp.int32, (288, 288), 1)
    wt2[...] = lax.dot_general(
        jnp.where(diag, 1.0, 0.0).astype(bf16), second_w[...], nt_dims, preferred_element_type=f32
    ).astype(bf16)

    def as_column(row_ref, count):
        eye = lax.broadcasted_iota(jnp.int32, (count, count), 0) == lax.broadcasted_iota(
            jnp.int32, (count, count), 1
        )
        return jnp.sum(jnp.where(eye, row_ref[...], 0.0), axis=1, keepdims=True)

    b1_col, b2_col = as_column(b1, HID), as_column(b2, OUTC)
    for copy in link_copies:
        copy.wait()

    def feature_slice(t, carry):
        x_two = [lbuf[t, pl.ds(comp, 8, stride=4), :] for comp in (0, 1)]
        y_two = [lbuf[t, pl.ds(comp, 8, stride=4), :] for comp in (2, 3)]
        for which, three in enumerate(loop_phases(x_two, y_two)):
            pairs = [sin_cos(psi) for psi in three]
            fs[pl.ds(2 * which, 8, stride=8), :] = (pairs[0][1] + pairs[1][1] + pairs[2][1]) * (1.0 / 3.0)
            fs[pl.ds(2 * which + 1, 8, stride=8), :] = (pairs[0][0] + pairs[1][0] + pairs[2][0]) * (1.0 / 3.0)
        row = pl.multiple_of(t * 80, 16)
        for z in range(8):
            blocks = nine_shifts(fs[z * 8 : z * 8 + 8, :])
            blocks.append(jnp.zeros((8, LANES), f32))
            fcols[pl.ds(row, 80), z * LANES : (z + 1) * LANES] = jnp.concatenate(blocks, axis=0).astype(bf16)
        return carry

    lax.fori_loop(0, 7, feature_slice, 0, unroll=True)

    def hidden_slice(t, carry):
        got = jnp.dot(
            w1p[...], fcols[pl.ds(pl.multiple_of(t * 80, 16), 240), :], preferred_element_type=f32
        )
        pre = got[0:32, 0:768] + got[32:64, 128:896] + got[64:96, 256:1024] + b1_col
        pres[t] = pre[:, 128:640]
        hid = pre / (1.0 + jnp.exp(-pre))
        row = pl.multiple_of(t * 288, 16)
        for z in range(6):
            blocks = nine_shifts(hid[:, z * LANES : (z + 1) * LANES])
            cols[pl.ds(row, 288), z * LANES : (z + 1) * LANES] = jnp.concatenate(blocks, axis=0).astype(bf16)
        return carry

    lax.fori_loop(0, 5, hidden_slice, 0, unroll=True)

    level = lax.broadcasted_iota(jnp.int32, (K, LANES), 0)

    def param_slice(t, carry):
        got = jnp.dot(
            w2k[...], cols[pl.ds(pl.multiple_of(t * 288, 16), 864), :], preferred_element_type=f32
        )
        par = got[0:48, 0:512] + got[48:96, 128:640] + got[96:144, 256:768] + b2_col
        grow = jnp.exp(-jnp.abs(par))
        soft = jnp.maximum(par, 0.0) + jnp.log1p(grow)
        sigs[t] = jnp.where(par >= 0.0, 1.0, grow) / (1.0 + grow)
        for z in range(LZ):
            for c in range(2):
                plane = t * LZ + z
                chosen = bins[pl.ds(c * PLANES + plane, 1), :]
                pick = level == chosen
                below = level < chosen
                after = level == ((chosen + 1) & 7)
                cut = soft[c * 24 : c * 24 + 24, z * LANES : (z + 1) * LANES]
                sw, sh, sd = cut[0:8], cut[8:16], cut[16:24]
                sums = (
                    sw, jnp.where(pick, sw, 0.0),
                    sh, jnp.where(pick, sh, 0.0), jnp.where(below, sh, 0.0),
                    jnp.where(pick, sd, 0.0), jnp.where(after, sd, 0.0),
                )
                for q, value in enumerate(sums):
                    red[q, pl.ds(c * 16 + plane, 1), :] = jnp.sum(value, axis=0, keepdims=True)
        return carry

    lax.fori_loop(0, LT, param_slice, 0, unroll=True)

    live = site[0, 0:12, :]
    g_log = live * site[1, 0:12, :]
    for c in range(2):
        x = lk[c * 12 : c * 12 + 12, :]
        tl = lk[48 + c * 12 : 60 + c * 12, :]
        xab[0:8, :] = lk[c * 12 + 4 : c * 12 + 12, :]
        xab[8:12, :] = lbuf[5, pl.ds(8 + c, LZ, stride=4), :]
        theta = x + shifted(tl, 0, 1) - xab[0:12, :] - tl
        my_cot = cot[c * 12 : c * 12 + 12, :]
        g_new = -live * my_cot
        rows = slice(c * 16, c * 16 + 12)
        sum_w, pick_w = red[0, rows, :], red[1, rows, :]
        sum_h, pick_h, low_h = red[2, rows, :], red[3, rows, :], red[4, rows, :]
        d0 = min_deriv + red[5, rows, :]
        d1 = min_deriv + red[6, rows, :]
        inv_w, inv_h = 1.0 / sum_w, 1.0 / sum_h
        frac_w, frac_h, frac_low = pick_w * inv_w, pick_h * inv_h, low_h * inv_h
        width = min_share + keep_share * frac_w
        height = min_share + keep_share * frac_h
        r = height / width
        u = 1.0 / (1.0 + jnp.exp(-theta))
        v = 1.0 - u
        q = u * v
        den = r + (d0 + d1 - 2.0 * r) * q
        top = r * u * u + d0 * q
        numer = d1 * u * u + 2.0 * r * q + d0 * v * v
        inv_den = 1.0 / den
        g_top = g_new * two_pi * height * inv_den
        g_den = -(g_top * top + 2.0 * g_log) * inv_den
        g_num = g_log / numer
        g_h = g_new * two_pi * top * inv_den + g_log / height
        g_r = g_top * u * u + g_den * (1.0 - 2.0 * q) + 2.0 * g_num * q + g_log / r
        g_d0 = (g_top + g_den) * q + g_num * v * v
        g_d1 = g_den * q + g_num * u * u
        g_q = g_top * d0 + g_den * (d0 + d1 - 2.0 * r) + 2.0 * g_num * r
        g_u = 2.0 * g_top * r * u + 2.0 * g_num * (d1 * u - d0 * v) + g_q * (1.0 - 2.0 * u)
        g_theta = g_u * q + g_log * (1.0 - 2.0 * u)
        all_h = g_h + g_r / width
        all_w = -g_r * r / width
        base = two_pi * g_new
        a_w = keep_share * all_w * inv_w
        coef[0, rows, :] = a_w
        coef[1, rows, :] = a_w * frac_w
        coef[2, rows, :] = keep_share * all_h * inv_h
        coef[3, rows, :] = keep_share * base * inv_h
        coef[4, rows, :] = keep_share * (all_h * frac_h + base * frac_low) * inv_h
        coef[5, rows, :] = g_d0
        coef[6, rows, :] = g_d1
        grad = g_theta + live * my_cot
        pgv[c, 4:16, :] = grad
        pgs[c * 4 : c * 4 + 4, :] = grad[8:12, :]

    phase_copy = pltpu.make_async_remote_copy(
        src_ref=pgs, dst_ref=pgr, send_sem=send_g, recv_sem=recv_g,
        device_id=neighbour(1, 0), device_id_type=MESH_ID,
    )
    phase_copy.start()

    def param_grad_slice(t, total):
        for z in range(LZ):
            plane = t * LZ + z
            parts = []
            for c in range(2):
                chosen = bins[pl.ds(c * PLANES + plane, 1), :]
                pick = level == chosen
                below = level < chosen
                after = level == ((chosen + 1) & 7)
                a = [coef[k, pl.ds(c * 16 + plane, 1), :] for k in range(7)]
                sig = sigs[t, c * 24 : c * 24 + 24, z * LANES : (z + 1) * LANES]
                parts.append((jnp.where(pick, a[0], 0.0) - a[1]) * sig[0:8])
                parts.append((jnp.where(pick, a[2], jnp.where(below, a[3], 0.0)) - a[4]) * sig[8:16])
                parts.append((jnp.where(pick, a[5], jnp.where(after, a[6], 0.0))) * sig[16:24])
            grad = jnp.concatenate(parts, axis=0)
            pbuf[t + 1, z + 1] = grad.astype(bf16)
            total = total + grad
        return total

    bias2 = jnp.sum(
        lax.fori_loop(0, LT, param_grad_slice, jnp.zeros((OUTC, LANES), f32), unroll=True), axis=1, keepdims=True
    )

    h_from = {-1: slice(1, 2), 0: slice(1, 4), 1: slice(3, 4)}
    h_into = {-1: slice(4, 5), 0: slice(1, 4), 1: slice(0, 1)}
    v_from = {-1: slice(1, 2), 0: slice(1, 5), 1: slice(4, 5)}
    v_into = {-1: slice(5, 6), 0: slice(1, 5), 1: slice(0, 1)}

    def send_halo(buf, send, recv):
        copies = []
        for i, (dt, dz) in enumerate(DIRS):
            copy = pltpu.make_async_remote_copy(
                src_ref=buf.at[h_from[dt], v_from[dz]],
                dst_ref=buf.at[h_into[dt], v_into[dz]],
                send_sem=send.at[i], recv_sem=recv.at[i],
                device_id=neighbour(dt, dz), device_id_type=MESH_ID,
            )
            copy.start()
            copies.append(copy)
        return copies

    param_copies = send_halo(pbuf, send_p, recv_p)

    def spread(buf, t, rows):
        own = jnp.concatenate([buf[t + 1, z + 1] for z in range(LZ)], axis=1)
        one = jnp.zeros((rows, LANES), bf16)
        two = jnp.zeros((rows, 2 * LANES), bf16)
        return jnp.concatenate(
            [
                jnp.concatenate([own, two], axis=1),
                jnp.concatenate([one, own, one], axis=1),
                jnp.concatenate([two, own], axis=1),
            ],
            axis=0,
        )

    spread_p = [spread(pbuf, t, OUTC) for t in range(LT)]
    for i in range(3):
        total = None
        for t in range(LT):
            part = lax.dot_general(
                spread_p[t], cols[(t + i) * 288 : (t + i + 1) * 288, :], nt_dims, preferred_element_type=f32
            )
            total = part if total is None else total + part
        gm2[i * 144 : (i + 1) * 144, :] = total[:, 0:128].astype(bf16)
        gm2[432 + i * 144 : 576 + i * 144, :] = total[:, 128:256].astype(bf16)
        tails[i * 144 : (i + 1) * 144, :] = jnp.concatenate(
            [total[:, 256:288], jnp.zeros((144, 96), f32)], axis=1
        )
    tails[432:448, :] = jnp.zeros((16, LANES), f32)
    tail = tails[0:112, :]
    for g in range(1, 4):
        tail = tail + pltpu.roll(tails[g * 112 : (g + 1) * 112, :], 32 * g, 1)
    gm2[864:976, :] = tail.astype(bf16)
    gm2[976:1024, :] = jnp.zeros((48, LANES), bf16)

    rows2, rows1 = 1024 // nx, 256 // nx

    def wide_rows(index, rows):
        return pl.ds(pl.multiple_of(index * rows, rows), rows)

    copies_a = to_wide(
        lambda index: gm2.at[wide_rows(index, rows2)], lambda k: got_a.at[k], send_a, recv_a
    )

    for copy in param_copies:
        copy.wait()

    def stacked(buf, t):
        rows = []
        for i in range(3):
            for j in range(3):
                rows.append(jnp.concatenate([buf[t + 2 - i, z + 2 - j] for z in range(LZ)], axis=1))
        return jnp.concatenate(rows, axis=0)

    def hidden_grad_slice(t, total):
        got = jnp.dot(wt2[...], stacked(pbuf, t), preferred_element_type=f32)
        for z in range(LZ):
            lanes = slice(z * LANES, (z + 1) * LANES)
            grad = shift_sum([got[b * HID : (b + 1) * HID, lanes] for b in range(9)])
            pre = pres[t + 1, :, lanes]
            sig = 1.0 / (1.0 + jnp.exp(-pre))
            grad = grad * (sig * (1.0 + pre * (1.0 - sig)))
            qbuf[t + 1, z + 1] = grad.astype(bf16)
            total = total + grad
        return total

    bias1 = jnp.sum(
        lax.fori_loop(0, LT, hidden_grad_slice, jnp.zeros((HID, LANES), f32), unroll=True), axis=1, keepdims=True
    )

    preact_copies = send_halo(qbuf, send_q, recv_q)

    tight80 = one_hot(80, 0)
    spread_q = [spread(qbuf, t, HID) for t in range(LT)]
    g1 = []
    for i in range(3):
        total = None
        for t in range(LT):
            row = (t + 1 + i) * 80
            part = lax.dot_general(
                spread_q[t], fcols[row : row + 80, 128:896], nt_dims, preferred_element_type=f32
            )
            total = part if total is None else total + part
        g1.append(jnp.dot(total.astype(bf16), tight80, preferred_element_type=f32))
    g1 = jnp.concatenate(g1, axis=0)
    g1 = jnp.concatenate([g1, jnp.zeros((288, 74), f32)], axis=1)
    gm1[0:144, :] = g1[0:144] + pltpu.roll(g1[144:288], 64, 1)
    bias = jnp.concatenate([bias2, bias1, jnp.zeros((32, 1), f32)], axis=0)
    lane = lax.broadcasted_iota(jnp.int32, (112, LANES), 1)
    gm1[144:256, :] = jnp.where(lane == 0, bias, 0.0)
    copies_e = to_wide(
        lambda index: gm1.at[wide_rows(index, rows1)], lambda k: got_e.at[k], send_e, recv_e
    )

    wt1[...] = lax.dot_general(
        one_hot(72, 0), first_w[...], nt_dims, preferred_element_type=f32
    ).astype(bf16)

    x_two = [lk[0:12, :], lk[12:24, :]]
    y_two = [lk[24:36, :], lk[36:48, :]]
    pairs = [[sin_cos(psi) for psi in three] for three in loop_phases(x_two, y_two)]

    phase_copy.wait()
    for copy in preact_copies:
        copy.wait()

    def feature_grad_slice(t, carry):
        got = jnp.dot(wt1[...], stacked(qbuf, t), preferred_element_type=f32)
        for z in range(LZ):
            lanes = slice(z * LANES, (z + 1) * LANES)
            grad = shift_sum([got[b * 8 : (b + 1) * 8, lanes] for b in range(9)])
            fgs[pl.ds(pl.multiple_of((t * LZ + z) * 8, 8), 8), :] = grad
        return carry

    lax.fori_loop(0, LT, feature_grad_slice, 0, unroll=True)

    def in_order(parts, count):
        total = parts[0].astype(f32)
        for k in range(1, count):
            total = total + parts[k].astype(f32)
        return total

    total = gm2[wide_rows(mx, rows2), :].astype(f32)
    for k, copy in enumerate(copies_a):
        copy.wait()
        total = total + got_a[wide_order[k]].astype(f32)
    mid_b[...] = (total * scale).astype(bf16)
    copies_b = to_deep(mid_b, got_b.at[deep], send_b, recv_b)
    got_b[deep] = mid_b[...]

    total = gm1[wide_rows(mx, rows1), :]
    for k, copy in enumerate(copies_e):
        copy.wait()
        total = total + got_e[wide_order[k]]
    total = total * scale
    mid_f[...] = total
    copies_f = to_deep(mid_f, got_f.at[deep], send_f, recv_f)
    got_f[deep] = total

    third = 1.0 / 3.0
    loop_grads = []
    for which in range(3):
        g_cos = fgs[pl.ds(2 * which, PLANES, stride=8), :] * third
        g_sin = fgs[pl.ds(2 * which + 1, PLANES, stride=8), :] * third
        three = [g_sin * cos_v - g_cos * sin_v for sin_v, cos_v in pairs[which]]
        loop_grads.append((three[0] - three[2], three[1] - three[2]))
    for c in range(2):
        dp, dw, dr = loop_grads[0][c], loop_grads[1][c], loop_grads[2][c]
        pair = dp + dr
        x_ctx = (
            dp + dw + dr
            - shifted(dp + dw, -1, 0)
            + shifted(dw, 0, -1)
            - shifted(dw, -1, -1)
            - shifted(dr, -2, 0)
        )
        y_ctx = (
            shifted(pair, 0, -1)
            - pair
            - dw
            + shifted(dw, 0, -2)
            + shifted(dr, -1, -1)
            - shifted(dr, -1, 0)
        )
        pgv[c, 0:4, :] = pgr[c * 4 : c * 4 + 4, :]
        grad = pgv[c, 4:16, :]
        prev = pgv[c, 0:12, :]
        link_out[c * 12 : c * 12 + 12, :] = grad - prev + x_ctx
        link_out[24 + c * 12 : 36 + c * 12, :] = y_ctx
        link_out[48 + c * 12 : 60 + c * 12, :] = cot[c * 12 : c * 12 + 12, :] - grad + shifted(grad, 0, -1)

    stores = [pltpu.make_async_copy(link_out, out_link, out_sem.at[0])]
    stores[0].start()

    for copy in copies_b:
        copy.wait()
    fin_d[...] = in_order(got_b, nd).astype(bf16)
    copies_d = to_wide(lambda index: fin_d, lambda k: out2.at[wide_rows(mx, rows2)], send_d, recv_d)
    stores.append(pltpu.make_async_copy(fin_d, out2.at[wide_rows(mx, rows2)], out_sem.at[1]))
    stores[1].start()

    for copy in copies_f:
        copy.wait()
    fin_g[...] = in_order(got_f, nd)
    copies_h = to_wide(lambda index: fin_g, lambda k: out1.at[wide_rows(mx, rows1)], send_h, recv_h)
    stores.append(pltpu.make_async_copy(fin_g, out1.at[wide_rows(mx, rows1)], out_sem.at[2]))
    stores[2].start()
    for copy in copies_d + stores + copies_h:
        copy.wait()


def write_kernel(link, sum2, sum1, out_link, out_first, out_bias1, out_second, out_bias2):
    for d in range(3):
        for c in range(2):
            for t in range(LT):
                out_link[d, c, t] = link[pl.ds(d * 24 + c * 12 + t * 4, LZ), :]
    out_second[:, 0:128] = sum2[0:432, :].astype(f32)
    out_second[:, 128:256] = sum2[432:864, :].astype(f32)
    tail = sum2[864:976, :].astype(f32)
    for g in range(4):
        count = min(112, 432 - g * 112)
        out_second[g * 112 : g * 112 + count, 256:288] = rolled(tail, -32 * g)[0:count, 0:32]
    half = sum1[0:144, :]
    out_first[0:144, :] = half[:, 0:54]
    out_first[144:288, :] = pltpu.roll(half, 64, 1)[:, 0:54]
    for out, begin, count in ((out_bias2, 144, OUTC), (out_bias1, 192, HID)):
        col = sum1[begin : begin + count, :][:, 0:1]
        eye = lax.broadcasted_iota(jnp.int32, (count, count), 0) == lax.broadcasted_iota(
            jnp.int32, (count, count), 1
        )
        out[...] = jnp.sum(jnp.where(eye, col, 0.0), axis=0, keepdims=True)


def vmem():
    return pl.BlockSpec(memory_space=pltpu.VMEM)


def local(
    link_phases, active, bin_index, first_weight, first_bias,
    second_weight, second_bias, cotangent, logdet_cotangent,
):
    nt, nz = lax.axis_size("ta"), lax.axis_size("gz")
    dma = pltpu.SemaphoreType.DMA
    mem = pltpu.VMEM
    nx, nd = 2 * nt, nz // 2
    rows2, rows1 = 1024 // nx, 256 // nx
    scale = 1.0 / math.sqrt(nt * nz * PLANES * LANES)
    link, sum2, sum1 = pl.pallas_call(
        functools.partial(main_kernel, scale),
        out_shape=(
            jax.ShapeDtypeStruct((72, LANES), f32),
            jax.ShapeDtypeStruct((1024, LANES), bf16),
            jax.ShapeDtypeStruct((256, LANES), f32),
        ),
        in_specs=[pl.BlockSpec(memory_space=pltpu.HBM)] * 9,
        out_specs=(pl.BlockSpec(memory_space=pltpu.HBM),) * 3,
        scratch_shapes=[
            mem((3, 2, LT, LZ, LANES), f32),
            mem((LT, LZ, LANES), jnp.int32),
            mem((2, LT, LZ, LANES), jnp.int32),
            mem((288, 54), bf16),
            mem((1, HID), f32),
            mem((432, 288), bf16),
            mem((1, OUTC), f32),
            mem((2, LT, LZ, LANES), f32),
            mem((LT, LZ, LANES), f32),
            mem((72, LANES), f32),
            mem((24, LANES), jnp.int32),
            mem((24, LANES), f32),
            mem((2, 16, LANES), f32),
            mem((96, 240), bf16),
            mem((144, 864), bf16),
            mem((288, 432), bf16),
            mem((72, 288), bf16),
            mem((7, 32, LANES), f32),
            mem((64, LANES), f32),
            mem((560, 1024), bf16),
            mem((5, HID, 512), f32),
            mem((1440, 768), bf16),
            mem((LT, OUTC, 512), f32),
            mem((7, 32, LANES), f32),
            mem((7, 32, LANES), f32),
            mem((16, LANES), f32),
            mem((8, LANES), f32),
            mem((8, LANES), f32),
            mem((2, 16, LANES), f32),
            mem((5, 6, OUTC, LANES), bf16),
            mem((5, 6, HID, LANES), bf16),
            mem((96, LANES), f32),
            mem((448, LANES), f32),
            mem((1024, LANES), bf16),
            mem((nx, rows2, LANES), bf16),
            mem((rows2, LANES), bf16),
            mem((nd, rows2, LANES), bf16),
            mem((rows2, LANES), bf16),
            mem((256, LANES), f32),
            mem((nx, rows1, LANES), f32),
            mem((rows1, LANES), f32),
            mem((nd, rows1, LANES), f32),
            mem((rows1, LANES), f32),
            mem((72, LANES), f32),
            dma((9,)), dma((3,)), dma((8,)), dma((8,)), dma((8,)), dma((8,)), dma((8,)), dma((8,)), dma, dma,
            dma((nx,)), dma((nx,)), dma((nd,)), dma((nd,)), dma((nx,)), dma((nx,)),
            dma((nx,)), dma((nx,)), dma((nd,)), dma((nd,)), dma((nx,)), dma((nx,)),
        ],
        compiler_params=pltpu.CompilerParams(
            collective_id=0, has_side_effects=True, vmem_limit_bytes=56 * 1024 * 1024
        ),
        name="main_kernel",
    )(
        link_phases, active, bin_index,
        first_weight.reshape(288, 54), first_bias.reshape(1, HID),
        second_weight.reshape(432, 288), second_bias.reshape(1, OUTC),
        cotangent, logdet_cotangent,
    )
    link_grad, first, bias1, second, bias2 = pl.pallas_call(
        write_kernel,
        out_shape=(
            jax.ShapeDtypeStruct((3, 2, LT, LZ, LANES), f32),
            jax.ShapeDtypeStruct((288, 54), f32),
            jax.ShapeDtypeStruct((1, HID), f32),
            jax.ShapeDtypeStruct((432, 288), f32),
            jax.ShapeDtypeStruct((1, OUTC), f32),
        ),
        in_specs=[vmem()] * 3,
        out_specs=(vmem(),) * 5,
        compiler_params=pltpu.CompilerParams(vmem_limit_bytes=56 * 1024 * 1024),
        name="write_kernel",
    )(link, sum2, sum1)
    return (
        link_grad,
        first.reshape(9, HID, 54),
        bias1.reshape(HID),
        second.reshape(9, OUTC, 288),
        bias2.reshape(OUTC),
    )


def solution(mesh):
    return jax.shard_map(
        local,
        mesh=mesh,
        in_specs=(
            P(None, None, "ta", "gz", None),
            P("ta", "gz", None),
            P(None, "ta", "gz", None),
            P(), P(), P(), P(),
            P(None, "ta", "gz", None),
            P("ta", "gz", None),
        ),
        out_specs=(P(None, None, "ta", "gz", None), P(), P(), P(), P()),
        check_vma=False,
    )
```

```python
import functools
import math

import jax
import jax.numpy as jnp
from jax import lax
from jax.experimental import pallas as pl
from jax.experimental.pallas import tpu as pltpu
from jax.sharding import PartitionSpec as P

K = 8
LT = 3
LZ = 4
LANES = 128
HID = 32
OUTC = 48
PLANES = LT * LZ
MESH_ID = pl.DeviceIdType.MESH

min_share = 0.001
min_deriv = 0.001
keep_share = 1.0 - K * min_share
two_pi = 2.0 * math.pi

f32 = jnp.float32
bf16 = jnp.bfloat16


def lane_x(rows):
    return lax.broadcasted_iota(jnp.int32, (rows, LANES), 1) % 8


def rolled(value, amount):
    amount = amount % LANES
    if amount == 0:
        return value
    return pltpu.roll(value, amount, 1)


def shifted(value, step_y, step_x):
    near = rolled(value, -(8 * step_y + step_x))
    if step_x == 0:
        return near
    xs = lane_x(value.shape[0])
    if step_x > 0:
        wrap = rolled(value, -(8 * step_y + step_x - 8))
        return jnp.where(xs < 8 - step_x, near, wrap)
    wrap = rolled(value, -(8 * step_y + step_x + 8))
    return jnp.where(xs >= -step_x, near, wrap)


def nine_shifts(value):
    return [shifted(value, sy, sx) for sy in (-1, 0, 1) for sx in (-1, 0, 1)]


def shift_sum(blocks):
    total = None
    for ix, dx in enumerate((-1, 0, 1)):
        part = None
        for iy, dy in enumerate((-1, 0, 1)):
            piece = rolled(blocks[3 * iy + ix], 8 * dy)
            part = piece if part is None else part + piece
        part = shifted(part, 0, -dx)
        total = part if total is None else total + part
    return total


def sin_cos(angle):
    turns = jnp.floor(angle * (2.0 / math.pi) + 0.5)
    rest = angle - turns * 1.5703125
    rest = rest - turns * 4.837512969970703125e-4
    rest = rest - turns * 7.54978995489188e-8
    sq = rest * rest
    s = rest + rest * sq * (-1.6666654611e-1 + sq * (8.3321608736e-3 - sq * 1.9515295891e-4))
    c = 1.0 - 0.5 * sq + sq * sq * (
        4.166664568298827e-2 + sq * (-1.388731625493765e-3 + sq * 2.443315711809948e-5)
    )
    quad = turns.astype(jnp.int32)
    swap = (quad & 1) == 1
    sin_v = jnp.where(swap, c, s)
    cos_v = jnp.where(swap, s, c)
    sin_v = jnp.where((quad & 2) == 2, -sin_v, sin_v)
    cos_v = jnp.where(((quad + 1) & 2) == 2, -cos_v, cos_v)
    return sin_v, cos_v


def loop_phases(x_two, y_two):
    plaq, wide, tall = [], [], []
    for x, y in zip(x_two, y_two):
        y_x = shifted(y, 0, 1)
        x_y = shifted(x, 1, 0)
        plaq.append(x + y_x - x_y - y)
        wide.append(x + shifted(x, 0, 1) + shifted(y, 0, 2) - shifted(x, 1, 1) - x_y - y)
        tall.append(x + y_x + shifted(y, 1, 1) - shifted(x, 2, 0) - shifted(y, 1, 0) - y)
    out = []
    for two in (plaq, wide, tall):
        out.append((two[0], two[1], -(two[0] + two[1])))
    return out


DIRS = [(dt, dz) for dt in (-1, 0, 1) for dz in (-1, 0, 1) if (dt, dz) != (0, 0)]


def neighbour(dt, dz):
    nt, nz = lax.axis_size("ta"), lax.axis_size("gz")
    mt, mz = lax.axis_index("ta"), lax.axis_index("gz")
    return (lax.rem(mt + dt + nt, nt), lax.rem(mz + dz + nz, nz))


def main_kernel(
    scale, *refs
):
    given, refs = refs[:9], refs[9:]
    (out_link, out2, out1), refs = refs[:3], refs[3:]
    held, refs = refs[:9], refs[9:]
    links, act, bins_in, first_w, b1, second_w, b2, cot_in, ldc_in = held
    (
        lk, bins, cot, site, w1p, w2k, wt2, wt1,
        lbuf, fs, fcols, pres, cols, sigs, red, coef, xab, pgs, pgr, pgv,
        pbuf, qbuf, fgs, tails, gm2, got_a, mid_b, got_b, fin_d,
        gm1, got_e, mid_f, got_f, fin_g, link_out,
        in_sem, out_sem, send_l, recv_l, send_p, recv_p, send_q, recv_q, send_g, recv_g,
        send_a, recv_a, send_b, recv_b, send_d, recv_d,
        send_e, recv_e, send_f, recv_f, send_h, recv_h,
    ) = refs
    loads = [pltpu.make_async_copy(src, dst, in_sem.at[i]) for i, (src, dst) in enumerate(zip(given, held))]
    for load in loads:
        load.start()

    nt, nz = lax.axis_size("ta"), lax.axis_size("gz")
    mt, mz = lax.axis_index("ta"), lax.axis_index("gz")
    nx, nd = 2 * nt, nz // 2
    side, deep = lax.rem(mz, 2), mz // 2
    mx = 2 * mt + side

    flips, weight = [(0, 1 - 2 * side)], 1
    while weight < nt:
        flips.append((weight * (1 - 2 * lax.rem(mt // weight, 2)), 0))
        weight *= 2

    def wide_peer(k):
        along, across = mt, mz
        for bit, (dt, dz) in enumerate(flips):
            if k >> bit & 1:
                along, across = along + dt, across + dz
        return (along, across)

    def wide_hops(k):
        steps = (0, 1, 2, 1)
        return steps[(k >> 2) & 3] + steps[((k >> 4) & 1) * 2 + (k & 1)]

    def deep_peer(k):
        return (mt, lax.rem(mz + 2 * k, nz))

    wide_order = sorted(range(1, nx), key=lambda k: -wide_hops(k))
    deep_order = sorted(range(1, nd), key=lambda k: -min(k, nd - k))
    barrier = pltpu.get_barrier_semaphore()
    cross = lax.rem(mz - 1 + 2 * side + nz, nz)
    greeted = [(lax.rem(mt + dt + nt, nt), cross) for dt in (-1, 0, 1)]
    greeted += [wide_peer(k) for k in wide_order] + [deep_peer(k) for k in deep_order]
    for peer in greeted:
        pl.semaphore_signal(barrier, inc=1, device_id=peer, device_id_type=MESH_ID)

    def to_wide(src, dst, send, recv):
        copies = []
        for k in wide_order:
            peer = wide_peer(k)
            copy = pltpu.make_async_remote_copy(
                src_ref=src(2 * peer[0] + lax.rem(peer[1], 2)), dst_ref=dst(k),
                send_sem=send.at[k], recv_sem=recv.at[k], device_id=peer, device_id_type=MESH_ID,
            )
            copy.start()
            copies.append(copy)
        return copies

    def to_deep(src, dst, send, recv):
        copies = []
        for k in deep_order:
            copy = pltpu.make_async_remote_copy(
                src_ref=src, dst_ref=dst,
                send_sem=send.at[k], recv_sem=recv.at[k], device_id=deep_peer(k), device_id_type=MESH_ID,
            )
            copy.start()
            copies.append(copy)
        return copies

    loads[0].wait()
    for d in range(3):
        for c in range(2):
            for t in range(LT):
                lk[pl.ds(d * 24 + c * 12 + t * 4, LZ), :] = links[d, c, t]
    for comp in range(4):
        for t in range(LT):
            lbuf[2 + t, pl.ds(8 + comp, LZ, stride=4), :] = lk[pl.ds(comp * PLANES + t * LZ, LZ), :]
    pl.semaphore_wait(barrier, len(greeted))

    t_from = {-1: slice(2, 4), 0: slice(2, 5), 1: slice(3, 5)}
    t_into = {-1: slice(5, 7), 0: slice(2, 5), 1: slice(0, 2)}
    z_from = {-1: slice(8, 16), 0: slice(8, 24), 1: slice(16, 24)}
    z_into = {-1: slice(24, 32), 0: slice(8, 24), 1: slice(0, 8)}
    link_copies = []
    for i, (dt, dz) in enumerate(DIRS):
        copy = pltpu.make_async_remote_copy(
            src_ref=lbuf.at[t_from[dt], z_from[dz]],
            dst_ref=lbuf.at[t_into[dt], z_into[dz]],
            send_sem=send_l.at[i], recv_sem=recv_l.at[i],
            device_id=neighbour(dt, dz), device_id_type=MESH_ID,
        )
        copy.start()
        link_copies.append(copy)
    fs[...] = jnp.zeros_like(fs)

    for load in loads[1:]:
        load.wait()
    for t in range(LT):
        site[0, pl.ds(t * LZ, LZ), :] = act[t].astype(f32)
        site[1, pl.ds(t * LZ, LZ), :] = ldc_in[t]
        for c in range(2):
            bins[pl.ds(c * 12 + t * LZ, LZ), :] = bins_in[c, t]
            cot[pl.ds(c * 12 + t * LZ, LZ), :] = cot_in[c, t]
    nt_dims = (((1,), (1,)), ((), ()))

    def one_hot(rows, padded_dim):
        shape = (rows, 54) if padded_dim == 0 else (54, rows)
        wide = lax.broadcasted_iota(jnp.int32, shape, padded_dim)
        tight = lax.broadcasted_iota(jnp.int32, shape, 1 - padded_dim)
        hit = (wide < 72) & (wide % 8 < 6) & (tight == (wide // 8) * 6 + wide % 8)
        return jnp.where(hit, 1.0, 0.0).astype(bf16)

    spread80 = one_hot(80, 1)
    w1p[...] = jnp.concatenate(
        [
            jnp.dot(first_w[i * 96 : (i + 1) * 96, :], spread80, preferred_element_type=f32)
            for i in range(3)
        ],
        axis=1,
    ).astype(bf16)
    w2k[...] = jnp.concatenate(
        [second_w[i * 144 : (i + 1) * 144, :].astype(f32) for i in range(3)], axis=1
    ).astype(bf16)
    diag = lax.broadcasted_iota(jnp.int32, (288, 288), 0) == lax.broadcasted_iota(jnp.int32, (288, 288), 1)
    wt2[...] = lax.dot_general(
        jnp.where(diag, 1.0, 0.0).astype(bf16), second_w[...], nt_dims, preferred_element_type=f32
    ).astype(bf16)

    def as_column(row_ref, count):
        eye = lax.broadcasted_iota(jnp.int32, (count, count), 0) == lax.broadcasted_iota(
            jnp.int32, (count, count), 1
        )
        return jnp.sum(jnp.where(eye, row_ref[...], 0.0), axis=1, keepdims=True)

    b1_col, b2_col = as_column(b1, HID), as_column(b2, OUTC)
    for copy in link_copies:
        copy.wait()

    def feature_slice(t, carry):
        x_two = [lbuf[t, pl.ds(comp, 8, stride=4), :] for comp in (0, 1)]
        y_two = [lbuf[t, pl.ds(comp, 8, stride=4), :] for comp in (2, 3)]
        for which, three in enumerate(loop_phases(x_two, y_two)):
            pairs = [sin_cos(psi) for psi in three]
            fs[pl.ds(2 * which, 8, stride=8), :] = (pairs[0][1] + pairs[1][1] + pairs[2][1]) * (1.0 / 3.0)
            fs[pl.ds(2 * which + 1, 8, stride=8), :] = (pairs[0][0] + pairs[1][0] + pairs[2][0]) * (1.0 / 3.0)
        row = pl.multiple_of(t * 80, 16)
        for z in range(8):
            blocks = nine_shifts(fs[z * 8 : z * 8 + 8, :])
            blocks.append(jnp.zeros((8, LANES), f32))
            fcols[pl.ds(row, 80), z * LANES : (z + 1) * LANES] = jnp.concatenate(blocks, axis=0).astype(bf16)
        return carry

    lax.fori_loop(0, 7, feature_slice, 0, unroll=True)

    def hidden_slice(t, carry):
        got = jnp.dot(
            w1p[...], fcols[pl.ds(pl.multiple_of(t * 80, 16), 240), :], preferred_element_type=f32
        )
        pre = got[0:32, 0:768] + got[32:64, 128:896] + got[64:96, 256:1024] + b1_col
        pres[t] = pre[:, 128:640]
        hid = pre / (1.0 + jnp.exp(-pre))
        row = pl.multiple_of(t * 288, 16)
        for z in range(6):
            blocks = nine_shifts(hid[:, z * LANES : (z + 1) * LANES])
            cols[pl.ds(row, 288), z * LANES : (z + 1) * LANES] = jnp.concatenate(blocks, axis=0).astype(bf16)
        return carry

    lax.fori_loop(0, 5, hidden_slice, 0, unroll=True)

    level = lax.broadcasted_iota(jnp.int32, (K, LANES), 0)

    def param_slice(t, carry):
        got = jnp.dot(
            w2k[...], cols[pl.ds(pl.multiple_of(t * 288, 16), 864), :], preferred_element_type=f32
        )
        par = got[0:48, 0:512] + got[48:96, 128:640] + got[96:144, 256:768] + b2_col
        grow = jnp.exp(-jnp.abs(par))
        soft = jnp.maximum(par, 0.0) + jnp.log1p(grow)
        sigs[t] = jnp.where(par >= 0.0, 1.0, grow) / (1.0 + grow)
        for z in range(LZ):
            for c in range(2):
                plane = t * LZ + z
                chosen = bins[pl.ds(c * PLANES + plane, 1), :]
                pick = level == chosen
                below = level < chosen
                after = level == ((chosen + 1) & 7)
                cut = soft[c * 24 : c * 24 + 24, z * LANES : (z + 1) * LANES]
                sw, sh, sd = cut[0:8], cut[8:16], cut[16:24]
                sums = (
                    sw, jnp.where(pick, sw, 0.0),
                    sh, jnp.where(pick, sh, 0.0), jnp.where(below, sh, 0.0),
                    jnp.where(pick, sd, 0.0), jnp.where(after, sd, 0.0),
                )
                for q, value in enumerate(sums):
                    red[q, pl.ds(c * 16 + plane, 1), :] = jnp.sum(value, axis=0, keepdims=True)
        return carry

    lax.fori_loop(0, LT, param_slice, 0, unroll=True)

    live = site[0, 0:12, :]
    g_log = live * site[1, 0:12, :]
    for c in range(2):
        x = lk[c * 12 : c * 12 + 12, :]
        tl = lk[48 + c * 12 : 60 + c * 12, :]
        xab[0:8, :] = lk[c * 12 + 4 : c * 12 + 12, :]
        xab[8:12, :] = lbuf[5, pl.ds(8 + c, LZ, stride=4), :]
        theta = x + shifted(tl, 0, 1) - xab[0:12, :] - tl
        my_cot = cot[c * 12 : c * 12 + 12, :]
        g_new = -live * my_cot
        rows = slice(c * 16, c * 16 + 12)
        sum_w, pick_w = red[0, rows, :], red[1, rows, :]
        sum_h, pick_h, low_h = red[2, rows, :], red[3, rows, :], red[4, rows, :]
        d0 = min_deriv + red[5, rows, :]
        d1 = min_deriv + red[6, rows, :]
        inv_w, inv_h = 1.0 / sum_w, 1.0 / sum_h
        frac_w, frac_h, frac_low = pick_w * inv_w, pick_h * inv_h, low_h * inv_h
        width = min_share + keep_share * frac_w
        height = min_share + keep_share * frac_h
        r = height / width
        u = 1.0 / (1.0 + jnp.exp(-theta))
        v = 1.0 - u
        q = u * v
        den = r + (d0 + d1 - 2.0 * r) * q
        top = r * u * u + d0 * q
        numer = d1 * u * u + 2.0 * r * q + d0 * v * v
        inv_den = 1.0 / den
        g_top = g_new * two_pi * height * inv_den
        g_den = -(g_top * top + 2.0 * g_log) * inv_den
        g_num = g_log / numer
        g_h = g_new * two_pi * top * inv_den + g_log / height
        g_r = g_top * u * u + g_den * (1.0 - 2.0 * q) + 2.0 * g_num * q + g_log / r
        g_d0 = (g_top + g_den) * q + g_num * v * v
        g_d1 = g_den * q + g_num * u * u
        g_q = g_top * d0 + g_den * (d0 + d1 - 2.0 * r) + 2.0 * g_num * r
        g_u = 2.0 * g_top * r * u + 2.0 * g_num * (d1 * u - d0 * v) + g_q * (1.0 - 2.0 * u)
        g_theta = g_u * q + g_log * (1.0 - 2.0 * u)
        all_h = g_h + g_r / width
        all_w = -g_r * r / width
        base = two_pi * g_new
        a_w = keep_share * all_w * inv_w
        coef[0, rows, :] = a_w
        coef[1, rows, :] = a_w * frac_w
        coef[2, rows, :] = keep_share * all_h * inv_h
        coef[3, rows, :] = keep_share * base * inv_h
        coef[4, rows, :] = keep_share * (all_h * frac_h + base * frac_low) * inv_h
        coef[5, rows, :] = g_d0
        coef[6, rows, :] = g_d1
        grad = g_theta + live * my_cot
        pgv[c, 4:16, :] = grad
        pgs[c * 4 : c * 4 + 4, :] = grad[8:12, :]

    phase_copy = pltpu.make_async_remote_copy(
        src_ref=pgs, dst_ref=pgr, send_sem=send_g, recv_sem=recv_g,
        device_id=neighbour(1, 0), device_id_type=MESH_ID,
    )
    phase_copy.start()

    def param_grad_slice(t, total):
        for z in range(LZ):
            plane = t * LZ + z
            parts = []
            for c in range(2):
                chosen = bins[pl.ds(c * PLANES + plane, 1), :]
                pick = level == chosen
                below = level < chosen
                after = level == ((chosen + 1) & 7)
                a = [coef[k, pl.ds(c * 16 + plane, 1), :] for k in range(7)]
                sig = sigs[t, c * 24 : c * 24 + 24, z * LANES : (z + 1) * LANES]
                parts.append((jnp.where(pick, a[0], 0.0) - a[1]) * sig[0:8])
                parts.append((jnp.where(pick, a[2], jnp.where(below, a[3], 0.0)) - a[4]) * sig[8:16])
                parts.append((jnp.where(pick, a[5], jnp.where(after, a[6], 0.0))) * sig[16:24])
            grad = jnp.concatenate(parts, axis=0)
            pbuf[t + 1, z + 1] = grad.astype(bf16)
            total = total + grad
        return total

    bias2 = jnp.sum(
        lax.fori_loop(0, LT, param_grad_slice, jnp.zeros((OUTC, LANES), f32), unroll=True), axis=1, keepdims=True
    )

    h_from = {-1: slice(1, 2), 0: slice(1, 4), 1: slice(3, 4)}
    h_into = {-1: slice(4, 5), 0: slice(1, 4), 1: slice(0, 1)}
    v_from = {-1: slice(1, 2), 0: slice(1, 5), 1: slice(4, 5)}
    v_into = {-1: slice(5, 6), 0: slice(1, 5), 1: slice(0, 1)}

    def send_halo(buf, send, recv):
        copies = []
        for i, (dt, dz) in enumerate(DIRS):
            copy = pltpu.make_async_remote_copy(
                src_ref=buf.at[h_from[dt], v_from[dz]],
                dst_ref=buf.at[h_into[dt], v_into[dz]],
                send_sem=send.at[i], recv_sem=recv.at[i],
                device_id=neighbour(dt, dz), device_id_type=MESH_ID,
            )
            copy.start()
            copies.append(copy)
        return copies

    param_copies = send_halo(pbuf, send_p, recv_p)

    def spread(buf, t, rows):
        own = jnp.concatenate([buf[t + 1, z + 1] for z in range(LZ)], axis=1)
        one = jnp.zeros((rows, LANES), bf16)
        two = jnp.zeros((rows, 2 * LANES), bf16)
        return jnp.concatenate(
            [
                jnp.concatenate([own, two], axis=1),
                jnp.concatenate([one, own, one], axis=1),
                jnp.concatenate([two, own], axis=1),
            ],
            axis=0,
        )

    spread_p = [spread(pbuf, t, OUTC) for t in range(LT)]
    for i in range(3):
        total = None
        for t in range(LT):
            part = lax.dot_general(
                spread_p[t], cols[(t + i) * 288 : (t + i + 1) * 288, :], nt_dims, preferred_element_type=f32
            )
            total = part if total is None else total + part
        gm2[i * 144 : (i + 1) * 144, :] = total[:, 0:128].astype(bf16)
        gm2[432 + i * 144 : 576 + i * 144, :] = total[:, 128:256].astype(bf16)
        tails[i * 144 : (i + 1) * 144, :] = jnp.concatenate(
            [total[:, 256:288], jnp.zeros((144, 96), f32)], axis=1
        )
    tails[432:448, :] = jnp.zeros((16, LANES), f32)
    tail = tails[0:112, :]
    for g in range(1, 4):
        tail = tail + pltpu.roll(tails[g * 112 : (g + 1) * 112, :], 32 * g, 1)
    gm2[864:976, :] = tail.astype(bf16)
    gm2[976:1024, :] = jnp.zeros((48, LANES), bf16)

    rows2, rows1 = 1024 // nx, 256 // nx

    def wide_rows(index, rows):
        return pl.ds(pl.multiple_of(index * rows, rows), rows)

    copies_a = to_wide(
        lambda index: gm2.at[wide_rows(index, rows2)], lambda k: got_a.at[k], send_a, recv_a
    )

    for copy in param_copies:
        copy.wait()

    def stacked(buf, t):
        rows = []
        for i in range(3):
            for j in range(3):
                rows.append(jnp.concatenate([buf[t + 2 - i, z + 2 - j] for z in range(LZ)], axis=1))
        return jnp.concatenate(rows, axis=0)

    def hidden_grad_slice(t, total):
        got = jnp.dot(wt2[...], stacked(pbuf, t), preferred_element_type=f32)
        for z in range(LZ):
            lanes = slice(z * LANES, (z + 1) * LANES)
            grad = shift_sum([got[b * HID : (b + 1) * HID, lanes] for b in range(9)])
            pre = pres[t + 1, :, lanes]
            sig = 1.0 / (1.0 + jnp.exp(-pre))
            grad = grad * (sig * (1.0 + pre * (1.0 - sig)))
            qbuf[t + 1, z + 1] = grad.astype(bf16)
            total = total + grad
        return total

    bias1 = jnp.sum(
        lax.fori_loop(0, LT, hidden_grad_slice, jnp.zeros((HID, LANES), f32), unroll=True), axis=1, keepdims=True
    )

    tight80 = one_hot(80, 0)
    spread_q = [spread(qbuf, t, HID) for t in range(LT)]
    g1 = []
    for i in range(3):
        total = None
        for t in range(LT):
            row = (t + 1 + i) * 80
            part = lax.dot_general(
                spread_q[t], fcols[row : row + 80, 128:896], nt_dims, preferred_element_type=f32
            )
            total = part if total is None else total + part
        g1.append(jnp.dot(total.astype(bf16), tight80, preferred_element_type=f32))
    g1 = jnp.concatenate(g1, axis=0)
    g1 = jnp.concatenate([g1, jnp.zeros((288, 74), f32)], axis=1)
    gm1[0:144, :] = g1[0:144] + pltpu.roll(g1[144:288], 64, 1)
    bias = jnp.concatenate([bias2, bias1, jnp.zeros((32, 1), f32)], axis=0)
    lane = lax.broadcasted_iota(jnp.int32, (112, LANES), 1)
    gm1[144:256, :] = jnp.where(lane == 0, bias, 0.0)
    copies_e = to_wide(
        lambda index: gm1.at[wide_rows(index, rows1)], lambda k: got_e.at[k], send_e, recv_e
    )

    preact_copies = send_halo(qbuf, send_q, recv_q)

    def in_order(parts, count):
        total = parts[0].astype(f32)
        for k in range(1, count):
            total = total + parts[k].astype(f32)
        return total

    total = gm2[wide_rows(mx, rows2), :].astype(f32)
    for k, copy in enumerate(copies_a):
        copy.wait()
        total = total + got_a[wide_order[k]].astype(f32)
    mid_b[...] = (total * scale).astype(bf16)
    copies_b = to_deep(mid_b, got_b.at[deep], send_b, recv_b)
    got_b[deep] = mid_b[...]

    wt1[...] = lax.dot_general(
        one_hot(72, 0), first_w[...], nt_dims, preferred_element_type=f32
    ).astype(bf16)

    x_two = [lk[0:12, :], lk[12:24, :]]
    y_two = [lk[24:36, :], lk[36:48, :]]
    pairs = [[sin_cos(psi) for psi in three] for three in loop_phases(x_two, y_two)]

    total = gm1[wide_rows(mx, rows1), :]
    for k, copy in enumerate(copies_e):
        copy.wait()
        total = total + got_e[wide_order[k]]
    total = total * scale
    mid_f[...] = total
    copies_f = to_deep(mid_f, got_f.at[deep], send_f, recv_f)
    got_f[deep] = total

    for copy in copies_b:
        copy.wait()
    fin_d[...] = in_order(got_b, nd).astype(bf16)
    copies_d = to_wide(lambda index: fin_d, lambda k: out2.at[wide_rows(mx, rows2)], send_d, recv_d)
    stores = [pltpu.make_async_copy(fin_d, out2.at[wide_rows(mx, rows2)], out_sem.at[1])]
    stores[0].start()

    for copy in copies_f:
        copy.wait()
    fin_g[...] = in_order(got_f, nd)
    copies_h = to_wide(lambda index: fin_g, lambda k: out1.at[wide_rows(mx, rows1)], send_h, recv_h)
    stores.append(pltpu.make_async_copy(fin_g, out1.at[wide_rows(mx, rows1)], out_sem.at[2]))
    stores[1].start()

    phase_copy.wait()
    for copy in preact_copies:
        copy.wait()

    def feature_grad_slice(t, carry):
        got = jnp.dot(wt1[...], stacked(qbuf, t), preferred_element_type=f32)
        for z in range(LZ):
            lanes = slice(z * LANES, (z + 1) * LANES)
            grad = shift_sum([got[b * 8 : (b + 1) * 8, lanes] for b in range(9)])
            fgs[pl.ds(pl.multiple_of((t * LZ + z) * 8, 8), 8), :] = grad
        return carry

    lax.fori_loop(0, LT, feature_grad_slice, 0, unroll=True)

    third = 1.0 / 3.0
    loop_grads = []
    for which in range(3):
        g_cos = fgs[pl.ds(2 * which, PLANES, stride=8), :] * third
        g_sin = fgs[pl.ds(2 * which + 1, PLANES, stride=8), :] * third
        three = [g_sin * cos_v - g_cos * sin_v for sin_v, cos_v in pairs[which]]
        loop_grads.append((three[0] - three[2], three[1] - three[2]))
    for c in range(2):
        dp, dw, dr = loop_grads[0][c], loop_grads[1][c], loop_grads[2][c]
        pair = dp + dr
        x_ctx = (
            dp + dw + dr
            - shifted(dp + dw, -1, 0)
            + shifted(dw, 0, -1)
            - shifted(dw, -1, -1)
            - shifted(dr, -2, 0)
        )
        y_ctx = (
            shifted(pair, 0, -1)
            - pair
            - dw
            + shifted(dw, 0, -2)
            + shifted(dr, -1, -1)
            - shifted(dr, -1, 0)
        )
        pgv[c, 0:4, :] = pgr[c * 4 : c * 4 + 4, :]
        grad = pgv[c, 4:16, :]
        prev = pgv[c, 0:12, :]
        link_out[c * 12 : c * 12 + 12, :] = grad - prev + x_ctx
        link_out[24 + c * 12 : 36 + c * 12, :] = y_ctx
        link_out[48 + c * 12 : 60 + c * 12, :] = cot[c * 12 : c * 12 + 12, :] - grad + shifted(grad, 0, -1)

    stores.append(pltpu.make_async_copy(link_out, out_link, out_sem.at[0]))
    stores[2].start()

    for copy in copies_d + stores + copies_h:
        copy.wait()


def write_kernel(link, sum2, sum1, out_link, out_first, out_bias1, out_second, out_bias2):
    for d in range(3):
        for c in range(2):
            for t in range(LT):
                out_link[d, c, t] = link[pl.ds(d * 24 + c * 12 + t * 4, LZ), :]
    out_second[:, 0:128] = sum2[0:432, :].astype(f32)
    out_second[:, 128:256] = sum2[432:864, :].astype(f32)
    tail = sum2[864:976, :].astype(f32)
    for g in range(4):
        count = min(112, 432 - g * 112)
        out_second[g * 112 : g * 112 + count, 256:288] = rolled(tail, -32 * g)[0:count, 0:32]
    half = sum1[0:144, :]
    out_first[0:144, :] = half[:, 0:54]
    out_first[144:288, :] = pltpu.roll(half, 64, 1)[:, 0:54]
    for out, begin, count in ((out_bias2, 144, OUTC), (out_bias1, 192, HID)):
        col = sum1[begin : begin + count, :][:, 0:1]
        eye = lax.broadcasted_iota(jnp.int32, (count, count), 0) == lax.broadcasted_iota(
            jnp.int32, (count, count), 1
        )
        out[...] = jnp.sum(jnp.where(eye, col, 0.0), axis=0, keepdims=True)


def vmem():
    return pl.BlockSpec(memory_space=pltpu.VMEM)


def local(
    link_phases, active, bin_index, first_weight, first_bias,
    second_weight, second_bias, cotangent, logdet_cotangent,
):
    nt, nz = lax.axis_size("ta"), lax.axis_size("gz")
    dma = pltpu.SemaphoreType.DMA
    mem = pltpu.VMEM
    nx, nd = 2 * nt, nz // 2
    rows2, rows1 = 1024 // nx, 256 // nx
    scale = 1.0 / math.sqrt(nt * nz * PLANES * LANES)
    link, sum2, sum1 = pl.pallas_call(
        functools.partial(main_kernel, scale),
        out_shape=(
            jax.ShapeDtypeStruct((72, LANES), f32),
            jax.ShapeDtypeStruct((1024, LANES), bf16),
            jax.ShapeDtypeStruct((256, LANES), f32),
        ),
        in_specs=[pl.BlockSpec(memory_space=pltpu.HBM)] * 9,
        out_specs=(pl.BlockSpec(memory_space=pltpu.HBM),) * 3,
        scratch_shapes=[
            mem((3, 2, LT, LZ, LANES), f32),
            mem((LT, LZ, LANES), jnp.int32),
            mem((2, LT, LZ, LANES), jnp.int32),
            mem((288, 54), bf16),
            mem((1, HID), f32),
            mem((432, 288), bf16),
            mem((1, OUTC), f32),
            mem((2, LT, LZ, LANES), f32),
            mem((LT, LZ, LANES), f32),
            mem((72, LANES), f32),
            mem((24, LANES), jnp.int32),
            mem((24, LANES), f32),
            mem((2, 16, LANES), f32),
            mem((96, 240), bf16),
            mem((144, 864), bf16),
            mem((288, 432), bf16),
            mem((72, 288), bf16),
            mem((7, 32, LANES), f32),
            mem((64, LANES), f32),
            mem((560, 1024), bf16),
            mem((5, HID, 512), f32),
            mem((1440, 768), bf16),
            mem((LT, OUTC, 512), f32),
            mem((7, 32, LANES), f32),
            mem((7, 32, LANES), f32),
            mem((16, LANES), f32),
            mem((8, LANES), f32),
            mem((8, LANES), f32),
            mem((2, 16, LANES), f32),
            mem((5, 6, OUTC, LANES), bf16),
            mem((5, 6, HID, LANES), bf16),
            mem((96, LANES), f32),
            mem((448, LANES), f32),
            mem((1024, LANES), bf16),
            mem((nx, rows2, LANES), bf16),
            mem((rows2, LANES), bf16),
            mem((nd, rows2, LANES), bf16),
            mem((rows2, LANES), bf16),
            mem((256, LANES), f32),
            mem((nx, rows1, LANES), f32),
            mem((rows1, LANES), f32),
            mem((nd, rows1, LANES), f32),
            mem((rows1, LANES), f32),
            mem((72, LANES), f32),
            dma((9,)), dma((3,)), dma((8,)), dma((8,)), dma((8,)), dma((8,)), dma((8,)), dma((8,)), dma, dma,
            dma((nx,)), dma((nx,)), dma((nd,)), dma((nd,)), dma((nx,)), dma((nx,)),
            dma((nx,)), dma((nx,)), dma((nd,)), dma((nd,)), dma((nx,)), dma((nx,)),
        ],
        compiler_params=pltpu.CompilerParams(
            collective_id=0, has_side_effects=True, vmem_limit_bytes=56 * 1024 * 1024
        ),
        name="main_kernel",
    )(
        link_phases, active, bin_index,
        first_weight.reshape(288, 54), first_bias.reshape(1, HID),
        second_weight.reshape(432, 288), second_bias.reshape(1, OUTC),
        cotangent, logdet_cotangent,
    )
    link_grad, first, bias1, second, bias2 = pl.pallas_call(
        write_kernel,
        out_shape=(
            jax.ShapeDtypeStruct((3, 2, LT, LZ, LANES), f32),
            jax.ShapeDtypeStruct((288, 54), f32),
            jax.ShapeDtypeStruct((1, HID), f32),
            jax.ShapeDtypeStruct((432, 288), f32),
            jax.ShapeDtypeStruct((1, OUTC), f32),
        ),
        in_specs=[vmem()] * 3,
        out_specs=(vmem(),) * 5,
        compiler_params=pltpu.CompilerParams(vmem_limit_bytes=56 * 1024 * 1024),
        name="write_kernel",
    )(link, sum2, sum1)
    return (
        link_grad,
        first.reshape(9, HID, 54),
        bias1.reshape(HID),
        second.reshape(9, OUTC, 288),
        bias2.reshape(OUTC),
    )


def solution(mesh):
    return jax.shard_map(
        local,
        mesh=mesh,
        in_specs=(
            P(None, None, "ta", "gz", None),
            P("ta", "gz", None),
            P(None, "ta", "gz", None),
            P(), P(), P(), P(),
            P(None, "ta", "gz", None),
            P("ta", "gz", None),
        ),
        out_specs=(P(None, None, "ta", "gz", None), P(), P(), P(), P()),
        check_vma=False,
    )
```

```python
import functools
import math

import jax
import jax.numpy as jnp
from jax import lax
from jax.experimental import pallas as pl
from jax.experimental.pallas import tpu as pltpu
from jax.sharding import PartitionSpec as P

K = 8
LT = 3
LZ = 4
LANES = 128
HID = 32
OUTC = 48
PLANES = LT * LZ
MESH_ID = pl.DeviceIdType.MESH

min_share = 0.001
min_deriv = 0.001
keep_share = 1.0 - K * min_share
two_pi = 2.0 * math.pi

f32 = jnp.float32
bf16 = jnp.bfloat16


def lane_x(rows):
    return lax.broadcasted_iota(jnp.int32, (rows, LANES), 1) % 8


def rolled(value, amount):
    amount = amount % LANES
    if amount == 0:
        return value
    return pltpu.roll(value, amount, 1)


def shifted(value, step_y, step_x):
    near = rolled(value, -(8 * step_y + step_x))
    if step_x == 0:
        return near
    xs = lane_x(value.shape[0])
    if step_x > 0:
        wrap = rolled(value, -(8 * step_y + step_x - 8))
        return jnp.where(xs < 8 - step_x, near, wrap)
    wrap = rolled(value, -(8 * step_y + step_x + 8))
    return jnp.where(xs >= -step_x, near, wrap)


def nine_shifts(value):
    return [shifted(value, sy, sx) for sy in (-1, 0, 1) for sx in (-1, 0, 1)]


def shift_sum(blocks):
    total = None
    for ix, dx in enumerate((-1, 0, 1)):
        part = None
        for iy, dy in enumerate((-1, 0, 1)):
            piece = rolled(blocks[3 * iy + ix], 8 * dy)
            part = piece if part is None else part + piece
        part = shifted(part, 0, -dx)
        total = part if total is None else total + part
    return total


def sin_cos(angle):
    turns = jnp.floor(angle * (2.0 / math.pi) + 0.5)
    rest = angle - turns * 1.5703125
    rest = rest - turns * 4.837512969970703125e-4
    rest = rest - turns * 7.54978995489188e-8
    sq = rest * rest
    s = rest + rest * sq * (-1.6666654611e-1 + sq * (8.3321608736e-3 - sq * 1.9515295891e-4))
    c = 1.0 - 0.5 * sq + sq * sq * (
        4.166664568298827e-2 + sq * (-1.388731625493765e-3 + sq * 2.443315711809948e-5)
    )
    quad = turns.astype(jnp.int32)
    swap = (quad & 1) == 1
    sin_v = jnp.where(swap, c, s)
    cos_v = jnp.where(swap, s, c)
    sin_v = jnp.where((quad & 2) == 2, -sin_v, sin_v)
    cos_v = jnp.where(((quad + 1) & 2) == 2, -cos_v, cos_v)
    return sin_v, cos_v


def loop_phases(x_two, y_two):
    plaq, wide, tall = [], [], []
    for x, y in zip(x_two, y_two):
        y_x = shifted(y, 0, 1)
        x_y = shifted(x, 1, 0)
        plaq.append(x + y_x - x_y - y)
        wide.append(x + shifted(x, 0, 1) + shifted(y, 0, 2) - shifted(x, 1, 1) - x_y - y)
        tall.append(x + y_x + shifted(y, 1, 1) - shifted(x, 2, 0) - shifted(y, 1, 0) - y)
    out = []
    for two in (plaq, wide, tall):
        out.append((two[0], two[1], -(two[0] + two[1])))
    return out


DIRS = [(dt, dz) for dt in (-1, 0, 1) for dz in (-1, 0, 1) if (dt, dz) != (0, 0)]


def neighbour(dt, dz):
    nt, nz = lax.axis_size("ta"), lax.axis_size("gz")
    mt, mz = lax.axis_index("ta"), lax.axis_index("gz")
    return (lax.rem(mt + dt + nt, nt), lax.rem(mz + dz + nz, nz))


def main_kernel(
    scale, *refs
):
    given, refs = refs[:9], refs[9:]
    (out_link, out2, out1), refs = refs[:3], refs[3:]
    held, refs = refs[:9], refs[9:]
    links, act, bins_in, first_w, b1, second_w, b2, cot_in, ldc_in = held
    (
        lk, bins, cot, site, w1p, w2k, wt2, wt1,
        lbuf, fs, fcols, pres, cols, sigs, red, coef, xab, pgs, pgr, pgv,
        pbuf, qbuf, fgs, tails, gm2, got_a, mid_b, got_b, fin_d,
        gm1, got_e, mid_f, got_f, fin_g, link_out,
        in_sem, out_sem, send_l, recv_l, send_p, recv_p, send_q, recv_q, send_g, recv_g,
        send_a, recv_a, send_b, recv_b, send_d, recv_d,
        send_e, recv_e, send_f, recv_f, send_h, recv_h,
    ) = refs
    loads = [pltpu.make_async_copy(src, dst, in_sem.at[i]) for i, (src, dst) in enumerate(zip(given, held))]
    for load in loads:
        load.start()

    nt, nz = lax.axis_size("ta"), lax.axis_size("gz")
    mt, mz = lax.axis_index("ta"), lax.axis_index("gz")
    nx, nd = 2 * nt, nz // 2
    side, deep = lax.rem(mz, 2), mz // 2
    mx = 2 * mt + side

    flips, weight = [(0, 1 - 2 * side)], 1
    while weight < nt:
        flips.append((weight * (1 - 2 * lax.rem(mt // weight, 2)), 0))
        weight *= 2

    def wide_peer(k):
        along, across = mt, mz
        for bit, (dt, dz) in enumerate(flips):
            if k >> bit & 1:
                along, across = along + dt, across + dz
        return (along, across)

    def wide_hops(k):
        steps = (0, 1, 2, 1)
        return steps[(k >> 2) & 3] + steps[((k >> 4) & 1) * 2 + (k & 1)]

    def deep_peer(k):
        return (mt, lax.rem(mz + 2 * k, nz))

    wide_order = sorted(range(1, nx), key=lambda k: -wide_hops(k))
    deep_order = sorted(range(1, nd), key=lambda k: -min(k, nd - k))
    barrier = pltpu.get_barrier_semaphore()
    cross = lax.rem(mz - 1 + 2 * side + nz, nz)
    greeted = [(lax.rem(mt + dt + nt, nt), cross) for dt in (-1, 0, 1)]
    greeted += [wide_peer(k) for k in wide_order] + [deep_peer(k) for k in deep_order]
    for peer in greeted:
        pl.semaphore_signal(barrier, inc=1, device_id=peer, device_id_type=MESH_ID)

    def all_of(ref, send, recv, peer):
        return pltpu.make_async_remote_copy(
            src_ref=ref, dst_ref=ref, send_sem=send, recv_sem=recv, device_id=peer, device_id_type=MESH_ID
        )

    def to_wide(src, dst, whole, send, recv):
        for k in wide_order:
            peer = wide_peer(k)
            pltpu.make_async_remote_copy(
                src_ref=src(2 * peer[0] + lax.rem(peer[1], 2)), dst_ref=dst(k),
                send_sem=send, recv_sem=recv, device_id=peer, device_id_type=MESH_ID,
            ).start()
        return all_of(whole.at[1:nx], send, recv, wide_peer(1))

    def to_deep(src, dst, whole, send, recv):
        for k in deep_order:
            pltpu.make_async_remote_copy(
                src_ref=src, dst_ref=dst,
                send_sem=send, recv_sem=recv, device_id=deep_peer(k), device_id_type=MESH_ID,
            ).start()
        return all_of(whole.at[1:nd], send, recv, deep_peer(1))

    loads[0].wait()
    for d in range(3):
        for c in range(2):
            for t in range(LT):
                lk[pl.ds(d * 24 + c * 12 + t * 4, LZ), :] = links[d, c, t]
    for comp in range(4):
        for t in range(LT):
            lbuf[2 + t, pl.ds(8 + comp, LZ, stride=4), :] = lk[pl.ds(comp * PLANES + t * LZ, LZ), :]
    pl.semaphore_wait(barrier, len(greeted))

    t_from = {-1: slice(2, 4), 0: slice(2, 5), 1: slice(3, 5)}
    t_into = {-1: slice(5, 7), 0: slice(2, 5), 1: slice(0, 2)}
    z_from = {-1: slice(8, 16), 0: slice(8, 24), 1: slice(16, 24)}
    z_into = {-1: slice(24, 32), 0: slice(8, 24), 1: slice(0, 8)}
    link_copies = []
    for i, (dt, dz) in enumerate(DIRS):
        copy = pltpu.make_async_remote_copy(
            src_ref=lbuf.at[t_from[dt], z_from[dz]],
            dst_ref=lbuf.at[t_into[dt], z_into[dz]],
            send_sem=send_l.at[i], recv_sem=recv_l.at[i],
            device_id=neighbour(dt, dz), device_id_type=MESH_ID,
        )
        copy.start()
        link_copies.append(copy)
    fs[...] = jnp.zeros_like(fs)

    for load in loads[1:]:
        load.wait()
    for t in range(LT):
        site[0, pl.ds(t * LZ, LZ), :] = act[t].astype(f32)
        site[1, pl.ds(t * LZ, LZ), :] = ldc_in[t]
        for c in range(2):
            bins[pl.ds(c * 12 + t * LZ, LZ), :] = bins_in[c, t]
            cot[pl.ds(c * 12 + t * LZ, LZ), :] = cot_in[c, t]
    nt_dims = (((1,), (1,)), ((), ()))

    def one_hot(rows, padded_dim):
        shape = (rows, 54) if padded_dim == 0 else (54, rows)
        wide = lax.broadcasted_iota(jnp.int32, shape, padded_dim)
        tight = lax.broadcasted_iota(jnp.int32, shape, 1 - padded_dim)
        hit = (wide < 72) & (wide % 8 < 6) & (tight == (wide // 8) * 6 + wide % 8)
        return jnp.where(hit, 1.0, 0.0).astype(bf16)

    spread80 = one_hot(80, 1)
    w1p[...] = jnp.concatenate(
        [
            jnp.dot(first_w[i * 96 : (i + 1) * 96, :], spread80, preferred_element_type=f32)
            for i in range(3)
        ],
        axis=1,
    ).astype(bf16)
    w2k[...] = jnp.concatenate(
        [second_w[i * 144 : (i + 1) * 144, :].astype(f32) for i in range(3)], axis=1
    ).astype(bf16)
    diag = lax.broadcasted_iota(jnp.int32, (288, 288), 0) == lax.broadcasted_iota(jnp.int32, (288, 288), 1)
    wt2[...] = lax.dot_general(
        jnp.where(diag, 1.0, 0.0).astype(bf16), second_w[...], nt_dims, preferred_element_type=f32
    ).astype(bf16)

    def as_column(row_ref, count):
        eye = lax.broadcasted_iota(jnp.int32, (count, count), 0) == lax.broadcasted_iota(
            jnp.int32, (count, count), 1
        )
        return jnp.sum(jnp.where(eye, row_ref[...], 0.0), axis=1, keepdims=True)

    b1_col, b2_col = as_column(b1, HID), as_column(b2, OUTC)
    for copy in link_copies:
        copy.wait()

    def feature_slice(t, carry):
        x_two = [lbuf[t, pl.ds(comp, 8, stride=4), :] for comp in (0, 1)]
        y_two = [lbuf[t, pl.ds(comp, 8, stride=4), :] for comp in (2, 3)]
        for which, three in enumerate(loop_phases(x_two, y_two)):
            pairs = [sin_cos(psi) for psi in three]
            fs[pl.ds(2 * which, 8, stride=8), :] = (pairs[0][1] + pairs[1][1] + pairs[2][1]) * (1.0 / 3.0)
            fs[pl.ds(2 * which + 1, 8, stride=8), :] = (pairs[0][0] + pairs[1][0] + pairs[2][0]) * (1.0 / 3.0)
        row = pl.multiple_of(t * 80, 16)
        for z in range(8):
            blocks = nine_shifts(fs[z * 8 : z * 8 + 8, :])
            blocks.append(jnp.zeros((8, LANES), f32))
            fcols[pl.ds(row, 80), z * LANES : (z + 1) * LANES] = jnp.concatenate(blocks, axis=0).astype(bf16)
        return carry

    lax.fori_loop(0, 7, feature_slice, 0, unroll=True)

    def hidden_slice(t, carry):
        got = jnp.dot(
            w1p[...], fcols[pl.ds(pl.multiple_of(t * 80, 16), 240), :], preferred_element_type=f32
        )
        pre = got[0:32, 0:768] + got[32:64, 128:896] + got[64:96, 256:1024] + b1_col
        pres[t] = pre[:, 128:640]
        hid = pre / (1.0 + jnp.exp(-pre))
        row = pl.multiple_of(t * 288, 16)
        for z in range(6):
            blocks = nine_shifts(hid[:, z * LANES : (z + 1) * LANES])
            cols[pl.ds(row, 288), z * LANES : (z + 1) * LANES] = jnp.concatenate(blocks, axis=0).astype(bf16)
        return carry

    lax.fori_loop(0, 5, hidden_slice, 0, unroll=True)

    level = lax.broadcasted_iota(jnp.int32, (K, LANES), 0)

    def param_slice(t, carry):
        got = jnp.dot(
            w2k[...], cols[pl.ds(pl.multiple_of(t * 288, 16), 864), :], preferred_element_type=f32
        )
        par = got[0:48, 0:512] + got[48:96, 128:640] + got[96:144, 256:768] + b2_col
        grow = jnp.exp(-jnp.abs(par))
        soft = jnp.maximum(par, 0.0) + jnp.log1p(grow)
        sigs[t] = jnp.where(par >= 0.0, 1.0, grow) / (1.0 + grow)
        for z in range(LZ):
            for c in range(2):
                plane = t * LZ + z
                chosen = bins[pl.ds(c * PLANES + plane, 1), :]
                pick = level == chosen
                below = level < chosen
                after = level == ((chosen + 1) & 7)
                cut = soft[c * 24 : c * 24 + 24, z * LANES : (z + 1) * LANES]
                sw, sh, sd = cut[0:8], cut[8:16], cut[16:24]
                sums = (
                    sw, jnp.where(pick, sw, 0.0),
                    sh, jnp.where(pick, sh, 0.0), jnp.where(below, sh, 0.0),
                    jnp.where(pick, sd, 0.0), jnp.where(after, sd, 0.0),
                )
                for q, value in enumerate(sums):
                    red[q, pl.ds(c * 16 + plane, 1), :] = jnp.sum(value, axis=0, keepdims=True)
        return carry

    lax.fori_loop(0, LT, param_slice, 0, unroll=True)

    live = site[0, 0:12, :]
    g_log = live * site[1, 0:12, :]
    for c in range(2):
        x = lk[c * 12 : c * 12 + 12, :]
        tl = lk[48 + c * 12 : 60 + c * 12, :]
        xab[0:8, :] = lk[c * 12 + 4 : c * 12 + 12, :]
        xab[8:12, :] = lbuf[5, pl.ds(8 + c, LZ, stride=4), :]
        theta = x + shifted(tl, 0, 1) - xab[0:12, :] - tl
        my_cot = cot[c * 12 : c * 12 + 12, :]
        g_new = -live * my_cot
        rows = slice(c * 16, c * 16 + 12)
        sum_w, pick_w = red[0, rows, :], red[1, rows, :]
        sum_h, pick_h, low_h = red[2, rows, :], red[3, rows, :], red[4, rows, :]
        d0 = min_deriv + red[5, rows, :]
        d1 = min_deriv + red[6, rows, :]
        inv_w, inv_h = 1.0 / sum_w, 1.0 / sum_h
        frac_w, frac_h, frac_low = pick_w * inv_w, pick_h * inv_h, low_h * inv_h
        width = min_share + keep_share * frac_w
        height = min_share + keep_share * frac_h
        r = height / width
        u = 1.0 / (1.0 + jnp.exp(-theta))
        v = 1.0 - u
        q = u * v
        den = r + (d0 + d1 - 2.0 * r) * q
        top = r * u * u + d0 * q
        numer = d1 * u * u + 2.0 * r * q + d0 * v * v
        inv_den = 1.0 / den
        g_top = g_new * two_pi * height * inv_den
        g_den = -(g_top * top + 2.0 * g_log) * inv_den
        g_num = g_log / numer
        g_h = g_new * two_pi * top * inv_den + g_log / height
        g_r = g_top * u * u + g_den * (1.0 - 2.0 * q) + 2.0 * g_num * q + g_log / r
        g_d0 = (g_top + g_den) * q + g_num * v * v
        g_d1 = g_den * q + g_num * u * u
        g_q = g_top * d0 + g_den * (d0 + d1 - 2.0 * r) + 2.0 * g_num * r
        g_u = 2.0 * g_top * r * u + 2.0 * g_num * (d1 * u - d0 * v) + g_q * (1.0 - 2.0 * u)
        g_theta = g_u * q + g_log * (1.0 - 2.0 * u)
        all_h = g_h + g_r / width
        all_w = -g_r * r / width
        base = two_pi * g_new
        a_w = keep_share * all_w * inv_w
        coef[0, rows, :] = a_w
        coef[1, rows, :] = a_w * frac_w
        coef[2, rows, :] = keep_share * all_h * inv_h
        coef[3, rows, :] = keep_share * base * inv_h
        coef[4, rows, :] = keep_share * (all_h * frac_h + base * frac_low) * inv_h
        coef[5, rows, :] = g_d0
        coef[6, rows, :] = g_d1
        grad = g_theta + live * my_cot
        pgv[c, 4:16, :] = grad
        pgs[c * 4 : c * 4 + 4, :] = grad[8:12, :]

    phase_copy = pltpu.make_async_remote_copy(
        src_ref=pgs, dst_ref=pgr, send_sem=send_g, recv_sem=recv_g,
        device_id=neighbour(1, 0), device_id_type=MESH_ID,
    )
    phase_copy.start()

    def param_grad_slice(t, total):
        for z in range(LZ):
            plane = t * LZ + z
            parts = []
            for c in range(2):
                chosen = bins[pl.ds(c * PLANES + plane, 1), :]
                pick = level == chosen
                below = level < chosen
                after = level == ((chosen + 1) & 7)
                a = [coef[k, pl.ds(c * 16 + plane, 1), :] for k in range(7)]
                sig = sigs[t, c * 24 : c * 24 + 24, z * LANES : (z + 1) * LANES]
                parts.append((jnp.where(pick, a[0], 0.0) - a[1]) * sig[0:8])
                parts.append((jnp.where(pick, a[2], jnp.where(below, a[3], 0.0)) - a[4]) * sig[8:16])
                parts.append((jnp.where(pick, a[5], jnp.where(after, a[6], 0.0))) * sig[16:24])
            grad = jnp.concatenate(parts, axis=0)
            pbuf[t + 1, z + 1] = grad.astype(bf16)
            total = total + grad
        return total

    bias2 = jnp.sum(
        lax.fori_loop(0, LT, param_grad_slice, jnp.zeros((OUTC, LANES), f32), unroll=True), axis=1, keepdims=True
    )

    h_from = {-1: slice(1, 2), 0: slice(1, 4), 1: slice(3, 4)}
    h_into = {-1: slice(4, 5), 0: slice(1, 4), 1: slice(0, 1)}
    v_from = {-1: slice(1, 2), 0: slice(1, 5), 1: slice(4, 5)}
    v_into = {-1: slice(5, 6), 0: slice(1, 5), 1: slice(0, 1)}

    def send_halo(buf, send, recv):
        for dt, dz in DIRS:
            pltpu.make_async_remote_copy(
                src_ref=buf.at[h_from[dt], v_from[dz]],
                dst_ref=buf.at[h_into[dt], v_into[dz]],
                send_sem=send, recv_sem=recv,
                device_id=neighbour(dt, dz), device_id_type=MESH_ID,
            ).start()
        return all_of(buf.at[0:3], send, recv, neighbour(1, 0))

    param_copies = send_halo(pbuf, send_p, recv_p)

    def spread(buf, t, rows):
        own = jnp.concatenate([buf[t + 1, z + 1] for z in range(LZ)], axis=1)
        one = jnp.zeros((rows, LANES), bf16)
        two = jnp.zeros((rows, 2 * LANES), bf16)
        return jnp.concatenate(
            [
                jnp.concatenate([own, two], axis=1),
                jnp.concatenate([one, own, one], axis=1),
                jnp.concatenate([two, own], axis=1),
            ],
            axis=0,
        )

    spread_p = [spread(pbuf, t, OUTC) for t in range(LT)]
    for i in range(3):
        total = None
        for t in range(LT):
            part = lax.dot_general(
                spread_p[t], cols[(t + i) * 288 : (t + i + 1) * 288, :], nt_dims, preferred_element_type=f32
            )
            total = part if total is None else total + part
        gm2[i * 144 : (i + 1) * 144, :] = total[:, 0:128].astype(bf16)
        gm2[432 + i * 144 : 576 + i * 144, :] = total[:, 128:256].astype(bf16)
        tails[i * 144 : (i + 1) * 144, :] = jnp.concatenate(
            [total[:, 256:288], jnp.zeros((144, 96), f32)], axis=1
        )
    tails[432:448, :] = jnp.zeros((16, LANES), f32)
    tail = tails[0:112, :]
    for g in range(1, 4):
        tail = tail + pltpu.roll(tails[g * 112 : (g + 1) * 112, :], 32 * g, 1)
    gm2[864:976, :] = tail.astype(bf16)
    gm2[976:1024, :] = jnp.zeros((48, LANES), bf16)

    rows2, rows1 = 1024 // nx, 256 // nx

    def wide_rows(index, rows):
        return pl.ds(pl.multiple_of(index * rows, rows), rows)

    copies_a = to_wide(
        lambda index: gm2.at[wide_rows(index, rows2)], lambda k: got_a.at[k], got_a, send_a, recv_a
    )

    param_copies.wait()

    def stacked(buf, t):
        rows = []
        for i in range(3):
            for j in range(3):
                rows.append(jnp.concatenate([buf[t + 2 - i, z + 2 - j] for z in range(LZ)], axis=1))
        return jnp.concatenate(rows, axis=0)

    def hidden_grad_slice(t, total):
        got = jnp.dot(wt2[...], stacked(pbuf, t), preferred_element_type=f32)
        for z in range(LZ):
            lanes = slice(z * LANES, (z + 1) * LANES)
            grad = shift_sum([got[b * HID : (b + 1) * HID, lanes] for b in range(9)])
            pre = pres[t + 1, :, lanes]
            sig = 1.0 / (1.0 + jnp.exp(-pre))
            grad = grad * (sig * (1.0 + pre * (1.0 - sig)))
            qbuf[t + 1, z + 1] = grad.astype(bf16)
            total = total + grad
        return total

    bias1 = jnp.sum(
        lax.fori_loop(0, LT, hidden_grad_slice, jnp.zeros((HID, LANES), f32), unroll=True), axis=1, keepdims=True
    )

    tight80 = one_hot(80, 0)
    spread_q = [spread(qbuf, t, HID) for t in range(LT)]
    g1 = []
    for i in range(3):
        total = None
        for t in range(LT):
            row = (t + 1 + i) * 80
            part = lax.dot_general(
                spread_q[t], fcols[row : row + 80, 128:896], nt_dims, preferred_element_type=f32
            )
            total = part if total is None else total + part
        g1.append(jnp.dot(total.astype(bf16), tight80, preferred_element_type=f32))
    g1 = jnp.concatenate(g1, axis=0)
    g1 = jnp.concatenate([g1, jnp.zeros((288, 74), f32)], axis=1)
    gm1[0:144, :] = g1[0:144] + pltpu.roll(g1[144:288], 64, 1)
    bias = jnp.concatenate([bias2, bias1, jnp.zeros((32, 1), f32)], axis=0)
    lane = lax.broadcasted_iota(jnp.int32, (112, LANES), 1)
    gm1[144:256, :] = jnp.where(lane == 0, bias, 0.0)
    copies_e = to_wide(
        lambda index: gm1.at[wide_rows(index, rows1)], lambda k: got_e.at[k], got_e, send_e, recv_e
    )

    preact_copies = send_halo(qbuf, send_q, recv_q)

    def in_order(parts, count):
        total = parts[0].astype(f32)
        for k in range(1, count):
            total = total + parts[k].astype(f32)
        return total

    total = gm2[wide_rows(mx, rows2), :].astype(f32)
    copies_a.wait()
    for k in range(1, nx):
        total = total + got_a[k].astype(f32)
    mid_b[...] = (total * scale).astype(bf16)
    copies_b = to_deep(mid_b, got_b.at[deep], got_b, send_b, recv_b)
    got_b[deep] = mid_b[...]

    wt1[...] = lax.dot_general(
        one_hot(72, 0), first_w[...], nt_dims, preferred_element_type=f32
    ).astype(bf16)

    x_two = [lk[0:12, :], lk[12:24, :]]
    y_two = [lk[24:36, :], lk[36:48, :]]
    pairs = [[sin_cos(psi) for psi in three] for three in loop_phases(x_two, y_two)]

    total = gm1[wide_rows(mx, rows1), :]
    copies_e.wait()
    for k in range(1, nx):
        total = total + got_e[k]
    total = total * scale
    mid_f[...] = total
    copies_f = to_deep(mid_f, got_f.at[deep], got_f, send_f, recv_f)
    got_f[deep] = total

    copies_b.wait()
    fin_d[...] = in_order(got_b, nd).astype(bf16)
    copies_d = to_wide(lambda index: fin_d, lambda k: out2.at[wide_rows(mx, rows2)], got_a, send_d, recv_d)
    stores = [pltpu.make_async_copy(fin_d, out2.at[wide_rows(mx, rows2)], out_sem.at[1])]
    stores[0].start()

    copies_f.wait()
    fin_g[...] = in_order(got_f, nd)
    copies_h = to_wide(lambda index: fin_g, lambda k: out1.at[wide_rows(mx, rows1)], got_e, send_h, recv_h)
    stores.append(pltpu.make_async_copy(fin_g, out1.at[wide_rows(mx, rows1)], out_sem.at[2]))
    stores[1].start()

    phase_copy.wait()
    preact_copies.wait()

    def feature_grad_slice(t, carry):
        got = jnp.dot(wt1[...], stacked(qbuf, t), preferred_element_type=f32)
        for z in range(LZ):
            lanes = slice(z * LANES, (z + 1) * LANES)
            grad = shift_sum([got[b * 8 : (b + 1) * 8, lanes] for b in range(9)])
            fgs[pl.ds(pl.multiple_of((t * LZ + z) * 8, 8), 8), :] = grad
        return carry

    lax.fori_loop(0, LT, feature_grad_slice, 0, unroll=True)

    third = 1.0 / 3.0
    loop_grads = []
    for which in range(3):
        g_cos = fgs[pl.ds(2 * which, PLANES, stride=8), :] * third
        g_sin = fgs[pl.ds(2 * which + 1, PLANES, stride=8), :] * third
        three = [g_sin * cos_v - g_cos * sin_v for sin_v, cos_v in pairs[which]]
        loop_grads.append((three[0] - three[2], three[1] - three[2]))
    for c in range(2):
        dp, dw, dr = loop_grads[0][c], loop_grads[1][c], loop_grads[2][c]
        pair = dp + dr
        x_ctx = (
            dp + dw + dr
            - shifted(dp + dw, -1, 0)
            + shifted(dw, 0, -1)
            - shifted(dw, -1, -1)
            - shifted(dr, -2, 0)
        )
        y_ctx = (
            shifted(pair, 0, -1)
            - pair
            - dw
            + shifted(dw, 0, -2)
            + shifted(dr, -1, -1)
            - shifted(dr, -1, 0)
        )
        pgv[c, 0:4, :] = pgr[c * 4 : c * 4 + 4, :]
        grad = pgv[c, 4:16, :]
        prev = pgv[c, 0:12, :]
        link_out[c * 12 : c * 12 + 12, :] = grad - prev + x_ctx
        link_out[24 + c * 12 : 36 + c * 12, :] = y_ctx
        link_out[48 + c * 12 : 60 + c * 12, :] = cot[c * 12 : c * 12 + 12, :] - grad + shifted(grad, 0, -1)

    stores.append(pltpu.make_async_copy(link_out, out_link, out_sem.at[0]))
    stores[2].start()

    for copy in [copies_d] + stores + [copies_h]:
        copy.wait()


def write_kernel(link, sum2, sum1, out_link, out_first, out_bias1, out_second, out_bias2):
    for d in range(3):
        for c in range(2):
            for t in range(LT):
                out_link[d, c, t] = link[pl.ds(d * 24 + c * 12 + t * 4, LZ), :]
    out_second[:, 0:128] = sum2[0:432, :].astype(f32)
    out_second[:, 128:256] = sum2[432:864, :].astype(f32)
    tail = sum2[864:976, :].astype(f32)
    for g in range(4):
        count = min(112, 432 - g * 112)
        out_second[g * 112 : g * 112 + count, 256:288] = rolled(tail, -32 * g)[0:count, 0:32]
    half = sum1[0:144, :]
    out_first[0:144, :] = half[:, 0:54]
    out_first[144:288, :] = pltpu.roll(half, 64, 1)[:, 0:54]
    for out, begin, count in ((out_bias2, 144, OUTC), (out_bias1, 192, HID)):
        col = sum1[begin : begin + count, :][:, 0:1]
        eye = lax.broadcasted_iota(jnp.int32, (count, count), 0) == lax.broadcasted_iota(
            jnp.int32, (count, count), 1
        )
        out[...] = jnp.sum(jnp.where(eye, col, 0.0), axis=0, keepdims=True)


def vmem():
    return pl.BlockSpec(memory_space=pltpu.VMEM)


def local(
    link_phases, active, bin_index, first_weight, first_bias,
    second_weight, second_bias, cotangent, logdet_cotangent,
):
    nt, nz = lax.axis_size("ta"), lax.axis_size("gz")
    dma = pltpu.SemaphoreType.DMA
    mem = pltpu.VMEM
    nx, nd = 2 * nt, nz // 2
    rows2, rows1 = 1024 // nx, 256 // nx
    scale = 1.0 / math.sqrt(nt * nz * PLANES * LANES)
    link, sum2, sum1 = pl.pallas_call(
        functools.partial(main_kernel, scale),
        out_shape=(
            jax.ShapeDtypeStruct((72, LANES), f32),
            jax.ShapeDtypeStruct((1024, LANES), bf16),
            jax.ShapeDtypeStruct((256, LANES), f32),
        ),
        in_specs=[pl.BlockSpec(memory_space=pltpu.HBM)] * 9,
        out_specs=(pl.BlockSpec(memory_space=pltpu.HBM),) * 3,
        scratch_shapes=[
            mem((3, 2, LT, LZ, LANES), f32),
            mem((LT, LZ, LANES), jnp.int32),
            mem((2, LT, LZ, LANES), jnp.int32),
            mem((288, 54), bf16),
            mem((1, HID), f32),
            mem((432, 288), bf16),
            mem((1, OUTC), f32),
            mem((2, LT, LZ, LANES), f32),
            mem((LT, LZ, LANES), f32),
            mem((72, LANES), f32),
            mem((24, LANES), jnp.int32),
            mem((24, LANES), f32),
            mem((2, 16, LANES), f32),
            mem((96, 240), bf16),
            mem((144, 864), bf16),
            mem((288, 432), bf16),
            mem((72, 288), bf16),
            mem((7, 32, LANES), f32),
            mem((64, LANES), f32),
            mem((560, 1024), bf16),
            mem((5, HID, 512), f32),
            mem((1440, 768), bf16),
            mem((LT, OUTC, 512), f32),
            mem((7, 32, LANES), f32),
            mem((7, 32, LANES), f32),
            mem((16, LANES), f32),
            mem((8, LANES), f32),
            mem((8, LANES), f32),
            mem((2, 16, LANES), f32),
            mem((5, 6, OUTC, LANES), bf16),
            mem((5, 6, HID, LANES), bf16),
            mem((96, LANES), f32),
            mem((448, LANES), f32),
            mem((1024, LANES), bf16),
            mem((nx, rows2, LANES), bf16),
            mem((rows2, LANES), bf16),
            mem((nd, rows2, LANES), bf16),
            mem((rows2, LANES), bf16),
            mem((256, LANES), f32),
            mem((nx, rows1, LANES), f32),
            mem((rows1, LANES), f32),
            mem((nd, rows1, LANES), f32),
            mem((rows1, LANES), f32),
            mem((72, LANES), f32),
            dma((9,)), dma((3,)), dma((8,)), dma((8,)), dma, dma, dma, dma, dma, dma,
            dma, dma, dma, dma, dma, dma, dma, dma, dma, dma, dma, dma,
        ],
        compiler_params=pltpu.CompilerParams(
            collective_id=0, has_side_effects=True, vmem_limit_bytes=56 * 1024 * 1024
        ),
        name="main_kernel",
    )(
        link_phases, active, bin_index,
        first_weight.reshape(288, 54), first_bias.reshape(1, HID),
        second_weight.reshape(432, 288), second_bias.reshape(1, OUTC),
        cotangent, logdet_cotangent,
    )
    link_grad, first, bias1, second, bias2 = pl.pallas_call(
        write_kernel,
        out_shape=(
            jax.ShapeDtypeStruct((3, 2, LT, LZ, LANES), f32),
            jax.ShapeDtypeStruct((288, 54), f32),
            jax.ShapeDtypeStruct((1, HID), f32),
            jax.ShapeDtypeStruct((432, 288), f32),
            jax.ShapeDtypeStruct((1, OUTC), f32),
        ),
        in_specs=[vmem()] * 3,
        out_specs=(vmem(),) * 5,
        compiler_params=pltpu.CompilerParams(vmem_limit_bytes=56 * 1024 * 1024),
        name="write_kernel",
    )(link, sum2, sum1)
    return (
        link_grad,
        first.reshape(9, HID, 54),
        bias1.reshape(HID),
        second.reshape(9, OUTC, 288),
        bias2.reshape(OUTC),
    )


def solution(mesh):
    return jax.shard_map(
        local,
        mesh=mesh,
        in_specs=(
            P(None, None, "ta", "gz", None),
            P("ta", "gz", None),
            P(None, "ta", "gz", None),
            P(), P(), P(), P(),
            P(None, "ta", "gz", None),
            P("ta", "gz", None),
        ),
        out_specs=(P(None, None, "ta", "gz", None), P(), P(), P(), P()),
        check_vma=False,
    )
```

```python
import functools
import math

import jax
import jax.numpy as jnp
from jax import lax
from jax.experimental import pallas as pl
from jax.experimental.pallas import tpu as pltpu
from jax.sharding import PartitionSpec as P

K = 8
LT = 3
LZ = 4
LANES = 128
HID = 32
OUTC = 48
PLANES = LT * LZ
MESH_ID = pl.DeviceIdType.MESH

min_share = 0.001
min_deriv = 0.001
keep_share = 1.0 - K * min_share
two_pi = 2.0 * math.pi

f32 = jnp.float32
bf16 = jnp.bfloat16


def lane_x(rows):
    return lax.broadcasted_iota(jnp.int32, (rows, LANES), 1) % 8


def rolled(value, amount):
    amount = amount % LANES
    if amount == 0:
        return value
    return pltpu.roll(value, amount, 1)


def shifted(value, step_y, step_x):
    near = rolled(value, -(8 * step_y + step_x))
    if step_x == 0:
        return near
    xs = lane_x(value.shape[0])
    if step_x > 0:
        wrap = rolled(value, -(8 * step_y + step_x - 8))
        return jnp.where(xs < 8 - step_x, near, wrap)
    wrap = rolled(value, -(8 * step_y + step_x + 8))
    return jnp.where(xs >= -step_x, near, wrap)


def nine_shifts(value):
    return [shifted(value, sy, sx) for sy in (-1, 0, 1) for sx in (-1, 0, 1)]


def shift_sum(blocks):
    total = None
    for ix, dx in enumerate((-1, 0, 1)):
        part = None
        for iy, dy in enumerate((-1, 0, 1)):
            piece = rolled(blocks[3 * iy + ix], 8 * dy)
            part = piece if part is None else part + piece
        part = shifted(part, 0, -dx)
        total = part if total is None else total + part
    return total


def sin_cos(angle):
    turns = jnp.floor(angle * (2.0 / math.pi) + 0.5)
    rest = angle - turns * 1.5703125
    rest = rest - turns * 4.837512969970703125e-4
    rest = rest - turns * 7.54978995489188e-8
    sq = rest * rest
    s = rest + rest * sq * (-1.6666654611e-1 + sq * (8.3321608736e-3 - sq * 1.9515295891e-4))
    c = 1.0 - 0.5 * sq + sq * sq * (
        4.166664568298827e-2 + sq * (-1.388731625493765e-3 + sq * 2.443315711809948e-5)
    )
    quad = turns.astype(jnp.int32)
    swap = (quad & 1) == 1
    sin_v = jnp.where(swap, c, s)
    cos_v = jnp.where(swap, s, c)
    sin_v = jnp.where((quad & 2) == 2, -sin_v, sin_v)
    cos_v = jnp.where(((quad + 1) & 2) == 2, -cos_v, cos_v)
    return sin_v, cos_v


def loop_phases(x_two, y_two):
    plaq, wide, tall = [], [], []
    for x, y in zip(x_two, y_two):
        y_x = shifted(y, 0, 1)
        x_y = shifted(x, 1, 0)
        plaq.append(x + y_x - x_y - y)
        wide.append(x + shifted(x, 0, 1) + shifted(y, 0, 2) - shifted(x, 1, 1) - x_y - y)
        tall.append(x + y_x + shifted(y, 1, 1) - shifted(x, 2, 0) - shifted(y, 1, 0) - y)
    out = []
    for two in (plaq, wide, tall):
        out.append((two[0], two[1], -(two[0] + two[1])))
    return out


DIRS = [(dt, dz) for dt in (-1, 0, 1) for dz in (-1, 0, 1) if (dt, dz) != (0, 0)]


def neighbour(dt, dz):
    nt, nz = lax.axis_size("ta"), lax.axis_size("gz")
    mt, mz = lax.axis_index("ta"), lax.axis_index("gz")
    return (lax.rem(mt + dt + nt, nt), lax.rem(mz + dz + nz, nz))


def main_kernel(
    scale, *refs
):
    given, refs = refs[:9], refs[9:]
    (out_link, out2, out1), refs = refs[:3], refs[3:]
    held, refs = refs[:9], refs[9:]
    links, act, bins_in, first_w, b1, second_w, b2, cot_in, ldc_in = held
    (
        lk, bins, cot, site, w1p, w2k, wt2, wt1,
        lbuf, fs, fcols, pres, cols, sigs, red, coef, xab, pgs, pgr, pgv,
        pbuf, qbuf, fgs, tails, gm2, got_a, mid_b, got_b, fin_d,
        gm1, got_e, mid_f, got_f, fin_g, link_out,
        in_sem, out_sem, send_l, recv_l, send_p, recv_p, send_q, recv_q, send_g, recv_g,
        send_a, recv_a, send_b, recv_b, send_d, recv_d,
        send_e, recv_e, send_f, recv_f, send_h, recv_h,
    ) = refs
    loads = [pltpu.make_async_copy(src, dst, in_sem.at[i]) for i, (src, dst) in enumerate(zip(given, held))]
    for load in loads:
        load.start()

    nt, nz = lax.axis_size("ta"), lax.axis_size("gz")
    mt, mz = lax.axis_index("ta"), lax.axis_index("gz")
    nx, nd = 2 * nt, nz // 2
    side, deep = lax.rem(mz, 2), mz // 2
    mx = 2 * mt + side

    flips, weight = [(0, 1 - 2 * side)], 1
    while weight < nt:
        flips.append((weight * (1 - 2 * lax.rem(mt // weight, 2)), 0))
        weight *= 2

    def wide_peer(k):
        along, across = mt, mz
        for bit, (dt, dz) in enumerate(flips):
            if k >> bit & 1:
                along, across = along + dt, across + dz
        return (along, across)

    def wide_hops(k):
        steps = (0, 1, 2, 1)
        return steps[(k >> 2) & 3] + steps[((k >> 4) & 1) * 2 + (k & 1)]

    def deep_peer(k):
        return (mt, lax.rem(mz + 2 * k, nz))

    wide_order = sorted(range(1, nx), key=lambda k: -wide_hops(k))
    deep_order = sorted(range(1, nd), key=lambda k: -min(k, nd - k))
    barrier = pltpu.get_barrier_semaphore()
    cross = lax.rem(mz - 1 + 2 * side + nz, nz)
    greeted = [(lax.rem(mt + dt + nt, nt), cross) for dt in (-1, 0, 1)]
    greeted += [wide_peer(k) for k in wide_order] + [deep_peer(k) for k in deep_order]
    for peer in greeted:
        pl.semaphore_signal(barrier, inc=1, device_id=peer, device_id_type=MESH_ID)

    def all_of(ref, send, recv, peer):
        return pltpu.make_async_remote_copy(
            src_ref=ref, dst_ref=ref, send_sem=send, recv_sem=recv, device_id=peer, device_id_type=MESH_ID
        )

    def to_wide(src, dst, whole, send, recv):
        for k in wide_order:
            peer = wide_peer(k)
            pltpu.make_async_remote_copy(
                src_ref=src(2 * peer[0] + lax.rem(peer[1], 2)), dst_ref=dst(k),
                send_sem=send, recv_sem=recv, device_id=peer, device_id_type=MESH_ID,
            ).start()
        return all_of(whole.at[1:nx], send, recv, wide_peer(1))

    def to_deep(src, dst, whole, send, recv):
        for k in deep_order:
            pltpu.make_async_remote_copy(
                src_ref=src, dst_ref=dst,
                send_sem=send, recv_sem=recv, device_id=deep_peer(k), device_id_type=MESH_ID,
            ).start()
        return all_of(whole.at[1:nd], send, recv, deep_peer(1))

    loads[0].wait()
    for d in range(3):
        for c in range(2):
            for t in range(LT):
                lk[pl.ds(d * 24 + c * 12 + t * 4, LZ), :] = links[d, c, t]
    for comp in range(4):
        for t in range(LT):
            lbuf[2 + t, pl.ds(8 + comp, LZ, stride=4), :] = lk[pl.ds(comp * PLANES + t * LZ, LZ), :]
    pl.semaphore_wait(barrier, len(greeted))

    t_from = {-1: slice(2, 4), 0: slice(2, 5), 1: slice(3, 5)}
    t_into = {-1: slice(5, 7), 0: slice(2, 5), 1: slice(0, 2)}
    z_from = {-1: slice(8, 16), 0: slice(8, 24), 1: slice(16, 24)}
    z_into = {-1: slice(24, 32), 0: slice(8, 24), 1: slice(0, 8)}
    for dt, dz in DIRS:
        copy = pltpu.make_async_remote_copy(
            src_ref=lbuf.at[t_from[dt], z_from[dz]],
            dst_ref=lbuf.at[t_into[dt], z_into[dz]],
            send_sem=send_l, recv_sem=recv_l,
            device_id=neighbour(dt, dz), device_id_type=MESH_ID,
        )
        copy.start()
    fs[...] = jnp.zeros_like(fs)

    for load in loads[1:]:
        load.wait()
    for t in range(LT):
        site[0, pl.ds(t * LZ, LZ), :] = act[t].astype(f32)
        site[1, pl.ds(t * LZ, LZ), :] = ldc_in[t]
        for c in range(2):
            bins[pl.ds(c * 12 + t * LZ, LZ), :] = bins_in[c, t]
            cot[pl.ds(c * 12 + t * LZ, LZ), :] = cot_in[c, t]
    nt_dims = (((1,), (1,)), ((), ()))

    def one_hot(rows, padded_dim):
        shape = (rows, 54) if padded_dim == 0 else (54, rows)
        wide = lax.broadcasted_iota(jnp.int32, shape, padded_dim)
        tight = lax.broadcasted_iota(jnp.int32, shape, 1 - padded_dim)
        hit = (wide < 72) & (wide % 8 < 6) & (tight == (wide // 8) * 6 + wide % 8)
        return jnp.where(hit, 1.0, 0.0).astype(bf16)

    spread80 = one_hot(80, 1)
    w1p[...] = jnp.concatenate(
        [
            jnp.dot(first_w[i * 96 : (i + 1) * 96, :], spread80, preferred_element_type=f32)
            for i in range(3)
        ],
        axis=1,
    ).astype(bf16)
    w2k[...] = jnp.concatenate(
        [second_w[i * 144 : (i + 1) * 144, :].astype(f32) for i in range(3)], axis=1
    ).astype(bf16)
    diag = lax.broadcasted_iota(jnp.int32, (288, 288), 0) == lax.broadcasted_iota(jnp.int32, (288, 288), 1)
    wt2[...] = lax.dot_general(
        jnp.where(diag, 1.0, 0.0).astype(bf16), second_w[...], nt_dims, preferred_element_type=f32
    ).astype(bf16)

    def as_column(row_ref, count):
        eye = lax.broadcasted_iota(jnp.int32, (count, count), 0) == lax.broadcasted_iota(
            jnp.int32, (count, count), 1
        )
        return jnp.sum(jnp.where(eye, row_ref[...], 0.0), axis=1, keepdims=True)

    b1_col, b2_col = as_column(b1, HID), as_column(b2, OUTC)
    all_of(gm1.at[0:176], send_l, recv_l, neighbour(1, 0)).wait()

    def feature_slice(t, carry):
        x_two = [lbuf[t, pl.ds(comp, 8, stride=4), :] for comp in (0, 1)]
        y_two = [lbuf[t, pl.ds(comp, 8, stride=4), :] for comp in (2, 3)]
        for which, three in enumerate(loop_phases(x_two, y_two)):
            pairs = [sin_cos(psi) for psi in three]
            fs[pl.ds(2 * which, 8, stride=8), :] = (pairs[0][1] + pairs[1][1] + pairs[2][1]) * (1.0 / 3.0)
            fs[pl.ds(2 * which + 1, 8, stride=8), :] = (pairs[0][0] + pairs[1][0] + pairs[2][0]) * (1.0 / 3.0)
        row = pl.multiple_of(t * 80, 16)
        for z in range(8):
            blocks = nine_shifts(fs[z * 8 : z * 8 + 8, :])
            blocks.append(jnp.zeros((8, LANES), f32))
            fcols[pl.ds(row, 80), z * LANES : (z + 1) * LANES] = jnp.concatenate(blocks, axis=0).astype(bf16)
        return carry

    lax.fori_loop(0, 7, feature_slice, 0, unroll=True)

    def hidden_slice(t, carry):
        got = jnp.dot(
            w1p[...], fcols[pl.ds(pl.multiple_of(t * 80, 16), 240), :], preferred_element_type=f32
        )
        pre = got[0:32, 0:768] + got[32:64, 128:896] + got[64:96, 256:1024] + b1_col
        sig = 1.0 / (1.0 + jnp.exp(-pre))
        hid = pre * sig
        pres[t] = (sig * (1.0 + pre * (1.0 - sig)))[:, 128:640]
        row = pl.multiple_of(t * 288, 16)
        for z in range(6):
            blocks = nine_shifts(hid[:, z * LANES : (z + 1) * LANES])
            cols[pl.ds(row, 288), z * LANES : (z + 1) * LANES] = jnp.concatenate(blocks, axis=0).astype(bf16)
        return carry

    lax.fori_loop(0, 5, hidden_slice, 0, unroll=True)

    level = lax.broadcasted_iota(jnp.int32, (K, LANES), 0)

    def param_slice(t, carry):
        got = jnp.dot(
            w2k[...], cols[pl.ds(pl.multiple_of(t * 288, 16), 864), :], preferred_element_type=f32
        )
        par = got[0:48, 0:512] + got[48:96, 128:640] + got[96:144, 256:768] + b2_col
        grow = jnp.exp(-jnp.abs(par))
        soft = jnp.maximum(par, 0.0) + jnp.log1p(grow)
        sigs[t] = jnp.where(par >= 0.0, 1.0, grow) / (1.0 + grow)
        for z in range(LZ):
            for c in range(2):
                plane = t * LZ + z
                chosen = bins[pl.ds(c * PLANES + plane, 1), :]
                pick = level == chosen
                below = level < chosen
                after = level == ((chosen + 1) & 7)
                cut = soft[c * 24 : c * 24 + 24, z * LANES : (z + 1) * LANES]
                sw, sh, sd = cut[0:8], cut[8:16], cut[16:24]
                sums = (
                    sw, jnp.where(pick, sw, 0.0),
                    sh, jnp.where(pick, sh, 0.0), jnp.where(below, sh, 0.0),
                    jnp.where(pick, sd, 0.0), jnp.where(after, sd, 0.0),
                )
                for q, value in enumerate(sums):
                    red[q, pl.ds(c * 16 + plane, 1), :] = jnp.sum(value, axis=0, keepdims=True)
        return carry

    lax.fori_loop(0, LT, param_slice, 0, unroll=True)

    live = site[0, 0:12, :]
    g_log = live * site[1, 0:12, :]
    for c in range(2):
        x = lk[c * 12 : c * 12 + 12, :]
        tl = lk[48 + c * 12 : 60 + c * 12, :]
        xab[0:8, :] = lk[c * 12 + 4 : c * 12 + 12, :]
        xab[8:12, :] = lbuf[5, pl.ds(8 + c, LZ, stride=4), :]
        theta = x + shifted(tl, 0, 1) - xab[0:12, :] - tl
        my_cot = cot[c * 12 : c * 12 + 12, :]
        g_new = -live * my_cot
        rows = slice(c * 16, c * 16 + 12)
        sum_w, pick_w = red[0, rows, :], red[1, rows, :]
        sum_h, pick_h, low_h = red[2, rows, :], red[3, rows, :], red[4, rows, :]
        d0 = min_deriv + red[5, rows, :]
        d1 = min_deriv + red[6, rows, :]
        inv_w, inv_h = 1.0 / sum_w, 1.0 / sum_h
        frac_w, frac_h, frac_low = pick_w * inv_w, pick_h * inv_h, low_h * inv_h
        width = min_share + keep_share * frac_w
        height = min_share + keep_share * frac_h
        r = height / width
        u = 1.0 / (1.0 + jnp.exp(-theta))
        v = 1.0 - u
        q = u * v
        den = r + (d0 + d1 - 2.0 * r) * q
        top = r * u * u + d0 * q
        numer = d1 * u * u + 2.0 * r * q + d0 * v * v
        inv_den = 1.0 / den
        g_top = g_new * two_pi * height * inv_den
        g_den = -(g_top * top + 2.0 * g_log) * inv_den
        g_num = g_log / numer
        g_h = g_new * two_pi * top * inv_den + g_log / height
        g_r = g_top * u * u + g_den * (1.0 - 2.0 * q) + 2.0 * g_num * q + g_log / r
        g_d0 = (g_top + g_den) * q + g_num * v * v
        g_d1 = g_den * q + g_num * u * u
        g_q = g_top * d0 + g_den * (d0 + d1 - 2.0 * r) + 2.0 * g_num * r
        g_u = 2.0 * g_top * r * u + 2.0 * g_num * (d1 * u - d0 * v) + g_q * (1.0 - 2.0 * u)
        g_theta = g_u * q + g_log * (1.0 - 2.0 * u)
        all_h = g_h + g_r / width
        all_w = -g_r * r / width
        base = two_pi * g_new
        a_w = keep_share * all_w * inv_w
        coef[0, rows, :] = a_w
        coef[1, rows, :] = a_w * frac_w
        coef[2, rows, :] = keep_share * all_h * inv_h
        coef[3, rows, :] = keep_share * base * inv_h
        coef[4, rows, :] = keep_share * (all_h * frac_h + base * frac_low) * inv_h
        coef[5, rows, :] = g_d0
        coef[6, rows, :] = g_d1
        grad = g_theta + live * my_cot
        pgv[c, 4:16, :] = grad
        pgs[c * 4 : c * 4 + 4, :] = grad[8:12, :]

    phase_copy = pltpu.make_async_remote_copy(
        src_ref=pgs, dst_ref=pgr, send_sem=send_g, recv_sem=recv_g,
        device_id=neighbour(1, 0), device_id_type=MESH_ID,
    )
    phase_copy.start()

    def param_grad_slice(t, total):
        for z in range(LZ):
            plane = t * LZ + z
            parts = []
            for c in range(2):
                chosen = bins[pl.ds(c * PLANES + plane, 1), :]
                pick = level == chosen
                below = level < chosen
                after = level == ((chosen + 1) & 7)
                a = [coef[k, pl.ds(c * 16 + plane, 1), :] for k in range(7)]
                sig = sigs[t, c * 24 : c * 24 + 24, z * LANES : (z + 1) * LANES]
                parts.append((jnp.where(pick, a[0], 0.0) - a[1]) * sig[0:8])
                parts.append((jnp.where(pick, a[2], jnp.where(below, a[3], 0.0)) - a[4]) * sig[8:16])
                parts.append((jnp.where(pick, a[5], jnp.where(after, a[6], 0.0))) * sig[16:24])
            grad = jnp.concatenate(parts, axis=0)
            pbuf[t + 1, z + 1] = grad.astype(bf16)
            total = total + grad
        return total

    bias2 = jnp.sum(
        lax.fori_loop(0, LT, param_grad_slice, jnp.zeros((OUTC, LANES), f32), unroll=True), axis=1, keepdims=True
    )

    h_from = {-1: slice(1, 2), 0: slice(1, 4), 1: slice(3, 4)}
    h_into = {-1: slice(4, 5), 0: slice(1, 4), 1: slice(0, 1)}
    v_from = {-1: slice(1, 2), 0: slice(1, 5), 1: slice(4, 5)}
    v_into = {-1: slice(5, 6), 0: slice(1, 5), 1: slice(0, 1)}

    def send_halo(buf, send, recv):
        for dt, dz in DIRS:
            pltpu.make_async_remote_copy(
                src_ref=buf.at[h_from[dt], v_from[dz]],
                dst_ref=buf.at[h_into[dt], v_into[dz]],
                send_sem=send, recv_sem=recv,
                device_id=neighbour(dt, dz), device_id_type=MESH_ID,
            ).start()
        return all_of(buf.at[0:3], send, recv, neighbour(1, 0))

    param_copies = send_halo(pbuf, send_p, recv_p)

    def spread(buf, t, rows):
        own = jnp.concatenate([buf[t + 1, z + 1] for z in range(LZ)], axis=1)
        one = jnp.zeros((rows, LANES), bf16)
        two = jnp.zeros((rows, 2 * LANES), bf16)
        return jnp.concatenate(
            [
                jnp.concatenate([own, two], axis=1),
                jnp.concatenate([one, own, one], axis=1),
                jnp.concatenate([two, own], axis=1),
            ],
            axis=0,
        )

    spread_p = [spread(pbuf, t, OUTC) for t in range(LT)]
    for i in range(3):
        total = None
        for t in range(LT):
            part = lax.dot_general(
                spread_p[t], cols[(t + i) * 288 : (t + i + 1) * 288, :], nt_dims, preferred_element_type=f32
            )
            total = part if total is None else total + part
        gm2[i * 144 : (i + 1) * 144, :] = total[:, 0:128].astype(bf16)
        gm2[432 + i * 144 : 576 + i * 144, :] = total[:, 128:256].astype(bf16)
        tails[i * 144 : (i + 1) * 144, :] = jnp.concatenate(
            [total[:, 256:288], jnp.zeros((144, 96), f32)], axis=1
        )
    tails[432:448, :] = jnp.zeros((16, LANES), f32)
    tail = tails[0:112, :]
    for g in range(1, 4):
        tail = tail + pltpu.roll(tails[g * 112 : (g + 1) * 112, :], 32 * g, 1)
    gm2[864:976, :] = tail.astype(bf16)
    gm2[976:1024, :] = jnp.zeros((48, LANES), bf16)

    rows2, rows1 = 1024 // nx, 256 // nx

    def wide_rows(index, rows):
        return pl.ds(pl.multiple_of(index * rows, rows), rows)

    copies_a = to_wide(
        lambda index: gm2.at[wide_rows(index, rows2)], lambda k: got_a.at[k], got_a, send_a, recv_a
    )

    param_copies.wait()

    def stacked(buf, t):
        rows = []
        for i in range(3):
            for j in range(3):
                rows.append(jnp.concatenate([buf[t + 2 - i, z + 2 - j] for z in range(LZ)], axis=1))
        return jnp.concatenate(rows, axis=0)

    def hidden_grad_slice(t, total):
        got = jnp.dot(wt2[...], stacked(pbuf, t), preferred_element_type=f32)
        for z in range(LZ):
            lanes = slice(z * LANES, (z + 1) * LANES)
            grad = shift_sum([got[b * HID : (b + 1) * HID, lanes] for b in range(9)])
            grad = grad * pres[t + 1, :, lanes]
            qbuf[t + 1, z + 1] = grad.astype(bf16)
            total = total + grad
        return total

    bias1 = jnp.sum(
        lax.fori_loop(0, LT, hidden_grad_slice, jnp.zeros((HID, LANES), f32), unroll=True), axis=1, keepdims=True
    )

    tight80 = one_hot(80, 0)
    spread_q = [spread(qbuf, t, HID) for t in range(LT)]
    g1 = []
    for i in range(3):
        total = None
        for t in range(LT):
            row = (t + 1 + i) * 80
            part = lax.dot_general(
                spread_q[t], fcols[row : row + 80, 128:896], nt_dims, preferred_element_type=f32
            )
            total = part if total is None else total + part
        g1.append(jnp.dot(total.astype(bf16), tight80, preferred_element_type=f32))
    g1 = jnp.concatenate(g1, axis=0)
    g1 = jnp.concatenate([g1, jnp.zeros((288, 74), f32)], axis=1)
    gm1[0:144, :] = g1[0:144] + pltpu.roll(g1[144:288], 64, 1)
    bias = jnp.concatenate([bias2, bias1, jnp.zeros((32, 1), f32)], axis=0)
    lane = lax.broadcasted_iota(jnp.int32, (112, LANES), 1)
    gm1[144:256, :] = jnp.where(lane == 0, bias, 0.0)
    def in_order(parts, count):
        total = parts[0].astype(f32)
        for k in range(1, count):
            total = total + parts[k].astype(f32)
        return total

    total = gm2[wide_rows(mx, rows2), :].astype(f32)
    copies_a.wait()
    for k in range(1, nx):
        total = total + got_a[k].astype(f32)
    mid_b[...] = (total * scale).astype(bf16)
    copies_b = to_deep(mid_b, got_b.at[deep], got_b, send_b, recv_b)
    got_b[deep] = mid_b[...]

    copies_e = to_wide(
        lambda index: gm1.at[wide_rows(index, rows1)], lambda k: got_e.at[k], got_e, send_e, recv_e
    )

    preact_copies = send_halo(qbuf, send_q, recv_q)

    wt1[...] = lax.dot_general(
        one_hot(72, 0), first_w[...], nt_dims, preferred_element_type=f32
    ).astype(bf16)

    x_two = [lk[0:12, :], lk[12:24, :]]
    y_two = [lk[24:36, :], lk[36:48, :]]
    pairs = [[sin_cos(psi) for psi in three] for three in loop_phases(x_two, y_two)]

    total = gm1[wide_rows(mx, rows1), :]
    copies_e.wait()
    for k in range(1, nx):
        total = total + got_e[k]
    total = total * scale
    mid_f[...] = total
    copies_f = to_deep(mid_f, got_f.at[deep], got_f, send_f, recv_f)
    got_f[deep] = total

    copies_b.wait()
    fin_d[...] = in_order(got_b, nd).astype(bf16)
    copies_d = to_wide(lambda index: fin_d, lambda k: out2.at[wide_rows(mx, rows2)], got_a, send_d, recv_d)
    stores = [pltpu.make_async_copy(fin_d, out2.at[wide_rows(mx, rows2)], out_sem.at[1])]
    stores[0].start()

    copies_f.wait()
    fin_g[...] = in_order(got_f, nd)
    copies_h = to_wide(lambda index: fin_g, lambda k: out1.at[wide_rows(mx, rows1)], got_e, send_h, recv_h)
    stores.append(pltpu.make_async_copy(fin_g, out1.at[wide_rows(mx, rows1)], out_sem.at[2]))
    stores[1].start()

    phase_copy.wait()
    preact_copies.wait()

    def feature_grad_slice(t, carry):
        got = jnp.dot(wt1[...], stacked(qbuf, t), preferred_element_type=f32)
        for z in range(LZ):
            lanes = slice(z * LANES, (z + 1) * LANES)
            grad = shift_sum([got[b * 8 : (b + 1) * 8, lanes] for b in range(9)])
            fgs[pl.ds(pl.multiple_of((t * LZ + z) * 8, 8), 8), :] = grad
        return carry

    lax.fori_loop(0, LT, feature_grad_slice, 0, unroll=True)

    third = 1.0 / 3.0
    loop_grads = []
    for which in range(3):
        g_cos = fgs[pl.ds(2 * which, PLANES, stride=8), :] * third
        g_sin = fgs[pl.ds(2 * which + 1, PLANES, stride=8), :] * third
        three = [g_sin * cos_v - g_cos * sin_v for sin_v, cos_v in pairs[which]]
        loop_grads.append((three[0] - three[2], three[1] - three[2]))
    for c in range(2):
        dp, dw, dr = loop_grads[0][c], loop_grads[1][c], loop_grads[2][c]
        pair = dp + dr
        x_ctx = (
            dp + dw + dr
            - shifted(dp + dw, -1, 0)
            + shifted(dw, 0, -1)
            - shifted(dw, -1, -1)
            - shifted(dr, -2, 0)
        )
        y_ctx = (
            shifted(pair, 0, -1)
            - pair
            - dw
            + shifted(dw, 0, -2)
            + shifted(dr, -1, -1)
            - shifted(dr, -1, 0)
        )
        pgv[c, 0:4, :] = pgr[c * 4 : c * 4 + 4, :]
        grad = pgv[c, 4:16, :]
        prev = pgv[c, 0:12, :]
        link_out[c * 12 : c * 12 + 12, :] = grad - prev + x_ctx
        link_out[24 + c * 12 : 36 + c * 12, :] = y_ctx
        link_out[48 + c * 12 : 60 + c * 12, :] = cot[c * 12 : c * 12 + 12, :] - grad + shifted(grad, 0, -1)

    stores.append(pltpu.make_async_copy(link_out, out_link, out_sem.at[0]))
    stores[2].start()

    for copy in [copies_d] + stores + [copies_h]:
        copy.wait()


def write_kernel(link, sum2, sum1, out_link, out_first, out_bias1, out_second, out_bias2):
    for d in range(3):
        for c in range(2):
            for t in range(LT):
                out_link[d, c, t] = link[pl.ds(d * 24 + c * 12 + t * 4, LZ), :]
    out_second[:, 0:128] = sum2[0:432, :].astype(f32)
    out_second[:, 128:256] = sum2[432:864, :].astype(f32)
    tail = sum2[864:976, :].astype(f32)
    for g in range(4):
        count = min(112, 432 - g * 112)
        out_second[g * 112 : g * 112 + count, 256:288] = rolled(tail, -32 * g)[0:count, 0:32]
    half = sum1[0:144, :]
    out_first[0:144, :] = half[:, 0:54]
    out_first[144:288, :] = pltpu.roll(half, 64, 1)[:, 0:54]
    for out, begin, count in ((out_bias2, 144, OUTC), (out_bias1, 192, HID)):
        col = sum1[begin : begin + count, :][:, 0:1]
        eye = lax.broadcasted_iota(jnp.int32, (count, count), 0) == lax.broadcasted_iota(
            jnp.int32, (count, count), 1
        )
        out[...] = jnp.sum(jnp.where(eye, col, 0.0), axis=0, keepdims=True)


def vmem():
    return pl.BlockSpec(memory_space=pltpu.VMEM)


def local(
    link_phases, active, bin_index, first_weight, first_bias,
    second_weight, second_bias, cotangent, logdet_cotangent,
):
    nt, nz = lax.axis_size("ta"), lax.axis_size("gz")
    dma = pltpu.SemaphoreType.DMA
    mem = pltpu.VMEM
    nx, nd = 2 * nt, nz // 2
    rows2, rows1 = 1024 // nx, 256 // nx
    scale = 1.0 / math.sqrt(nt * nz * PLANES * LANES)
    link, sum2, sum1 = pl.pallas_call(
        functools.partial(main_kernel, scale),
        out_shape=(
            jax.ShapeDtypeStruct((72, LANES), f32),
            jax.ShapeDtypeStruct((1024, LANES), bf16),
            jax.ShapeDtypeStruct((256, LANES), f32),
        ),
        in_specs=[pl.BlockSpec(memory_space=pltpu.HBM)] * 9,
        out_specs=(pl.BlockSpec(memory_space=pltpu.HBM),) * 3,
        scratch_shapes=[
            mem((3, 2, LT, LZ, LANES), f32),
            mem((LT, LZ, LANES), jnp.int32),
            mem((2, LT, LZ, LANES), jnp.int32),
            mem((288, 54), bf16),
            mem((1, HID), f32),
            mem((432, 288), bf16),
            mem((1, OUTC), f32),
            mem((2, LT, LZ, LANES), f32),
            mem((LT, LZ, LANES), f32),
            mem((72, LANES), f32),
            mem((24, LANES), jnp.int32),
            mem((24, LANES), f32),
            mem((2, 16, LANES), f32),
            mem((96, 240), bf16),
            mem((144, 864), bf16),
            mem((288, 432), bf16),
            mem((72, 288), bf16),
            mem((7, 32, LANES), f32),
            mem((64, LANES), f32),
            mem((560, 1024), bf16),
            mem((5, HID, 512), f32),
            mem((1440, 768), bf16),
            mem((LT, OUTC, 512), f32),
            mem((7, 32, LANES), f32),
            mem((7, 32, LANES), f32),
            mem((16, LANES), f32),
            mem((8, LANES), f32),
            mem((8, LANES), f32),
            mem((2, 16, LANES), f32),
            mem((5, 6, OUTC, LANES), bf16),
            mem((5, 6, HID, LANES), bf16),
            mem((96, LANES), f32),
            mem((448, LANES), f32),
            mem((1024, LANES), bf16),
            mem((nx, rows2, LANES), bf16),
            mem((rows2, LANES), bf16),
            mem((nd, rows2, LANES), bf16),
            mem((rows2, LANES), bf16),
            mem((256, LANES), f32),
            mem((nx, rows1, LANES), f32),
            mem((rows1, LANES), f32),
            mem((nd, rows1, LANES), f32),
            mem((rows1, LANES), f32),
            mem((72, LANES), f32),
            dma((9,)), dma((3,)), dma, dma, dma, dma, dma, dma, dma, dma,
            dma, dma, dma, dma, dma, dma, dma, dma, dma, dma, dma, dma,
        ],
        compiler_params=pltpu.CompilerParams(
            collective_id=0, has_side_effects=True, vmem_limit_bytes=56 * 1024 * 1024
        ),
        name="main_kernel",
    )(
        link_phases, active, bin_index,
        first_weight.reshape(288, 54), first_bias.reshape(1, HID),
        second_weight.reshape(432, 288), second_bias.reshape(1, OUTC),
        cotangent, logdet_cotangent,
    )
    link_grad, first, bias1, second, bias2 = pl.pallas_call(
        write_kernel,
        out_shape=(
            jax.ShapeDtypeStruct((3, 2, LT, LZ, LANES), f32),
            jax.ShapeDtypeStruct((288, 54), f32),
            jax.ShapeDtypeStruct((1, HID), f32),
            jax.ShapeDtypeStruct((432, 288), f32),
            jax.ShapeDtypeStruct((1, OUTC), f32),
        ),
        in_specs=[vmem()] * 3,
        out_specs=(vmem(),) * 5,
        compiler_params=pltpu.CompilerParams(vmem_limit_bytes=56 * 1024 * 1024),
        name="write_kernel",
    )(link, sum2, sum1)
    return (
        link_grad,
        first.reshape(9, HID, 54),
        bias1.reshape(HID),
        second.reshape(9, OUTC, 288),
        bias2.reshape(OUTC),
    )


def solution(mesh):
    return jax.shard_map(
        local,
        mesh=mesh,
        in_specs=(
            P(None, None, "ta", "gz", None),
            P("ta", "gz", None),
            P(None, "ta", "gz", None),
            P(), P(), P(), P(),
            P(None, "ta", "gz", None),
            P("ta", "gz", None),
        ),
        out_specs=(P(None, None, "ta", "gz", None), P(), P(), P(), P()),
        check_vma=False,
    )
```
